32 devices in a mesh: dp: 16 (over z, y, x), mp: 2 (over core).
Axes of the slice: x: 2, y: 2, z: 4, core: 2. Of those that a mesh axis runs over, the one named last changes fastest.
Arguments:
- tokens: bfloat16 [11264, 1280], P('dp'), may hold values from -6 to 6
- cotangent: bfloat16 [11264, 1280], P('dp'), may hold values from -6 to 6
- segment_ids: int32 [704, 16], P('dp'), may hold values from 0 to 15, as said below
- valid_mask: int32 [704, 16], P('dp'), may hold values from 0 to 1, as said below
- frequency: int32 [704, 1], P('dp'), may hold values from 0 to 2
- query_weight: bfloat16 [1280, 1280], P('dp', 'mp'), may hold values from -0.15625 to 0.15625
- key_weight: bfloat16 [1280, 1280], P('dp', 'mp'), may hold values from -0.15625 to 0.15625
- value_weight: bfloat16 [1280, 1280], P('dp', 'mp'), may hold values from -0.15625 to 0.15625
- output_weight: bfloat16 [1280, 1280], P('mp', 'dp'), may hold values from -0.25 to 0.25
- attn_gain: bfloat16 [1280], P('dp'), may hold values from 0.5 to 1.5
- mlp_gain: bfloat16 [1280], P('dp'), may hold values from 0.5 to 1.5
- up_weight: bfloat16 [1280, 1280], P('dp', 'mp'), may hold values from -0.15625 to 0.15625
- up_bias: bfloat16 [1280], P('mp'), may hold values from -4 to 4
- down_weight: bfloat16 [1280, 1280], P('mp', 'dp'), may hold values from -0.25 to 0.25
- down_bias: bfloat16 [1280], P('dp'), may hold values from -4 to 4
Outputs:
- layer_out: bfloat16 [11264, 1280], P('dp')
- input_grad: float32 [11264, 1280], P('dp')
- query_grad: float32 [1280, 1280], P('dp', 'mp')
- key_grad: float32 [1280, 1280], P('dp', 'mp')
- value_grad: float32 [1280, 1280], P('dp', 'mp')
- output_grad: float32 [1280, 1280], P('mp', 'dp')
- attn_gain_grad: float32 [1280], P('dp')
- mlp_gain_grad: float32 [1280], P('dp')
- up_weight_grad: float32 [1280, 1280], P('dp', 'mp')
- up_bias_grad: float32 [1280], P('mp')
- down_weight_grad: float32 [1280, 1280], P('mp', 'dp')
- down_bias_grad: float32 [1280], P('dp')
The draws below stay inside these ranges and needn't reach their ends.
Inputs may be any that keep to these rules, and one draw needn't show every extreme that they name: `segment_ids`: in each row the ids start at 0, never fall and rise by at most one from patch to patch; patches with equal ids belong to one packed series; some row gives every patch a series of its own. `valid_mask`: in each row a run of padding is followed by real patches up to the row's end; the last patch of every row is real. `frequency`: every class of 0 to 2 is given to some row.
All inputs are finite; a program needn't handle non-finite values.
Results may differ from the reference program's by a relative error of at most 0.011.
Values may be sent and summed in bfloat16 or wider, within the bound.
No kernel may reach another device: no remote copies, remote signals or barrier semaphores. Data moves between devices by JAX's collectives and lax.ppermute only.
A program may use at most 192 MiB of HBM per device.

```python
import math
from functools import partial
import jax
import jax.numpy as jnp
from jax import lax

D = 1280
H = 16
HD = 80
FF = 1280
PATCHES = 16
NCLASS = 3
ROWS_DEV = 44
ROWS = 704
TOK_DEV = 704
TOKENS = 11264
N_DP = 16


def draw_segment_ids(key, part):
    key = jax.random.fold_in(key, 7)
    pick_key = jax.random.fold_in(key, 13)
    places = jnp.arange(PATCHES, dtype=jnp.int32)[None, :]
    row_index = jnp.arange(ROWS, dtype=jnp.int32)[:, None]
    chosen_row = jax.random.randint(pick_key, (), 0, ROWS)
    breaks = (jax.random.randint(key, (ROWS, PATCHES), 0, 4) == 0).astype(jnp.int32)
    breaks = jnp.where(row_index == chosen_row, 1, breaks).astype(jnp.int32)
    breaks = breaks * (places > 0).astype(jnp.int32)
    return jnp.cumsum(breaks, axis=1).astype(jnp.int32)


def draw_valid_mask(key, part):
    key = jax.random.fold_in(key, 11)
    row_index = jnp.arange(ROWS, dtype=jnp.int32)[:, None]
    least_pad = (PATCHES - 5) * (ROWS - 1 - row_index) // max(ROWS - 1, 1)
    most_pad = jnp.minimum(least_pad + 5, PATCHES - 1)
    random_bits = jax.random.randint(key, (ROWS, 1), 0, 1 << 20)
    padding = random_bits % (most_pad - least_pad + 1) + least_pad
    places = jnp.arange(PATCHES, dtype=jnp.int32)[None, :]
    return (places >= padding).astype(jnp.int32)


def with_spikes(entries, own_key, source, target, blocks, factor):
    def block_of(axis_at):
        return (jnp.arange(entries.shape[axis_at]) // (entries.shape[axis_at] // blocks)).reshape((-1,) + (1,) * (entries.ndim - 1 - axis_at))

    near = jax.random.permutation(own_key, blocks)[block_of(target)]
    second = (block_of(target) + blocks // 2) % blocks
    return jnp.where((block_of(source) == near) | (block_of(source) == second), factor * entries, entries)


def block_scale(own_key, dims, pieces, low, top_value):
    factor_of, own = 1.0, jax.random.fold_in(own_key, 6)
    for dim, shards_of in pieces:
        draws = jnp.exp(jax.random.uniform(jax.random.fold_in(own, dim), (shards_of,), jnp.float32, low / len(pieces), top_value / len(pieces)))
        factor_of = factor_of * jnp.repeat(draws, dims[dim] // shards_of).reshape([-1 if axis == dim else 1 for axis in range(len(dims))])
    return factor_of


def distinct(stream_key, rows, number_of, top, lift):
    sequence = jax.random.permutation(jax.random.fold_in(stream_key, 1), number_of)
    pull = sequence
    for power in range(3):
        pull = pull * pull // number_of
    pull = pull * lift // number_of
    lots = jax.random.randint(jax.random.fold_in(stream_key, 2), (rows, number_of), 0, 4096) + pull
    fixed_rows = jax.random.permutation(jax.random.fold_in(stream_key, 3), rows)[jnp.arange(number_of) % rows]
    lots = jnp.where(jnp.arange(rows)[:, None] == fixed_rows[None, :], 1 << 14, lots)
    priority = lots * number_of + jnp.arange(number_of)
    return lax.top_k(priority.astype(jnp.int32), top)[1].astype(jnp.int32)


def normal_values(rng, extent, deviation, bound, pieces=(), held_as=jnp.bfloat16):
    result = deviation * jax.random.normal(rng, extent, jnp.float32)
    if pieces:
        result = result * block_scale(rng, extent, pieces, -0.22, 0.18)
    return jnp.clip(result, -bound, bound).astype(held_as)


def gaussian_with(rng, extent, deviation, limit, split, heavy, kind=jnp.bfloat16):
    drawn = deviation * jax.random.normal(rng, extent, jnp.float32)
    if split:
        drawn = drawn * block_scale(rng, extent, split, -0.22, 0.18)
    return jnp.clip(with_spikes(drawn, jax.random.fold_in(rng, 3), *heavy), -limit, limit).astype(kind)


def setup_inputs(seed: int = 0) -> dict:
    key_list = jax.random.split(jax.random.key(seed), 16)
    return {
        "tokens": gaussian_with(key_list[0], (TOKENS, D), 1.0, 6.0, ((0, 16),), (0, 1, 16, 2.0)),
        "cotangent": gaussian_with(key_list[1], (TOKENS, D), 1.0, 6.0, ((0, 16),), (0, 1, 16, 2.0)),
        "segment_ids": draw_segment_ids(jax.random.fold_in(key_list[15], 71), 0),
        "valid_mask": draw_valid_mask(jax.random.fold_in(key_list[15], 71), 0),
        "frequency": distinct(key_list[4], ROWS, NCLASS, 1, 10922),
        "query_weight": normal_values(key_list[5], (D, H * HD), D ** -0.5, 0.15625, ((0, 16), (1, 2))),
        "key_weight": normal_values(key_list[6], (D, H * HD), D ** -0.5, 0.15625, ((0, 16), (1, 2))),
        "value_weight": normal_values(key_list[7], (D, H * HD), D ** -0.5, 0.15625, ((0, 16), (1, 2))),
        "output_weight": normal_values(key_list[8], (H * HD, D), (H * HD // 2) ** -0.5, 0.25, ((0, 2), (1, 16))),
        "attn_gain": jnp.clip(1.0 + 0.1 * jax.random.normal(key_list[9], (D,), jnp.float32), 0.5, 1.5).astype(jnp.bfloat16),
        "mlp_gain": jnp.clip(1.0 + 0.1 * jax.random.normal(key_list[10], (D,), jnp.float32), 0.5, 1.5).astype(jnp.bfloat16),
        "up_weight": normal_values(key_list[11], (D, FF), D ** -0.5, 0.15625, ((0, 16), (1, 2))),
        "up_bias": normal_values(key_list[12], (FF,), 0.3, 4.0, ((0, 2),)),
        "down_weight": normal_values(key_list[13], (FF, D), (FF // 2) ** -0.5, 0.25, ((0, 2), (1, 16))),
        "down_bias": normal_values(key_list[14], (D,), 0.3, 4.0, ((0, 16),)),
    }


precise = lax.Precision.HIGHEST

@jax.custom_vjp
def low(v):
    return lax.optimization_barrier(v.astype(jnp.bfloat16)).astype(jnp.float32)

@jax.custom_vjp
def low_back(v):
    return v

def low_keep(v):
    return (low(v), None)

def low_pass(kept, grad):
    return (grad,)

def back_keep(v):
    return (v, None)

def back_low(kept, grad):
    return (low(grad),)
low.defvjp(low_keep, low_pass)
low_back.defvjp(back_keep, back_low)

def rms_scale(field):
    return lax.rsqrt(lax.optimization_barrier(jnp.mean(field * field, axis=-1, keepdims=True)) + 1e-06)

def rope_tables(length, width):
    half_width = width // 2
    rates = jnp.exp(-math.log(10000.0) * (2.0 * jnp.arange(half_width, dtype=jnp.float32) / width))
    angles = jnp.arange(length, dtype=jnp.float32)[:, None] * rates[None, :]
    return (jnp.cos(angles)[:, None, :], jnp.sin(angles)[:, None, :])

def rotate(field, cosine_table, sine_table):
    half_width = field.shape[-1] // 2
    first_half = field[..., :half_width]
    second_half = field[..., half_width:]
    return jnp.concatenate([first_half * cosine_table - second_half * sine_table, second_half * cosine_table + first_half * sine_table], axis=-1)

def allowed_pairs(segment_ids, valid_mask):
    places = jnp.arange(segment_ids.shape[1], dtype=jnp.int32)
    same_series = segment_ids[:, :, None] == segment_ids[:, None, :]
    causal = places[None, :, None] >= places[None, None, :]
    visible = (valid_mask[:, None, :] == 1) | (places[None, :, None] == places[None, None, :])
    return (same_series & causal & visible)[:, None, :, :]

def layer_block(inputs, segment_ids, valid_mask, params):
    wq, wk, wv, wo, gain_one, gain_two, w_up, b_up, w_down, b_down = params
    block_rows = segment_ids.shape[0]
    head_count = wq.shape[1] // HD
    shape_four = (block_rows, PATCHES, head_count, HD)
    cosine_table, sine_table = rope_tables(PATCHES, HD)
    normed_one = low(inputs * rms_scale(inputs) * gain_one)
    query_pre = low_back(jnp.dot(normed_one, wq, precision=precise))
    key_pre = low_back(jnp.dot(normed_one, wk, precision=precise))
    value_pre = low_back(jnp.dot(normed_one, wv, precision=precise))
    queries = low(rotate(query_pre.reshape(shape_four), cosine_table, sine_table))
    key_rot = low(rotate(key_pre.reshape(shape_four), cosine_table, sine_table))
    values = low(value_pre).reshape(shape_four)
    scores = low_back(jnp.einsum('rqhd,rkhd->rhqk', queries, key_rot, precision=precise) / math.sqrt(HD))
    scores = jnp.where(allowed_pairs(segment_ids, valid_mask), scores, -1e+30)
    exponent = jnp.exp(scores - lax.optimization_barrier(jnp.max(scores, axis=-1, keepdims=True)))
    softmax_out = exponent / lax.optimization_barrier(jnp.sum(exponent, axis=-1, keepdims=True))
    mixture = jnp.einsum('rhqk,rkhd->rqhd', low(softmax_out), values, precision=precise)
    mixture = low(low_back(mixture.reshape(block_rows * PATCHES, head_count * HD)))
    attention = low_back(jnp.dot(mixture, wo, precision=precise))
    hidden = inputs + attention
    normed_two = low(hidden * rms_scale(hidden) * gain_two)
    pre_act = low_back(jnp.dot(normed_two, w_up, precision=precise) + b_up)
    activated = low(jax.nn.silu(pre_act))
    feed_out = low_back(jnp.dot(activated, w_down, precision=precise) + b_down)
    return hidden + feed_out

def reference(tokens, cotangent, segment_ids, valid_mask, frequency, query_weight, key_weight, value_weight, output_weight, attn_gain, mlp_gain, up_weight, up_bias, down_weight, down_bias):
    member = (frequency == jnp.arange(NCLASS, dtype=jnp.int32)[None, :]).astype(jnp.int32)
    row_valid = lax.optimization_barrier(jnp.sum(valid_mask, axis=1))
    class_count = lax.optimization_barrier(jnp.sum(member * row_valid[:, None], axis=0))
    total = jnp.sum(class_count)
    row_count = lax.optimization_barrier(jnp.sum(member * class_count[None, :], axis=1))
    row_weight = total.astype(jnp.float32) / (NCLASS * row_count.astype(jnp.float32))
    token_weight = (valid_mask.astype(jnp.float32) * row_weight[:, None]).reshape(TOKENS, 1)
    upstream = cotangent.astype(jnp.float32) * token_weight
    params = tuple((weight.astype(jnp.float32) for weight in (query_weight, key_weight, value_weight, output_weight, attn_gain, mlp_gain, up_weight, up_bias, down_weight, down_bias)))
    segment_blocks = segment_ids.reshape(N_DP, ROWS_DEV, PATCHES)
    valid_blocks = valid_mask.reshape(N_DP, ROWS_DEV, PATCHES)

    def forward(inputs, weights):
        block_fn = jax.checkpoint(partial(layer_block, params=weights))
        token_blocks = inputs.reshape(N_DP, TOK_DEV, D)
        outputs = lax.map(lambda item: block_fn(item[0], item[1], item[2]), (token_blocks, segment_blocks, valid_blocks))
        return outputs.reshape(TOKENS, D)
    layer, pullback = jax.vjp(forward, tokens.astype(jnp.float32), params)
    input_grad, grads = pullback(upstream)
    return (layer.astype(jnp.bfloat16), input_grad, grads[0], grads[1], grads[2], grads[3], grads[4], grads[5], grads[6], grads[7], grads[8], grads[9])
```

```python
import functools
import math

import jax
import jax.numpy as jnp
from jax import lax
from jax.experimental import pallas as pl
from jax.experimental.pallas import tpu as pltpu
from jax.sharding import PartitionSpec as P

HD = 80
NCLASS = 3
EXTRA = 16
BF = jnp.bfloat16
F32 = jnp.float32


def pairs(move):
    out = []
    for z in range(4):
        for y in range(2):
            for x in range(2):
                a, b, c = move(z, y, x)
                out.append(((z * 2 + y) * 2 + x, (a * 2 + b) * 2 + c))
    return out


def over_x(field):
    return lax.ppermute(field, "dp", pairs(lambda z, y, x: (z, y, 1 - x)))


def over_y(field):
    return lax.ppermute(field, "dp", pairs(lambda z, y, x: (z, 1 - y, x)))


def up_z(field):
    return lax.ppermute(field, "dp", pairs(lambda z, y, x: ((z + 1) % 4, y, x)))


def over_mp(field):
    return lax.ppermute(field, "mp", [(0, 1), (1, 0)])


def gather_square(block):
    half = block.shape[0] // 2
    from_x = over_x(block)
    from_y = over_y(block)
    first = over_y(from_x[:half])
    second = over_x(from_y[half:])
    return jnp.stack([block, from_x, from_y, jnp.concatenate([first, second])])


def gather_line(block):
    parts = [block]
    for _ in range(3):
        parts.append(up_z(parts[-1]))
    return jnp.stack(parts)


def relative_of_absolute():
    me = lax.axis_index("dp")
    z, y, x = me // 4, (me // 2) % 2, me % 2
    absolute = jnp.arange(16, dtype=jnp.int32)
    za, ya, xa = absolute // 4, (absolute // 2) % 2, absolute % 2
    return (z - za + 4) % 4, (y ^ ya) * 2 + (x ^ xa)


def gather_rows(first, second):
    if lax.axis_size("dp") != 16:
        return tuple(lax.all_gather(f, "dp") for f in (first, second))
    line, square = relative_of_absolute()
    one = gather_line(gather_square(first).reshape(-1, first.shape[1]))
    one = one.reshape((16,) + first.shape)
    two = gather_square(gather_line(second).reshape(-1, second.shape[1]))
    two = two.reshape((16,) + second.shape)
    return jnp.take(one, line * 4 + square, axis=0), jnp.take(two, square * 4 + line, axis=0)


def scatter_square(parts):
    half = parts.shape[1] // 2
    diagonal = parts[3].astype(BF)
    via_x = over_x(diagonal[:half])
    via_y = over_y(diagonal[half:])
    to_y = jnp.concatenate([parts[2, :half] + via_x.astype(F32), parts[2, half:]]).astype(BF)
    to_x = jnp.concatenate([parts[1, :half], parts[1, half:] + via_y.astype(F32)]).astype(BF)
    return parts[0] + (over_x(to_x).astype(F32) + over_y(to_y).astype(F32))


def scatter_line(parts):
    total = parts[1]
    for k in (2, 3, 0):
        total = parts[k] + up_z(total.astype(BF)).astype(F32)
    return total


def scatter_rows(first, second):
    if lax.axis_size("dp") != 16:
        return tuple(
            lax.psum_scatter(f, "dp", scatter_dimension=0, tiled=False) for f in (first, second)
        )
    me = lax.axis_index("dp")
    z, y, x = me // 4, (me // 2) % 2, me % 2
    k = jnp.arange(4, dtype=jnp.int32)
    za = (z - k + 4) % 4
    sa = (y ^ (k // 2)) * 2 + (x ^ (k % 2))
    one = jnp.take(first, (za[:, None] * 4 + sa[None, :]).reshape(-1), axis=0)
    two = jnp.take(second, (sa[:, None] + za[None, :] * 4).reshape(-1), axis=0)
    cols = first.shape[2]
    one = scatter_line(one.reshape(4, -1, cols))
    one = scatter_square(one.reshape(4, -1, cols))
    two = scatter_square(two.reshape(4, -1, cols))
    two = scatter_line(two.reshape(4, -1, cols))
    return one, two


def rms_scale(field):
    return lax.rsqrt(jnp.mean(field * field, axis=-1, keepdims=True) + 1e-06)


def rope_tables(length, width):
    half_width = width // 2
    rates = jnp.exp(-math.log(10000.0) * (2.0 * jnp.arange(half_width, dtype=jnp.float32) / width))
    angles = jnp.arange(length, dtype=jnp.float32)[:, None] * rates[None, :]
    return (jnp.cos(angles)[:, None, :], jnp.sin(angles)[:, None, :])


def rotate(field, cosine_table, sine_table):
    half_width = field.shape[-1] // 2
    first_half = field[..., :half_width]
    second_half = field[..., half_width:]
    return jnp.concatenate(
        [
            first_half * cosine_table - second_half * sine_table,
            second_half * cosine_table + first_half * sine_table,
        ],
        axis=-1,
    )


def allowed_pairs(segment_ids, valid_mask):
    places = jnp.arange(segment_ids.shape[1], dtype=jnp.int32)
    same_series = segment_ids[:, :, None] == segment_ids[:, None, :]
    causal = places[None, :, None] >= places[None, None, :]
    visible = (valid_mask[:, None, :] == 1) | (places[None, :, None] == places[None, None, :])
    return (same_series & causal & visible)[:, None, :, :]


def norm_back(field, scale, gain, grad):
    gain_grad = jnp.sum(grad * field * scale, axis=0)
    scaled = grad * gain
    inner = jnp.mean(scaled * field, axis=-1, keepdims=True)
    return (gain_grad, scale * scaled - field * (scale * scale * scale) * inner)


def two_parts(vector):
    high = vector.astype(BF).astype(F32)
    return high, vector - high


def local(
    tokens,
    cotangent,
    segment_ids,
    valid_mask,
    frequency,
    query_weight,
    key_weight,
    value_weight,
    output_weight,
    attn_gain,
    mlp_gain,
    up_weight,
    up_bias,
    down_weight,
    down_bias,
):
    dp = lax.axis_size("dp")
    block_rows, patches = segment_ids.shape
    token_count = block_rows * patches
    share, head_width = query_weight.shape
    width = tokens.shape[1]
    local_heads = head_width // HD
    shape_four = (block_rows, patches, local_heads, HD)
    score_root = math.sqrt(HD)
    member = (frequency == jnp.arange(NCLASS, dtype=jnp.int32)[None, :]).astype(jnp.int32)
    row_valid = jnp.sum(valid_mask, axis=1)
    local_counts = jnp.sum(member * row_valid[:, None], axis=0)
    small = jnp.concatenate(
        [attn_gain, mlp_gain, down_bias, (local_counts // 16).astype(BF), (local_counts % 16).astype(BF)]
    )
    extra = jnp.pad(small[None, :], ((0, EXTRA - 1), (0, head_width - small.shape[0])))
    got_v, got_qk = gather_rows(
        value_weight, jnp.concatenate([query_weight, key_weight, extra])
    )
    wv_full = got_v.reshape(width, head_width)
    wq_full = got_qk[:, :share].reshape(width, head_width)
    wk_full = got_qk[:, share : 2 * share].reshape(width, head_width)
    small_all = got_qk[:, 2 * share, :]
    gain_one = small_all[:, :share].reshape(width).astype(F32)
    gain_two = small_all[:, share : 2 * share].reshape(width).astype(F32)
    bias_two = small_all[:, 2 * share : 3 * share].reshape(width).astype(F32)
    counts = small_all[:, 3 * share : 3 * share + 2 * NCLASS].astype(F32)
    counts = jnp.sum(counts, axis=0)
    class_count = (counts[:NCLASS] * 16.0 + counts[NCLASS:]).astype(jnp.int32)

    second_in = (output_weight.T, up_weight, down_weight.T)
    got_qk, second_in = lax.optimization_barrier((got_qk, second_in))
    wo_t, up_rows, down_t = second_in
    got_o, got_ud = gather_rows(wo_t, jnp.concatenate([up_rows, down_t]))
    wo_t = got_o.reshape(width, head_width)
    up_full = got_ud[:, :share].reshape(width, head_width)
    down_t = got_ud[:, share:].reshape(width, head_width)

    total = jnp.sum(class_count)
    row_count = jnp.sum(member * class_count[None, :], axis=1)
    row_weight = total.astype(jnp.float32) / (NCLASS * row_count.astype(jnp.float32))
    token_weight = (valid_mask.astype(jnp.float32) * row_weight[:, None]).reshape(token_count, 1)
    upstream = cotangent.astype(jnp.float32) * token_weight

    cosine_table, sine_table = rope_tables(patches, HD)
    allowed = allowed_pairs(segment_ids, valid_mask)
    inputs = tokens.astype(jnp.float32)
    scale_one = rms_scale(inputs)
    normed_one = (inputs * scale_one * gain_one).astype(jnp.bfloat16)
    query_pre = jnp.dot(normed_one, wq_full, preferred_element_type=jnp.float32)
    key_pre = jnp.dot(normed_one, wk_full, preferred_element_type=jnp.float32)
    value_pre = jnp.dot(normed_one, wv_full, preferred_element_type=jnp.float32)
    queries = rotate(query_pre.reshape(shape_four), cosine_table, sine_table).astype(jnp.bfloat16)
    key_rot = rotate(key_pre.reshape(shape_four), cosine_table, sine_table).astype(jnp.bfloat16)
    values = value_pre.reshape(shape_four).astype(jnp.bfloat16)
    scores = (
        jnp.einsum("rqhd,rkhd->rhqk", queries, key_rot, preferred_element_type=jnp.float32)
        / score_root
    )
    scores = jnp.where(allowed, scores, -1e30)
    exponent = jnp.exp(scores - jnp.max(scores, axis=-1, keepdims=True))
    softmax_out = exponent / jnp.sum(exponent, axis=-1, keepdims=True)
    softmax_low = softmax_out.astype(jnp.bfloat16)
    mixture = jnp.einsum("rhqk,rkhd->rqhd", softmax_low, values, preferred_element_type=jnp.float32)
    mixture = mixture.reshape(token_count, head_width).astype(jnp.bfloat16)
    attn_part = jnp.einsum("nc,dc->nd", mixture, wo_t, preferred_element_type=jnp.float32).astype(BF)
    hidden = inputs + (attn_part.astype(F32) + over_mp(attn_part).astype(F32))
    scale_two = rms_scale(hidden)
    normed_two = (hidden * scale_two * gain_two).astype(jnp.bfloat16)
    pre_act = jnp.dot(normed_two, up_full, preferred_element_type=jnp.float32) + up_bias.astype(
        jnp.float32
    )
    activated = jax.nn.silu(pre_act).astype(jnp.bfloat16)
    down_part = jnp.einsum("nf,df->nd", activated, down_t, preferred_element_type=jnp.float32)
    down_part = down_part.astype(BF)
    layer_out = hidden + (down_part.astype(F32) + over_mp(down_part).astype(F32) + bias_two)
    layer_out = layer_out.astype(BF)

    down_low = upstream.astype(jnp.bfloat16)
    down_bias_local = jnp.sum(down_low, axis=0, dtype=jnp.float32)
    down_weight_local = jnp.einsum(
        "nd,nf->df", down_low, activated, preferred_element_type=jnp.float32
    )
    act_grad = jnp.dot(down_low, down_t, preferred_element_type=jnp.float32)
    sigmoid_val = jax.nn.sigmoid(pre_act)
    pre_grad = (act_grad * sigmoid_val * (1.0 + pre_act * (1.0 - sigmoid_val))).astype(jnp.bfloat16)
    up_bias_local = jnp.sum(pre_grad, axis=0, dtype=jnp.float32)
    up_weight_local = jnp.einsum(
        "nd,nf->df", normed_two, pre_grad, preferred_element_type=jnp.float32
    )
    normed_two_part = jnp.einsum(
        "nf,df->nd", pre_grad, up_full, preferred_element_type=jnp.float32
    ).astype(BF)
    normed_two_grad = normed_two_part.astype(F32) + over_mp(normed_two_part).astype(F32)
    mlp_gain_local, hidden_from_norm = norm_back(hidden, scale_two, gain_two, normed_two_grad)
    hidden_grad = upstream + hidden_from_norm

    attn_low = hidden_grad.astype(jnp.bfloat16)
    output_local = jnp.einsum("nd,nc->dc", attn_low, mixture, preferred_element_type=jnp.float32)

    blocks = lambda grad: grad.reshape(dp, share, head_width)
    bias_rows = jnp.stack([jnp.broadcast_to(v, (dp, head_width)) for v in two_parts(up_bias_local)], 1)
    vectors = [v.reshape(dp, share) for f in (mlp_gain_local, down_bias_local) for v in two_parts(f)]
    vector_row = jnp.concatenate(vectors, 1)
    vector_row = jnp.pad(vector_row, ((0, 0), (0, head_width - vector_row.shape[1])))
    rows = jnp.concatenate([bias_rows, vector_row[:, None]], 1)
    rows = jnp.pad(rows, ((0, 0), (0, EXTRA - 3), (0, 0)))
    sum_o, sum_ud = scatter_rows(
        blocks(output_local),
        jnp.concatenate([blocks(up_weight_local), blocks(down_weight_local), rows], 1),
    )
    output_grad = sum_o.T
    up_weight_grad = sum_ud[:share]
    down_weight_grad = sum_ud[share : 2 * share].T
    up_bias_grad = sum_ud[2 * share] + sum_ud[2 * share + 1]
    vec = sum_ud[2 * share + 2]
    mlp_gain_grad = vec[:share] + vec[share : 2 * share]
    down_bias_grad = vec[2 * share : 3 * share] + vec[3 * share : 4 * share]

    mixture_grad = jnp.dot(attn_low, wo_t, preferred_element_type=jnp.float32)
    mixture_grad = mixture_grad.astype(jnp.bfloat16).reshape(shape_four)
    softmax_grad = jnp.einsum(
        "rqhd,rkhd->rhqk", mixture_grad, values, preferred_element_type=jnp.float32
    )
    value_pre_grad = jnp.einsum(
        "rhqk,rqhd->rkhd", softmax_low, mixture_grad, preferred_element_type=jnp.float32
    )
    value_pre_grad = value_pre_grad.reshape(token_count, head_width).astype(jnp.bfloat16)
    scores_grad = softmax_out * (
        softmax_grad - jnp.sum(softmax_out * softmax_grad, axis=-1, keepdims=True)
    )
    scores_grad = scores_grad.astype(jnp.bfloat16)
    query_rot_grad = (
        jnp.einsum("rhqk,rkhd->rqhd", scores_grad, key_rot, preferred_element_type=jnp.float32)
        / score_root
    )
    key_rot_grad = (
        jnp.einsum("rhqk,rqhd->rkhd", scores_grad, queries, preferred_element_type=jnp.float32)
        / score_root
    )
    query_pre_grad = (
        rotate(query_rot_grad, cosine_table, -sine_table)
        .reshape(token_count, head_width)
        .astype(jnp.bfloat16)
    )
    key_pre_grad = (
        rotate(key_rot_grad, cosine_table, -sine_table)
        .reshape(token_count, head_width)
        .astype(jnp.bfloat16)
    )
    query_local = jnp.einsum(
        "nd,nc->dc", normed_one, query_pre_grad, preferred_element_type=jnp.float32
    )
    key_local = jnp.einsum(
        "nd,nc->dc", normed_one, key_pre_grad, preferred_element_type=jnp.float32
    )
    value_local = jnp.einsum(
        "nd,nc->dc", normed_one, value_pre_grad, preferred_element_type=jnp.float32
    )
    normed_one_part = jnp.einsum(
        "nc,dc->nd", query_pre_grad, wq_full, preferred_element_type=jnp.float32
    )
    normed_one_part = normed_one_part + jnp.einsum(
        "nc,dc->nd", key_pre_grad, wk_full, preferred_element_type=jnp.float32
    )
    normed_one_part = normed_one_part + jnp.einsum(
        "nc,dc->nd", value_pre_grad, wv_full, preferred_element_type=jnp.float32
    )
    normed_one_part = normed_one_part.astype(BF)
    normed_one_grad = normed_one_part.astype(F32) + over_mp(normed_one_part).astype(F32)
    attn_gain_local, input_from_norm = norm_back(inputs, scale_one, gain_one, normed_one_grad)
    input_grad = hidden_grad + input_from_norm
    gain_row = jnp.concatenate([v.reshape(dp, share) for v in two_parts(attn_gain_local)], 1)
    gain_row = jnp.pad(gain_row, ((0, 0), (0, head_width - gain_row.shape[1])))[:, None]
    gain_row = jnp.pad(gain_row, ((0, 0), (0, EXTRA - 1), (0, 0)))
    sum_v, sum_qk = scatter_rows(
        blocks(value_local),
        jnp.concatenate([blocks(query_local), blocks(key_local), gain_row], 1),
    )
    query_grad = sum_qk[:share]
    key_grad = sum_qk[share : 2 * share]
    value_grad = sum_v
    attn_gain_grad = sum_qk[2 * share, :share] + sum_qk[2 * share, share : 2 * share]
    return (
        layer_out,
        input_grad,
        query_grad,
        key_grad,
        value_grad,
        output_grad,
        attn_gain_grad,
        mlp_gain_grad,
        up_weight_grad,
        up_bias_grad,
        down_weight_grad,
        down_bias_grad,
    )


def solution(mesh):
    rows = P("dp", None)
    wide = P("dp", "mp")
    tall = P("mp", "dp")
    return jax.shard_map(
        local,
        mesh=mesh,
        in_specs=(rows,) * 5
        + (wide, wide, wide, tall, P("dp"), P("dp"), wide, P("mp"), tall, P("dp")),
        out_specs=(rows, rows, wide, wide, wide, tall, P("dp"), P("dp"), wide, P("mp"), tall, P("dp")),
        check_vma=False,
    )
```

```python
import functools
import math

import jax
import jax.numpy as jnp
import numpy as np
from jax import lax
from jax.experimental import pallas as pl
from jax.experimental.pallas import tpu as pltpu
from jax.sharding import PartitionSpec as P

HD = 80
NCLASS = 3
PATCHES = 16
EXTRA = 16
TILE = 352
BLOCKS = {352: (128, 128, 96), 176: (96, 80)}[TILE]
LANES = 128
BF = jnp.bfloat16
F32 = jnp.float32
ROOT = math.sqrt(HD)
VMEM_LIMIT = 48 * 1024 * 1024


def pairs(move):
    out = []
    for z in range(4):
        for y in range(2):
            for x in range(2):
                a, b, c = move(z, y, x)
                out.append(((z * 2 + y) * 2 + x, (a * 2 + b) * 2 + c))
    return out


def over_x(field):
    return lax.ppermute(field, "dp", pairs(lambda z, y, x: (z, y, 1 - x)))


def over_y(field):
    return lax.ppermute(field, "dp", pairs(lambda z, y, x: (z, 1 - y, x)))


def up_z(field):
    return lax.ppermute(field, "dp", pairs(lambda z, y, x: ((z + 1) % 4, y, x)))


def up_z_two(field):
    return lax.ppermute(field, "dp", pairs(lambda z, y, x: ((z + 2) % 4, y, x)))


def over_mp(field):
    return lax.ppermute(field, "mp", [(0, 1), (1, 0)])


def gridded():
    return lax.axis_size("dp") == 16


def chip_order():
    me = lax.axis_index("dp")
    z, y, x = me // 4, (me // 2) % 2, me % 2
    k = jnp.arange(16, dtype=jnp.int32)
    line, square = k // 4, k % 4
    return ((z - line + 4) % 4) * 4 + (y ^ (square // 2)) * 2 + (x ^ (square % 2))


def gather_square_first(block):
    if not gridded():
        return ("whole", (lax.all_gather(block, "dp"),))
    half = block.shape[0] // 2
    from_x = over_x(block)
    from_y = over_y(block)
    first = over_y(from_x[:half])
    second = over_x(from_y[half:])
    parts = [jnp.concatenate([block, from_x, from_y, first, second]).reshape((4,) + block.shape)]
    for _ in range(3):
        parts.append(up_z(parts[-1]))
    return ("line", tuple(parts))


def gather_line_first(block):
    if not gridded():
        return ("whole", (lax.all_gather(block, "dp"),))
    parts = [block]
    for _ in range(3):
        parts.append(up_z(parts[-1]))
    own = jnp.stack(parts)
    from_x = over_x(own)
    from_y = over_y(own)
    first = over_y(from_x[:2])
    second = over_x(from_y[2:])
    return ("square", (own, from_x, from_y, first, second))


def pieces(kind):
    if kind == "line":
        return [(k, s, k, s) for k in range(4) for s in range(4)]
    out = [(s, k, k, s) for s in range(3) for k in range(4)]
    return out + [(3 + k // 2, k % 2, k, 3) for k in range(4)]


def scatter_square_sum(own, gx, gy, first, second):
    via_x = over_x(first)
    via_y = over_y(second)
    to_y = jnp.concatenate([(gy[:2].astype(F32) + via_x.astype(F32)).astype(BF), gy[2:]])
    to_x = jnp.concatenate([gx[:2], (gx[2:].astype(F32) + via_y.astype(F32)).astype(BF)])
    return own, over_x(to_x), over_y(to_y)


def scatter_square_first(parts):
    if not gridded():
        return lax.psum_scatter(parts[0].astype(F32), "dp", scatter_dimension=0, tiled=True)
    terms = scatter_square_sum(*parts)
    at = lambda k: sum(t[k].astype(F32) for t in terms)
    total = at(1)
    for k in (2, 3, 0):
        total = at(k) + up_z(total.astype(BF)).astype(F32)
    return total


def scatter_line_first(parts):
    if not gridded():
        return lax.psum_scatter(parts[0].astype(F32), "dp", scatter_dimension=0, tiled=True)
    total = parts[1]
    for k in (2, 3, 0):
        total = (parts[k].astype(F32) + up_z(total).astype(F32)).astype(BF)
    half = total.shape[1] // 2
    via_x = over_x(total[3, :half])
    via_y = over_y(total[3, half:])
    to_y = jnp.concatenate([(total[2, :half].astype(F32) + via_x.astype(F32)).astype(BF), total[2, half:]])
    to_x = jnp.concatenate([total[1, :half], (total[1, half:].astype(F32) + via_y.astype(F32)).astype(BF)])
    return total[0].astype(F32) + (over_x(to_x).astype(F32) + over_y(to_y).astype(F32))


def sum_small(field):
    if not gridded():
        return lax.psum(field, "dp")
    field = field + over_x(field)
    field = field + over_y(field)
    field = field + up_z_two(field)
    return field + lax.ppermute(field, "dp", pairs(lambda z, y, x: (z ^ 1, y, x)))


NN = (((1,), (0,)), ((), ()))
NT = (((1,), (1,)), ((), ()))
TN = (((0,), (0,)), ((), ()))


def dot(a, b, dims=NN):
    return lax.dot_general(a, b, dims, preferred_element_type=F32)


class Weights:
    def __init__(self, wanted, share):
        self.share = share
        self.wanted = wanted
        self.arrays = []
        for (kind, group), _, _ in wanted:
            for array in group:
                if not any(array is a for a in self.arrays):
                    self.arrays.append(array)

    def specs(self):
        return [pl.BlockSpec(memory_space=pl.ANY)] * len(self.arrays)

    def start(self, which, refs, order, into, sem):
        (kind, group), row, rows = self.wanted[which]
        find = lambda array: refs[[a is array for a in self.arrays].index(True)]
        if kind == "whole":
            chips = group[0].shape[0]
            if rows % 16 == 0 and row % 16 == 0:
                def body(c, carry):
                    to = into.at[pl.ds(pl.multiple_of(c * rows, 16), rows)]
                    pltpu.make_async_copy(find(group[0]).at[c, pl.ds(row, rows)], to, sem).start()
                    return carry
                lax.fori_loop(0, chips, body, 0)
            else:
                raise ValueError("rows")
            return
        for array, index, line, square in pieces(kind):
            chip = order[line * 4 + square]
            to = into.at[pl.ds(pl.multiple_of(chip * rows, 16), rows)]
            pltpu.make_async_copy(find(group[array]).at[index, pl.ds(row, rows)], to, sem).start()


def wait_all(into, sem):
    pltpu.make_async_copy(into, into, sem).wait()


def tile_spec(shape):
    if len(shape) == 3:
        return pl.BlockSpec((shape[0], TILE, shape[2]), lambda i: (0, i, 0))
    return pl.BlockSpec((TILE, shape[1]), lambda i: (i, 0))


def whole_spec(shape):
    return pl.BlockSpec(shape, lambda i: (0,) * len(shape))


def run(name, body, order, tiles, wholes, weights, out_tiles, out_wholes, scratch=(), flops=0, extra_bytes=0):
    tokens = tiles[0].shape[1] if tiles[0].ndim == 3 else tiles[0].shape[0]
    inputs = [order, *tiles, *wholes, *(weights.arrays if weights else ())]
    outs = [*out_tiles, *out_wholes]
    in_specs = [pl.BlockSpec(memory_space=pltpu.SMEM)]
    in_specs += [tile_spec(a.shape) for a in tiles] + [whole_spec(a.shape) for a in wholes]
    if weights:
        in_specs += weights.specs()
    cost = sum(math.prod(a.shape) * a.dtype.itemsize for a in [*inputs[1:], *outs])
    result = pl.pallas_call(
        body,
        name=name,
        grid=(tokens // TILE,),
        in_specs=in_specs,
        out_specs=[tile_spec(o.shape) for o in out_tiles] + [whole_spec(o.shape) for o in out_wholes],
        out_shape=outs,
        scratch_shapes=list(scratch),
        compiler_params=pltpu.CompilerParams(
            vmem_limit_bytes=VMEM_LIMIT, dimension_semantics=("arbitrary",)
        ),
        cost_estimate=pl.CostEstimate(flops=int(flops), bytes_accessed=int(cost), transcendentals=0),
    )(*inputs)
    return result


def window(h):
    first = h * HD // LANES
    return first, (h * HD + HD - 1) // LANES - first + 1


def head_lanes(h):
    first, count = window(h)
    lane = lax.broadcasted_iota(jnp.int32, (1, count * LANES), 1) + first * LANES
    return (lane >= h * HD) & (lane < h * HD + HD)


def columns(h):
    first, count = window(h)
    return slice(first * LANES, (first + count) * LANES)


def add_window(sums, h, part):
    first, count = window(h)
    for c in range(count):
        piece = part[:, c * LANES : (c + 1) * LANES]
        sums[first + c] = piece if sums[first + c] is None else sums[first + c] + piece


def rope(v, cos, left_sin, right_sin):
    rows, cols = v.shape
    left = pltpu.roll(v, cols - HD // 2, 1)
    right = pltpu.roll(v, HD // 2, 1)
    three = lambda f: f.reshape(rows // PATCHES, PATCHES, cols)
    out = three(v) * cos[...] + three(left) * left_sin + three(right) * right_sin
    return out.reshape(rows, cols)


def rope_tables(heads):
    half = HD // 2
    i = np.arange(half, dtype=np.float32)
    rates = np.exp(np.float32(-math.log(10000.0)) * (np.float32(2.0) * i / np.float32(HD))).astype(np.float32)
    angle = np.arange(PATCHES, dtype=np.float32)[:, None] * rates[None, :]
    cos, sin = np.cos(angle).astype(np.float32), np.sin(angle).astype(np.float32)
    zero = np.zeros_like(sin)
    full = lambda a, b: np.tile(np.concatenate([a, b], 1), (1, heads))
    return full(cos, cos), full(-sin, zero), full(zero, sin)


def row_of(small, at):
    return jnp.concatenate([small[at : at + 1, :], small[at + 1 : at + 2, :]], axis=1)


def token_weight(info, small):
    counts = [small[6:7, c : c + 1] * 16.0 + small[6:7, NCLASS + c : NCLASS + c + 1] for c in range(NCLASS)]
    total = counts[0] + counts[1] + counts[2]
    return sum(info[:, 1 + c : 2 + c] * (total / (NCLASS * counts[c])) for c in range(NCLASS))


def scale_of(field):
    return lax.rsqrt(jnp.mean(field * field, axis=-1, keepdims=True) + 1e-06)


def attention_forward(order, tokens, info, coderow, cos, left_sin, right_sin, weights, share, heads):
    cols, width = heads * HD, tokens.shape[1]
    chips = width // share
    count = tokens.shape[0]
    n_pieces = len(weights.arrays)

    def body(order, tokens, info, coderow, cos, left_sin, right_sin, *refs):
        got, refs = refs[:n_pieces], refs[n_pieces:]
        normed, q_out, k_out, v_out, probs, mixture, small, w, extras, sems = refs
        step = pl.program_id(0)

        @pl.when(step == 0)
        def _():
            weights.start(3, got, order, extras, sems.at[3])
            for n in range(3):
                weights.start(n, got, order, w.at[n], sems.at[n])
            wait_all(extras, sems.at[3])
            total = extras[pl.ds(0, EXTRA)].astype(F32)
            for c in range(1, chips):
                total = total + extras[pl.ds(c * EXTRA, EXTRA)].astype(F32)
            small[...] = total

        x = tokens[...].astype(F32)
        normed[...] = (x * scale_of(x) * row_of(small, 0)).astype(BF)

        @pl.when(step == 0)
        def _():
            for n in range(3):
                wait_all(w.at[n], sems.at[n])

        low = normed[...]
        q_out[...] = rope(dot(low, w[0]), cos, left_sin[...], right_sin[...]).astype(BF)
        k_out[...] = rope(dot(low, w[1]), cos, left_sin[...], right_sin[...]).astype(BF)
        v_out[...] = dot(low, w[2]).astype(BF)
        start = 0
        for b, size in enumerate(BLOCKS):
            rows = slice(start, start + size)
            key_at = lax.broadcasted_iota(jnp.int32, (size, size), 0)
            query_at = lax.broadcasted_iota(jnp.int32, (size, size), 1)
            same = info[rows, 0:1] == coderow[step * len(BLOCKS) + b][:, :size]
            allowed = (same & (key_at < query_at)) | (key_at == query_at)
            sums = [None] * (cols // LANES)
            for h in range(heads):
                here, lanes = columns(h), head_lanes(h)
                query = jnp.where(lanes, q_out[rows, here], jnp.zeros((), BF))
                scores = dot(k_out[rows, here], query, NT) * (1.0 / ROOT)
                scores = jnp.where(allowed, scores, -1e30)
                exponent = jnp.exp(scores - jnp.max(scores, axis=0, keepdims=True))
                soft = exponent * (1.0 / jnp.sum(exponent, axis=0, keepdims=True))
                probs[h, rows, 0:size] = soft
                value = jnp.where(lanes, v_out[rows, here], jnp.zeros((), BF))
                add_window(sums, h, dot(soft.astype(BF), value, TN))
            mixture[rows, :] = jnp.concatenate(sums, axis=1).astype(BF)
            start += size

    shape = jax.ShapeDtypeStruct
    return run(
        "attention_forward",
        body,
        order,
        [tokens, info],
        [coderow, cos, left_sin, right_sin],
        weights,
        [shape((count, width), BF)]
        + [shape((count, cols), BF)] * 3
        + [shape((heads, count, LANES), F32), shape((count, cols), BF)],
        [shape((EXTRA, cols), F32)],
        [
            pltpu.VMEM((3, width, cols), BF),
            pltpu.VMEM((chips * EXTRA, cols), BF),
            pltpu.SemaphoreType.DMA((4,)),
        ],
        flops=6 * count * width * cols,
    )


def attention_backward(order, q, k, v, probs, mixture_grad, cos, left_sin, right_sin, heads):
    count, cols = q.shape

    def body(order, q, k, v, probs, mg, cos, left_sin, right_sin, dq_out, dk_out, dv_out, dq, dk):
        start = 0
        zero = jnp.zeros((), BF)
        for size in BLOCKS:
            rows = slice(start, start + size)
            sums = [[None] * (cols // LANES) for _ in range(3)]
            for h in range(heads):
                here, lanes = columns(h), head_lanes(h)
                soft = probs[h, rows, 0:size]
                grad = jnp.where(lanes, mg[rows, here], zero)
                query = jnp.where(lanes, q[rows, here], zero)
                key = jnp.where(lanes, k[rows, here], zero)
                soft_grad = dot(v[rows, here], grad, NT)
                inner = jnp.sum(soft * soft_grad, axis=0, keepdims=True)
                score_grad = (soft * (soft_grad - inner)).astype(BF)
                add_window(sums[2], h, dot(soft.astype(BF), grad))
                add_window(sums[0], h, dot(score_grad, key, TN))
                add_window(sums[1], h, dot(score_grad, query))
            dv_out[rows, :] = jnp.concatenate(sums[2], axis=1).astype(BF)
            dq[rows, :] = jnp.concatenate(sums[0], axis=1)
            dk[rows, :] = jnp.concatenate(sums[1], axis=1)
            start += size
        for grad, out in ((dq, dq_out), (dk, dk_out)):
            turned = rope(grad[...] * (1.0 / ROOT), cos, -left_sin[...], -right_sin[...])
            out[...] = turned.astype(BF)

    shape = jax.ShapeDtypeStruct
    return run(
        "attention_backward",
        body,
        order,
        [q, k, v, probs, mixture_grad],
        [cos, left_sin, right_sin],
        None,
        [shape((count, cols), BF)] * 3,
        [],
        [pltpu.VMEM((TILE, cols), F32)] * 2,
        flops=12 * count * LANES * cols,
    )


def project_back(name, order, fields, weights):
    count, cols = fields[0].shape
    width = weights.share * (16 if weights.wanted[0][0][0] != "whole" else weights.wanted[0][0][1][0].shape[0])
    n_fields, n_pieces = len(fields), len(weights.arrays)

    def body(order, *refs):
        inputs, got = refs[:n_fields], refs[n_fields : n_fields + n_pieces]
        out, w, sems = refs[n_fields + n_pieces :]

        @pl.when(pl.program_id(0) == 0)
        def _():
            for n in range(n_fields):
                weights.start(n, got, order, w.at[n], sems.at[n])
            for n in range(n_fields):
                wait_all(w.at[n], sems.at[n])

        total = dot(inputs[0][...], w[0], NT)
        for n in range(1, n_fields):
            total = total + dot(inputs[n][...], w[n], NT)
        out[...] = total.astype(BF)

    return run(
        name,
        body,
        order,
        fields,
        [],
        weights,
        [jax.ShapeDtypeStruct((count, width), BF)],
        [],
        [pltpu.VMEM((n_fields, width, cols), BF), pltpu.SemaphoreType.DMA((n_fields,))],
        flops=2 * n_fields * count * width * cols,
    )[0]


def weigh_cotangent(order, cotangent, info, small):
    def body(order, cot, info, small, low, total):
        low[...] = (cot[...].astype(F32) * token_weight(info, small)).astype(BF)
        part = jnp.sum(low[...].astype(F32), axis=0, keepdims=True)
        total[...] = jnp.where(pl.program_id(0) == 0, part, total[...] + part)

    shape = jax.ShapeDtypeStruct
    return run(
        "weigh_cotangent",
        body,
        order,
        [cotangent, info],
        [small],
        None,
        [shape(cotangent.shape, BF)],
        [shape((1, cotangent.shape[1]), F32)],
    )


def mlp_up(order, tokens, mine, other, small, up_bias, weights):
    count, width = tokens.shape
    cols = up_bias.shape[1]
    n_pieces = len(weights.arrays)

    def body(order, tokens, mine, other, small, bias, *refs):
        got = refs[:n_pieces]
        hidden, normed, act, slope, w, sems = refs[n_pieces:]

        @pl.when(pl.program_id(0) == 0)
        def _():
            weights.start(0, got, order, w, sems.at[0])

        field = tokens[...].astype(F32) + (mine[...].astype(F32) + other[...].astype(F32))
        hidden[...] = field
        normed[...] = (field * scale_of(field) * row_of(small, 2)).astype(BF)

        @pl.when(pl.program_id(0) == 0)
        def _():
            wait_all(w, sems.at[0])

        pre = dot(normed[...], w[...]) + bias[...].astype(F32)
        sig = 1.0 / (1.0 + jnp.exp(-pre))
        act[...] = (pre * sig).astype(BF)
        slope[...] = sig * (1.0 + pre * (1.0 - sig))

    shape = jax.ShapeDtypeStruct
    return run(
        "mlp_up",
        body,
        order,
        [tokens, mine, other],
        [small, up_bias],
        weights,
        [shape((count, width), F32), shape((count, width), BF), shape((count, cols), BF), shape((count, cols), F32)],
        [],
        [pltpu.VMEM((width, cols), BF), pltpu.SemaphoreType.DMA((1,))],
        flops=2 * count * width * cols,
    )


def mlp_back(order, low, slope, weights):
    count, width = low.shape
    cols = slope.shape[1]
    n_pieces = len(weights.arrays)

    def body(order, low, slope, *refs):
        got = refs[:n_pieces]
        pre_grad, part, total, w, sems = refs[n_pieces:]

        @pl.when(pl.program_id(0) == 0)
        def _():
            for n in range(2):
                weights.start(n, got, order, w.at[n], sems.at[n])
            for n in range(2):
                wait_all(w.at[n], sems.at[n])

        pre_grad[...] = (dot(low[...], w[0]) * slope[...]).astype(BF)
        grad = pre_grad[...]
        here = jnp.sum(grad.astype(F32), axis=0, keepdims=True)
        total[...] = jnp.where(pl.program_id(0) == 0, here, total[...] + here)
        part[...] = dot(grad, w[1], NT).astype(BF)

    shape = jax.ShapeDtypeStruct
    return run(
        "mlp_back",
        body,
        order,
        [low, slope],
        [],
        weights,
        [shape((count, cols), BF), shape((count, width), BF)],
        [shape((1, cols), F32)],
        [pltpu.VMEM((2, width, cols), BF), pltpu.SemaphoreType.DMA((2,))],
        flops=4 * count * width * cols,
    )


def finish_output(order, hidden, mine, other, small):
    def body(order, hidden, mine, other, small, out):
        down = mine[...].astype(F32) + other[...].astype(F32)
        out[...] = (hidden[...] + (down + row_of(small, 4))).astype(BF)

    return run(
        "finish_output",
        body,
        order,
        [hidden, mine, other],
        [small],
        None,
        [jax.ShapeDtypeStruct(hidden.shape, BF)],
        [],
    )[0]


def hidden_back(order, hidden, mine, other, cotangent, info, small, weights):
    count, width = hidden.shape
    cols = small.shape[1]
    n_pieces = len(weights.arrays)

    def body(order, hidden, mine, other, cot, info, small, *refs):
        got = refs[:n_pieces]
        grad_out, low, mg, total, w, sems = refs[n_pieces:]

        @pl.when(pl.program_id(0) == 0)
        def _():
            weights.start(0, got, order, w, sems.at[0])

        field = hidden[...]
        scale = scale_of(field)
        grad = mine[...].astype(F32) + other[...].astype(F32)
        part = jnp.sum(grad * field * scale, axis=0, keepdims=True)
        total[...] = jnp.where(pl.program_id(0) == 0, part, total[...] + part)
        scaled = grad * row_of(small, 2)
        inner = jnp.mean(scaled * field, axis=-1, keepdims=True)
        upstream = cot[...].astype(F32) * token_weight(info, small)
        result = upstream + (scale * scaled - field * (scale * scale * scale * inner))
        grad_out[...] = result
        low[...] = result.astype(BF)

        @pl.when(pl.program_id(0) == 0)
        def _():
            wait_all(w, sems.at[0])

        mg[...] = dot(low[...], w[...]).astype(BF)

    shape = jax.ShapeDtypeStruct
    return run(
        "hidden_back",
        body,
        order,
        [hidden, mine, other, cotangent, info],
        [small],
        weights,
        [shape((count, width), F32), shape((count, width), BF), shape((count, cols), BF)],
        [shape((1, width), F32)],
        [pltpu.VMEM((width, cols), BF), pltpu.SemaphoreType.DMA((1,))],
        flops=2 * count * width * cols,
    )


def input_back(order, tokens, mine, other, hidden_grad, small):
    def body(order, tokens, mine, other, hidden_grad, small, out, total):
        field = tokens[...].astype(F32)
        scale = scale_of(field)
        grad = mine[...].astype(F32) + other[...].astype(F32)
        part = jnp.sum(grad * field * scale, axis=0, keepdims=True)
        total[...] = jnp.where(pl.program_id(0) == 0, part, total[...] + part)
        scaled = grad * row_of(small, 0)
        inner = jnp.mean(scaled * field, axis=-1, keepdims=True)
        out[...] = hidden_grad[...] + (scale * scaled - field * (scale * scale * scale * inner))

    shape = jax.ShapeDtypeStruct
    return run(
        "input_back",
        body,
        order,
        [tokens, mine, other, hidden_grad],
        [small],
        None,
        [shape(tokens.shape, F32)],
        [shape((1, tokens.shape[1]), F32)],
    )


def weight_grads(name, order, left, rights, kind, share):
    count, width = left.shape
    cols = rights[0].shape[1]
    step_cols = 256
    chips = width // share
    n = len(rights)
    rows = n * share
    if not gridded():
        outs = [(width * n, cols)]
    elif kind == "line":
        outs = [(4, rows, cols)] * 4
    else:
        outs = [(4, rows, cols)] * 3 + [(2, rows, cols)] * 2
    steps = width // step_cols
    meshed = gridded()

    def body(order, left, *refs):
        right, out, (scratch, sem) = refs[:n], refs[n:-2], refs[-2:]
        step = pl.program_id(0)
        for r in range(n):
            at = pl.ds(pl.multiple_of(step * step_cols, step_cols), step_cols)
            scratch[r, at, :] = dot(left[...], right[r][...], TN).astype(BF)

        @pl.when(step == steps - 1)
        def _():
            if not meshed:
                for r in range(n):
                    pltpu.make_async_copy(scratch.at[r], out[0].at[pl.ds(r * width, width)], sem).start()
            else:
                for array, index, line, square in pieces(kind):
                    chip = order[line * 4 + square]
                    for r in range(n):
                        pltpu.make_async_copy(
                            scratch.at[r, pl.ds(pl.multiple_of(chip * share, 16), share)],
                            out[array].at[index, pl.ds(r * share, share)],
                            sem,
                        ).start()
            wait_all(scratch, sem)

    result = pl.pallas_call(
        body,
        name=name,
        grid=(steps,),
        in_specs=[pl.BlockSpec(memory_space=pltpu.SMEM), pl.BlockSpec((count, step_cols), lambda i: (0, i))]
        + [whole_spec((count, cols))] * n,
        out_specs=[pl.BlockSpec(memory_space=pl.ANY)] * len(outs),
        out_shape=[jax.ShapeDtypeStruct(o, BF) for o in outs],
        scratch_shapes=[pltpu.VMEM((n, width, cols), BF), pltpu.SemaphoreType.DMA],
        compiler_params=pltpu.CompilerParams(
            vmem_limit_bytes=VMEM_LIMIT, dimension_semantics=("arbitrary",)
        ),
        cost_estimate=pl.CostEstimate(
            flops=2 * n * count * width * cols,
            bytes_accessed=2 * (count * width + n * count * cols + n * width * cols),
            transcendentals=0,
        ),
    )(order, left, *rights)
    if not meshed and n > 1:
        full = result[0].reshape(n, chips, share, cols)
        return [jnp.moveaxis(full, 0, 1).reshape(width * n, cols)]
    return result


def whole_blocks(gathered, row, rows):
    kind, (array,) = gathered
    part = array[:, row : row + rows]
    return ("whole", (part.reshape(1, -1, part.shape[2]),))


def local(
    tokens,
    cotangent,
    segment_ids,
    valid_mask,
    frequency,
    query_weight,
    key_weight,
    value_weight,
    output_weight,
    attn_gain,
    mlp_gain,
    up_weight,
    up_bias,
    down_weight,
    down_bias,
):
    dp = lax.axis_size("dp")
    me = lax.axis_index("dp")
    block_rows, patches = segment_ids.shape
    count, width = tokens.shape
    share, cols = query_weight.shape
    heads = cols // HD
    order = chip_order()

    member = (frequency == jnp.arange(NCLASS, dtype=jnp.int32)[None, :]).astype(jnp.int32)
    row_valid = jnp.sum(valid_mask, axis=1)
    local_counts = jnp.sum(member * row_valid[:, None], axis=0)
    here = (jnp.arange(dp, dtype=jnp.int32) == me)[:, None]
    vectors = jnp.stack([attn_gain, mlp_gain, down_bias])
    vectors = jnp.where(here[None], vectors[:, None, :], jnp.zeros((), BF)).reshape(6, cols)
    count_row = jnp.concatenate([local_counts // 16, local_counts % 16]).astype(BF)
    count_row = jnp.pad(count_row[None], ((0, 0), (0, cols - 2 * NCLASS)))
    extra = jnp.pad(jnp.concatenate([vectors, count_row]), ((0, EXTRA - 7), (0, 0)))

    code = (jnp.arange(block_rows, dtype=jnp.int32)[:, None] * PATCHES + segment_ids).astype(F32)
    of_class = (valid_mask[:, :, None] * member[:, None, :]).astype(F32).reshape(count, NCLASS)
    key_code = jnp.where(valid_mask == 1, code, -1.0).reshape(count, 1)
    info = jnp.pad(jnp.concatenate([key_code, of_class], 1), ((0, 0), (0, 7 - NCLASS)))
    flat, rows, start = code.reshape(1, count), [], 0
    for _ in range(count // TILE):
        for size in BLOCKS:
            rows.append(jnp.pad(flat[:, start : start + size], ((0, 0), (0, LANES - size))))
            start += size
    coderow = jnp.stack(rows)
    tables = rope_tables(heads)

    got_qk = gather_line_first(jnp.concatenate([query_weight, key_weight, extra]))
    got_v = gather_square_first(value_weight)
    output_rows, down_rows = output_weight.T, down_weight.T
    got_qk_own, output_rows, up_rows, down_rows = lax.optimization_barrier(
        (got_qk[1][0], output_rows, up_weight, down_rows)
    )
    got_qk = (got_qk[0], (got_qk_own,) + got_qk[1][1:])
    got_o = gather_line_first(output_rows)
    got_ud = gather_line_first(jnp.concatenate([up_rows, down_rows]))
    if gridded():
        parts = {
            "q": (got_qk, 0, share),
            "k": (got_qk, share, share),
            "e": (got_qk, 2 * share, EXTRA),
            "v": (got_v, 0, share),
            "o": (got_o, 0, share),
            "u": (got_ud, 0, share),
            "d": (got_ud, share, share),
        }
    else:
        parts = {
            "q": (whole_blocks(got_qk, 0, share), 0, width),
            "k": (whole_blocks(got_qk, share, share), 0, width),
            "e": (whole_blocks(got_qk, 2 * share, EXTRA), 0, dp * EXTRA),
            "v": (whole_blocks(got_v, 0, share), 0, width),
            "o": (whole_blocks(got_o, 0, share), 0, width),
            "u": (whole_blocks(got_ud, 0, share), 0, width),
            "d": (whole_blocks(got_ud, share, share), 0, width),
        }
    take = lambda names: Weights([parts[n] for n in names], width // 16 if gridded() else width)

    normed_one, queries, keys, values, probs, mixture, small = attention_forward(
        order, tokens, info, coderow, *tables, take("qkve"), share, heads
    )
    attn_part = project_back("attention_out", order, [mixture], take("o"))
    attn_other = over_mp(attn_part)
    down_low, down_bias_sum = weigh_cotangent(order, cotangent, info, small)
    hidden, normed_two, activated, slope = mlp_up(
        order, tokens, attn_part, attn_other, small, up_bias[None], take("u")
    )
    pre_grad, normed_two_part, up_bias_sum = mlp_back(order, down_low, slope, take("du"))
    normed_two_other = over_mp(normed_two_part)
    down_part = project_back("mlp_down", order, [activated], take("d"))
    down_other = over_mp(down_part)
    up_local = weight_grads("up_grads", order, normed_two, [pre_grad], "square", share)
    down_local = weight_grads("down_grads", order, down_low, [activated], "square", share)
    layer_out = finish_output(order, hidden, down_part, down_other, small)
    hidden_grad, attn_low, mixture_grad, mlp_gain_sum = hidden_back(
        order, hidden, normed_two_part, normed_two_other, cotangent, info, small, take("o")
    )
    output_local = weight_grads("output_grads", order, attn_low, [mixture], "square", share)
    query_pre_grad, key_pre_grad, value_pre_grad = attention_backward(
        order, queries, keys, values, probs, mixture_grad, *tables, heads
    )
    value_local = weight_grads("value_grads", order, normed_one, [value_pre_grad], "line", share)
    qk_local = weight_grads(
        "query_key_grads", order, normed_one, [query_pre_grad, key_pre_grad], "square", share
    )
    normed_one_part = project_back(
        "attention_in_back", order, [query_pre_grad, key_pre_grad, value_pre_grad], take("qkv")
    )
    normed_one_other = over_mp(normed_one_part)
    input_grad, attn_gain_sum = input_back(
        order, tokens, normed_one_part, normed_one_other, hidden_grad, small
    )

    down_grad = scatter_square_first(down_local)
    up_grad = scatter_square_first(up_local)
    output_grad = scatter_square_first(output_local)
    value_grad = scatter_line_first(value_local)
    qk_grad = scatter_square_first(qk_local)
    sums = sum_small(
        jnp.concatenate(
            [s.reshape(-1, cols) for s in (attn_gain_sum, mlp_gain_sum, down_bias_sum, up_bias_sum)]
            + [jnp.zeros((1, cols), F32)]
        )
    )
    own = lax.dynamic_slice_in_dim(sums[:6].reshape(3, dp, share), me, 1, 1)[:, 0]
    return (
        layer_out,
        input_grad,
        qk_grad[:share],
        qk_grad[share:],
        value_grad,
        output_grad.T,
        own[0],
        own[1],
        up_grad,
        sums[6],
        down_grad.T,
        own[2],
    )


def solution(mesh):
    rows = P("dp", None)
    wide = P("dp", "mp")
    tall = P("mp", "dp")
    return jax.shard_map(
        local,
        mesh=mesh,
        in_specs=(rows,) * 5
        + (wide, wide, wide, tall, P("dp"), P("dp"), wide, P("mp"), tall, P("dp")),
        out_specs=(rows, rows, wide, wide, wide, tall, P("dp"), P("dp"), wide, P("mp"), tall, P("dp")),
        check_vma=False,
    )
```

```python
import math

import jax
import jax.numpy as jnp
import numpy as np
from jax import lax
from jax.experimental import pallas as pl
from jax.experimental.pallas import tpu as pltpu
from jax.sharding import PartitionSpec as P

HD = 80
NCLASS = 3
PATCHES = 16
TILE = 352
LANES = 128
BF = jnp.bfloat16
F32 = jnp.float32
ROOT = math.sqrt(HD)
ROOM = 6 * 1024 * 1024
SMALL = 8


def pairs(move):
    out = []
    for z in range(4):
        for y in range(2):
            for x in range(2):
                a, b, c = move(z, y, x)
                out.append(((z * 2 + y) * 2 + x, (a * 2 + b) * 2 + c))
    return out


def over_x(field):
    return lax.ppermute(field, "dp", pairs(lambda z, y, x: (z, y, 1 - x)))


def over_y(field):
    return lax.ppermute(field, "dp", pairs(lambda z, y, x: (z, 1 - y, x)))


def over_diagonal(field):
    return lax.ppermute(field, "dp", pairs(lambda z, y, x: (z, 1 - y, 1 - x)))


def up_z(field, k):
    return lax.ppermute(field, "dp", pairs(lambda z, y, x: ((z + k) % 4, y, x)))


def over_mp(field):
    return lax.ppermute(field, "mp", [(0, 1), (1, 0)])


def gridded():
    return lax.axis_size("dp") == 16


def chip_order():
    me = lax.axis_index("dp")
    z, y, x = me // 4, (me // 2) % 2, me % 2
    k = jnp.arange(16, dtype=jnp.int32)
    line, square = k // 4, k % 4
    return ((z - line + 4) % 4) * 4 + (y ^ (square // 2)) * 2 + (x ^ (square % 2))


def together(*values):
    return lax.optimization_barrier(values)


def halves(rows):
    cut = (rows // 2 + 15) // 16 * 16
    return slice(0, cut), slice(cut, rows)


def to_line(field, k):
    return up_z(field, 4 - k)


def shifted(block):
    return [block, up_z(block, 1), up_z(block, 2), up_z(block, 3)]


def small_over_square(field):
    return field + (over_x(field) + over_y(field) + over_diagonal(field))


def small_over_line(field):
    return field + (up_z(field, 1) + up_z(field, 2) + up_z(field, 3))


COST = 1.0

NN = (((1,), (0,)), ((), ()))
NT = (((1,), (1,)), ((), ()))
TN = (((0,), (0,)), ((), ()))
shape = jax.ShapeDtypeStruct


def dot(a, b, dims=NN):
    return lax.dot_general(a, b, dims, preferred_element_type=F32)


def run(name, body, inputs, outs, scratch=(), flops=0, order=None, aliases=None):
    specs = [pl.BlockSpec(memory_space=pltpu.VMEM)] * len(inputs)
    if order is not None:
        inputs, specs = [order, *inputs], [pl.BlockSpec(memory_space=pltpu.SMEM), *specs]
    moved = sum(math.prod(a.shape) * a.dtype.itemsize for a in [*inputs, *outs])
    return pl.pallas_call(
        body,
        name=name,
        in_specs=specs,
        out_specs=[pl.BlockSpec(memory_space=pltpu.VMEM)] * len(outs),
        out_shape=outs,
        scratch_shapes=list(scratch),
        input_output_aliases=aliases or {},
        compiler_params=pltpu.CompilerParams(
            vmem_limit_bytes=ROOM + moved + sum(math.prod(f.shape) * f.dtype.itemsize for f in scratch)
        ),
        cost_estimate=pl.CostEstimate(flops=int(COST * flops), bytes_accessed=int(COST * moved), transcendentals=0),
    )(*inputs)


def tiles(count, size=TILE):
    return [slice(start, start + size) for start in range(0, count, size)]


def window(h):
    first = h * HD // LANES
    return first, (h * HD + HD - 1) // LANES - first + 1


def head_lanes(h):
    first, count = window(h)
    lane = lax.broadcasted_iota(jnp.int32, (1, count * LANES), 1) + first * LANES
    return (lane >= h * HD) & (lane < h * HD + HD)


def columns(h):
    first, count = window(h)
    return slice(first * LANES, (first + count) * LANES)


def add_window(sums, h, part):
    first, count = window(h)
    for c in range(count):
        piece = part[:, c * LANES : (c + 1) * LANES]
        sums[first + c] = piece if sums[first + c] is None else sums[first + c] + piece


def rope(v, cos, left_sin, right_sin):
    rows, cols = v.shape
    left = pltpu.roll(v, cols - HD // 2, 1)
    right = pltpu.roll(v, HD // 2, 1)
    three = lambda f: f.reshape(rows // PATCHES, PATCHES, cols)
    out = three(v) * cos + three(left) * left_sin + three(right) * right_sin
    return out.reshape(rows, cols)


def rope_tables(heads):
    half = HD // 2
    i = np.arange(half, dtype=np.float32)
    rates = np.exp(np.float32(-math.log(10000.0)) * (np.float32(2.0) * i / np.float32(HD))).astype(np.float32)
    angle = np.arange(PATCHES, dtype=np.float32)[:, None] * rates[None, :]
    cos, sin = np.cos(angle).astype(np.float32), np.sin(angle).astype(np.float32)
    zero = np.zeros_like(sin)
    full = lambda a, b: np.tile(np.concatenate([a, b], 1), (1, heads))
    return full(cos, cos), full(-sin, zero), full(zero, sin)


def row_of(small, at):
    return jnp.concatenate([small[at : at + 1, :], small[at + 1 : at + 2, :]], axis=1)


def token_weight(info, rows, small):
    counts = [small[6:7, c : c + 1] for c in range(NCLASS)]
    total = counts[0] + counts[1] + counts[2]
    return sum(info[rows, 1 + c : 2 + c] * (total / (NCLASS * counts[c])) for c in range(NCLASS))


def scale_of(field):
    return lax.rsqrt(jnp.mean(field * field, axis=-1, keepdims=True) + 1e-06)


def upper(rows):
    return rows // 2 // 16 * 16 + 16


def query_blocks(count, do):
    full = count // LANES

    def body(b, carry):
        do(b, pl.ds(pl.multiple_of(b * LANES, LANES), LANES), LANES)
        return carry

    lax.fori_loop(0, full, body, 0)
    if count % LANES:
        do(full, slice(full * LANES, count), count % LANES)


def combine(name, body, inputs, outs):
    return run(name, lambda *refs: body(refs[: len(inputs)], refs[len(inputs) :]), inputs, outs)


def stacked(name, *fields):
    def body(ins, outs):
        for n, ref in enumerate(ins):
            outs[0][n] = ref[...]

    return combine(name, body, fields, [shape((len(fields), *fields[0].shape), fields[0].dtype)])[0]


def cut_out(name, *wanted):
    def body(ins, outs):
        for ref, out, (_, first, end) in zip(ins, outs, wanted):
            out[...] = ref[first:end]

    outs = [shape((end - first, *f.shape[1:]), f.dtype) for f, first, end in wanted]
    return combine(name, body, [f for f, _, _ in wanted], outs)


def plus(*fields):
    return sum(f.astype(F32) for f in fields)


def put_relay(gx, gy, via_x, via_y, to_x, to_y, top):
    to_x[:top] = gx[:top]
    to_x[top:] = plus(gx[top:], via_y[...]).astype(BF)
    to_y[:top] = plus(gy[:top], via_x[...]).astype(BF)
    to_y[top:] = gy[top:]


def relay(name, gx, gy, via_x, via_y, top):
    body = lambda ins, outs: put_relay(*ins, *outs, top)
    return combine(name, body, [gx, gy, via_x, via_y], [shape(gx.shape, BF)] * 2)


def square_sums(name, own, from_x, from_y):
    def body(ins, outs):
        for k in range(4):
            outs[k][...] = plus(*(r[k] for r in ins)).astype(outs[k].dtype)

    block = own.shape[1:]
    return combine(name, body, [own, from_x, from_y], [shape(block, F32)] + [shape(block, BF)] * 3)


def line_sums(name, groups):
    sizes = [len(g) for g in groups]

    def body(ins, outs):
        at = 0
        for size, out in zip(sizes, outs):
            out[...] = plus(*(r[...] for r in ins[at : at + size]))
            at += size

    return combine(name, body, [f for g in groups for f in g], [shape(g[0].shape, F32) for g in groups])


def place(name, order, gathered, names, share, into=None):
    arrays = []
    for array, *_ in gathered:
        if not any(array is a for a in arrays):
            arrays.append(array)
    cols = arrays[0].shape[-1]
    into = list(into or ())

    def body(order, *refs):
        out = refs[len(arrays) + len(into) :]
        for array, index, line, square, start in gathered:
            ref = refs[[a is array for a in arrays].index(True)]
            chip = order[line * 4 + square] * share
            for n in range(names):
                low, high = max(start, n * share), min(start + array.shape[-2], (n + 1) * share)
                if low < high:
                    to = pl.ds(pl.multiple_of(chip + (low - n * share), 16), high - low)
                    rows = slice(low - start, high - start)
                    out[n][to, :] = ref[rows, :] if index is None else ref[index, rows, :]

    aliases = {1 + len(arrays) + n: n for n in range(len(into))}
    return run(
        name, body, [*arrays, *into], [shape((16 * share, cols), BF)] * names, order=order, aliases=aliases
    )


def project(tokens, tables, small, wq, wk, wv):
    count, width = tokens.shape
    cols = wq.shape[1]

    def body(tokens, cos, left_sin, right_sin, small, wq, wk, wv, normed, q_out, k_out, v_out):
        turn = cos[...], left_sin[...], right_sin[...]
        for rows in tiles(count):
            x = tokens[rows, :].astype(F32)
            low = (x * scale_of(x) * row_of(small, 0)).astype(BF)
            normed[rows, :] = low
            q_out[rows, :] = rope(dot(low, wq[...]), *turn).astype(BF)
            k_out[rows, :] = rope(dot(low, wk[...]), *turn).astype(BF)
            v_out[rows, :] = dot(low, wv[...]).astype(BF)

    return run(
        "project",
        body,
        [tokens, *tables, small, wq, wk, wv],
        [shape((count, width), BF)] + [shape((count, cols), BF)] * 3,
        flops=6 * count * width * cols,
    )


def attend(info, coderow, queries, keys, values, heads):
    count, cols = queries.shape

    def body(info, coderow, q, k, v, probs, mixture):
        def one_block(b, rows, size):
            key_at = lax.broadcasted_iota(jnp.int32, (size, size), 0)
            query_at = lax.broadcasted_iota(jnp.int32, (size, size), 1)
            same = info[rows, 0:1] == coderow[b][:, :size]
            allowed = (same & (key_at < query_at)) | (key_at == query_at)
            sums = [None] * (cols // LANES)
            for h in range(heads):
                here, lanes = columns(h), head_lanes(h)
                query = jnp.where(lanes, q[rows, here], jnp.zeros((), BF))
                scores = dot(k[rows, here], query, NT) * (1.0 / ROOT)
                scores = jnp.where(allowed, scores, -1e30)
                exponent = jnp.exp(scores - jnp.max(scores, axis=0, keepdims=True))
                soft = exponent * (1.0 / jnp.sum(exponent, axis=0, keepdims=True))
                probs[h, rows, 0:size] = soft
                value = jnp.where(lanes, v[rows, here], jnp.zeros((), BF))
                add_window(sums, h, dot(soft.astype(BF), value, TN))
            mixture[rows, :] = jnp.concatenate(sums, axis=1).astype(BF)

        query_blocks(count, one_block)

    return run(
        "attend",
        body,
        [info, coderow, queries, keys, values],
        [shape((heads, count, LANES), F32), shape((count, cols), BF)],
        flops=40 * count * LANES * cols,
    )


def attention_backward(q, k, v, probs, mixture_grad, tables, heads):
    count, cols = q.shape

    def body(q, k, v, probs, mg, cos, left_sin, right_sin, dq_out, dk_out, dv_out, dq, dk):
        zero = jnp.zeros((), BF)

        def back(b, rows, size):
            sums = [[None] * (cols // LANES) for _ in range(3)]
            for h in range(heads):
                here, lanes = columns(h), head_lanes(h)
                soft = probs[h, rows, 0:size]
                grad = jnp.where(lanes, mg[rows, here], zero)
                query = jnp.where(lanes, q[rows, here], zero)
                key = jnp.where(lanes, k[rows, here], zero)
                soft_grad = dot(v[rows, here], grad, NT)
                inner = jnp.sum(soft * soft_grad, axis=0, keepdims=True)
                score_grad = (soft * (soft_grad - inner)).astype(BF)
                add_window(sums[2], h, dot(soft.astype(BF), grad))
                add_window(sums[0], h, dot(score_grad, key, TN))
                add_window(sums[1], h, dot(score_grad, query))
            dv_out[rows, :] = jnp.concatenate(sums[2], axis=1).astype(BF)
            dq[rows, :] = jnp.concatenate(sums[0], axis=1)
            dk[rows, :] = jnp.concatenate(sums[1], axis=1)

        query_blocks(count, back)
        turn = cos[...], -left_sin[...], -right_sin[...]
        for grad, out in ((dq, dq_out), (dk, dk_out)):
            for rows in tiles(count):
                out[rows, :] = rope(grad[rows, :] * (1.0 / ROOT), *turn).astype(BF)

    return run(
        "attention_backward",
        body,
        [q, k, v, probs, mixture_grad, *tables],
        [shape((count, cols), BF)] * 3,
        [pltpu.VMEM((count, cols), F32)] * 2,
        flops=12 * count * LANES * cols,
    )


def project_back(name, fields, weights):
    count, cols = fields[0].shape
    width, n = weights[0].shape[0], len(fields)

    def body(*refs):
        out = refs[-1]
        for rows in tiles(count):
            total = dot(refs[0][rows, :], refs[n][...], NT)
            for f in range(1, n):
                total = total + dot(refs[f][rows, :], refs[n + f][...], NT)
            out[rows, :] = total.astype(BF)

    return run(
        name, body, [*fields, *weights], [shape((count, width), BF)], flops=2 * n * count * width * cols
    )[0]


def weigh_cotangent(cotangent, info, small):
    count, width = cotangent.shape

    def body(cot, info, small, low, total):
        parts = []
        for rows in tiles(count):
            low[rows, :] = (cot[rows, :].astype(F32) * token_weight(info, rows, small)).astype(BF)
            parts.append(jnp.sum(low[rows, :].astype(F32), axis=0, keepdims=True))
        total[...] = sum(parts)

    return run(
        "weigh_cotangent",
        body,
        [cotangent, info, small],
        [shape((count, width), BF), shape((1, width), F32)],
    )


def mlp_up(tokens, mine, other, small, up_bias, weight):
    count, width = tokens.shape
    cols = up_bias.shape[1]

    def body(tokens, mine, other, small, bias, w, hidden, normed, act, slope):
        for rows in tiles(count):
            field = tokens[rows, :].astype(F32) + (mine[rows, :].astype(F32) + other[rows, :].astype(F32))
            hidden[rows, :] = field
            low = (field * scale_of(field) * row_of(small, 2)).astype(BF)
            normed[rows, :] = low
            pre = dot(low, w[...]) + bias[...].astype(F32)
            sig = 1.0 / (1.0 + jnp.exp(-pre))
            act[rows, :] = (pre * sig).astype(BF)
            slope[rows, :] = sig * (1.0 + pre * (1.0 - sig))

    return run(
        "mlp_up",
        body,
        [tokens, mine, other, small, up_bias, weight],
        [shape((count, width), F32), shape((count, width), BF), shape((count, cols), BF), shape((count, cols), F32)],
        flops=2 * count * width * cols,
    )


def mlp_back(low, slope, down, up):
    count, width = low.shape
    cols = slope.shape[1]

    def body(low, slope, down, up, pre_grad, part, total):
        sums = []
        for rows in tiles(count):
            grad = (dot(low[rows, :], down[...]) * slope[rows, :]).astype(BF)
            pre_grad[rows, :] = grad
            sums.append(jnp.sum(grad.astype(F32), axis=0, keepdims=True))
            part[rows, :] = dot(grad, up[...], NT).astype(BF)
        total[...] = sum(sums)

    return run(
        "mlp_back",
        body,
        [low, slope, down, up],
        [shape((count, cols), BF), shape((count, width), BF), shape((1, cols), F32)],
        flops=4 * count * width * cols,
    )


def finish_output(hidden, mine, other, small):
    def body(hidden, mine, other, small, out):
        for rows in tiles(hidden.shape[0]):
            down = mine[rows, :].astype(F32) + other[rows, :].astype(F32)
            out[rows, :] = (hidden[rows, :] + (down + row_of(small, 4))).astype(BF)

    return run("finish_output", body, [hidden, mine, other, small], [shape(hidden.shape, BF)])[0]


def norm_back(field, scale, gain, grad):
    total = jnp.sum(grad * field * scale, axis=0, keepdims=True)
    scaled = grad * gain
    inner = jnp.mean(scaled * field, axis=-1, keepdims=True)
    return total, scale * scaled - field * (scale * scale * scale * inner)


def hidden_back(hidden, mine, other, cotangent, info, small, weight):
    count, width = hidden.shape
    cols = weight.shape[1]

    def body(hidden, mine, other, cot, info, small, w, grad_out, low, mg, total):
        parts = []
        for rows in tiles(count):
            field = hidden[rows, :]
            grad = mine[rows, :].astype(F32) + other[rows, :].astype(F32)
            part, through = norm_back(field, scale_of(field), row_of(small, 2), grad)
            parts.append(part)
            result = cot[rows, :].astype(F32) * token_weight(info, rows, small) + through
            grad_out[rows, :] = result
            low[rows, :] = result.astype(BF)
            mg[rows, :] = dot(result.astype(BF), w[...]).astype(BF)
        total[...] = sum(parts)

    return run(
        "hidden_back",
        body,
        [hidden, mine, other, cotangent, info, small, weight],
        [shape((count, width), F32), shape((count, width), BF), shape((count, cols), BF), shape((1, width), F32)],
        flops=2 * count * width * cols,
    )


def input_back(tokens, mine, other, hidden_grad, small):
    count, width = tokens.shape

    def body(tokens, mine, other, hidden_grad, small, out, total):
        parts = []
        for rows in tiles(count):
            field = tokens[rows, :].astype(F32)
            grad = mine[rows, :].astype(F32) + other[rows, :].astype(F32)
            part, through = norm_back(field, scale_of(field), row_of(small, 0), grad)
            parts.append(part)
            out[rows, :] = hidden_grad[rows, :] + through
        total[...] = sum(parts)

    return run(
        "input_back",
        body,
        [tokens, mine, other, hidden_grad, small],
        [shape((count, width), F32), shape((1, width), F32)],
    )


def weight_grads(name, order, left, rights, share, kind):
    count, width = left.shape
    cols = rights[0].shape[1]
    n = len(rights)
    rows = n * share
    if kind == "whole":
        outs = [shape((width, cols), BF)] * n
    elif kind == "square":
        outs = [shape((4, rows, cols), BF)] * 3 + [shape((2, rows, cols), BF)] * 2
    else:
        cut = upper(rows)
        outs = ([shape((rows, cols), BF)] * 3 + [shape((cut, cols), BF), shape((rows - cut, cols), BF)]) * 4

    def body(*refs):
        order, refs = (None, refs) if kind == "whole" else (refs[0], refs[1:])
        left, right, out = refs[0], refs[1 : n + 1], refs[n + 1 : n + 1 + len(outs)]
        whole = out if kind == "whole" else [refs[-1].at[r] for r in range(n)]
        for at in tiles(width, width // 2):
            for r in range(n):
                whole[r][at, :] = dot(left[:, at], right[r][...], TN).astype(BF)
        if kind == "whole":
            return
        for line in range(4):
            for square in range(4):
                chip = order[line * 4 + square]
                for r in range(n):
                    block = whole[r][pl.ds(pl.multiple_of(chip * share, 16), share), :]
                    to = slice(r * share, (r + 1) * share)
                    if kind == "line" and square < 3:
                        out[line * 5 + square][to, :] = block
                    elif kind == "line":
                        start, end = r * share, (r + 1) * share
                        mid = min(max(cut, start), end)
                        if start < mid:
                            out[line * 5 + 3][start:mid, :] = block[: mid - start]
                        if mid < end:
                            out[line * 5 + 4][mid - cut : end - cut, :] = block[mid - start :]
                    elif square < 3:
                        out[square][line, to, :] = block
                    else:
                        out[3 + line // 2][line % 2, to, :] = block

    return run(
        name,
        body,
        [left, *rights],
        outs,
        [] if kind == "whole" else [pltpu.VMEM((n, width, cols), BF)],
        flops=2 * n * count * width * cols,
        order=order,
    )


def local(
    tokens,
    cotangent,
    segment_ids,
    valid_mask,
    frequency,
    query_weight,
    key_weight,
    value_weight,
    output_weight,
    attn_gain,
    mlp_gain,
    up_weight,
    up_bias,
    down_weight,
    down_bias,
):
    dp = lax.axis_size("dp")
    me = lax.axis_index("dp")
    block_rows, patches = segment_ids.shape
    count, width = tokens.shape
    share, cols = query_weight.shape
    heads = cols // HD
    member = (frequency == jnp.arange(NCLASS, dtype=jnp.int32)[None, :]).astype(jnp.int32)
    row_valid = jnp.sum(valid_mask, axis=1)
    local_counts = jnp.sum(member * row_valid[:, None], axis=0)
    here = (jnp.arange(dp, dtype=jnp.int32) == me)[:, None]
    vectors = jnp.stack([attn_gain, mlp_gain, down_bias]).astype(F32)
    vectors = jnp.where(here[None], vectors[:, None, :], 0.0).reshape(6, cols)
    count_row = jnp.pad(local_counts.astype(F32)[None], ((0, 1), (0, cols - NCLASS)))
    small = jnp.concatenate([vectors, count_row])

    code = (jnp.arange(block_rows, dtype=jnp.int32)[:, None] * PATCHES + segment_ids).astype(F32)
    of_class = (valid_mask[:, :, None] * member[:, None, :]).astype(F32).reshape(count, NCLASS)
    key_code = jnp.where(valid_mask == 1, code, -1.0).reshape(count, 1)
    info = jnp.pad(jnp.concatenate([key_code, of_class], 1), ((0, 0), (0, 7 - NCLASS)))
    coderow = jnp.pad(code.reshape(1, count), ((0, 0), (0, -count % LANES))).reshape(-1, 1, LANES)

    weights = (query_weight, key_weight, value_weight, output_weight.T, up_weight, down_weight.T)
    layer = on_grid if gridded() else off_grid
    layer_out, input_grad, grads, sums = layer(
        tokens, cotangent, info, coderow, rope_tables(heads), small, weights, up_bias[None], heads
    )
    query_grad, key_grad, value_grad, output_grad, up_grad, down_grad = grads
    attn_gain_grad, mlp_gain_grad, down_bias_grad, up_bias_grad = sums
    return (
        layer_out,
        input_grad,
        query_grad,
        key_grad,
        value_grad,
        output_grad.T,
        attn_gain_grad.reshape(share),
        mlp_gain_grad.reshape(share),
        up_grad,
        up_bias_grad.reshape(cols),
        down_grad.T,
        down_bias_grad.reshape(share),
    )


def small_sums(*vectors):
    cols = vectors[-1].shape[1]

    def body(ins, outs):
        outs[0][...] = jnp.zeros_like(outs[0])
        at = 0
        for ref in ins:
            for start in range(0, ref.shape[1], cols):
                outs[0][at : at + 1, :] = ref[:, start : start + cols]
                at += 1

    return combine("small_sums", body, vectors, [shape((SMALL, cols), F32)])[0]


def own_parts(me, sums, share):
    cols = sums.shape[1]
    chips = 2 * cols // share

    def body(me, sums, *outs):
        for n in range(3):
            row = row_of(sums, 2 * n)
            part = jnp.zeros((1, share), F32)
            for c in range(chips):
                part = jnp.where(me[0] == c, row[:, c * share : (c + 1) * share], part)
            outs[n][...] = part
        outs[3][...] = sums[6:7, :]

    outs = [shape((1, share), F32)] * 3 + [shape((1, cols), F32)]
    return run("own_parts", body, [sums], outs, order=me.astype(jnp.int32).reshape(1))


def off_grid(tokens, cotangent, info, coderow, tables, small, weights, up_bias, heads):
    small = lax.psum(small, "dp")
    share = weights[0].shape[0]
    wq, wk, wv, wo, wu, wd = (lax.all_gather(w, "dp", axis=0, tiled=True) for w in weights)
    normed_one, queries, keys, values = project(tokens, tables, small, wq, wk, wv)
    probs, mixture = attend(info, coderow, queries, keys, values, heads)
    attn_part = project_back("attention_out", [mixture], [wo])
    attn_other = over_mp(attn_part)
    down_low, down_bias_sum = weigh_cotangent(cotangent, info, small)
    hidden, normed_two, activated, slope = mlp_up(tokens, attn_part, attn_other, small, up_bias, wu)
    pre_grad, normed_two_part, up_bias_sum = mlp_back(down_low, slope, wd, wu)
    normed_two_other = over_mp(normed_two_part)
    down_part = project_back("mlp_down", [activated], [wd])
    layer_out = finish_output(hidden, down_part, over_mp(down_part), small)
    hidden_grad, attn_low, mixture_grad, mlp_gain_sum = hidden_back(
        hidden, normed_two_part, normed_two_other, cotangent, info, small, wo
    )
    dq, dk, dv = attention_backward(queries, keys, values, probs, mixture_grad, tables, heads)
    normed_one_part = project_back("attention_in_back", [dq, dk, dv], [wq, wk, wv])
    input_grad, attn_gain_sum = input_back(
        tokens, normed_one_part, over_mp(normed_one_part), hidden_grad, small
    )
    locals_ = weight_grads("attention_grads", None, normed_one, [dq, dk, dv], share, "whole")
    for left, right in ((attn_low, mixture), (normed_two, pre_grad), (down_low, activated)):
        locals_ += weight_grads("weight_grads", None, left, [right], share, "whole")
    grads = [lax.psum_scatter(g.astype(F32), "dp", scatter_dimension=0, tiled=True) for g in locals_]
    sums = lax.psum(small_sums(attn_gain_sum, mlp_gain_sum, down_bias_sum, up_bias_sum), "dp")
    return layer_out, input_grad, grads, own_parts(lax.axis_index("dp"), sums, share)


def on_grid(tokens, cotangent, info, coderow, tables, small, weights, up_bias, heads):
    order, me = chip_order(), lax.axis_index("dp")
    share, cols = weights[0].shape
    first = stacked("stack_first", *weights[:3]).reshape(3 * share, cols)
    second = stacked("stack_second", *weights[3:]).reshape(3 * share, cols)
    cut = upper(3 * share)
    put = lambda name, pieces, into: place(name, order, pieces, 3, share, into)

    small_got = over_x(small)
    one, three = up_z(first, 1), up_z(first, 3)
    own_x, own_y = over_x(first), over_y(first)
    own_d = over_y(own_x)
    first, own_x, own_y, one, three, own_d, small, small_got, info, coderow, order, me, up_bias = together(
        first, own_x, own_y, one, three, own_d, small, small_got, info, coderow, order, me, up_bias
    )
    small = small + small_got
    two = up_z(first, 2)
    one_x, three_y, three_x, one_y = over_x(one), over_y(three), over_x(three), over_y(one)
    small_got = over_y(small)
    attn = put(
        "place_0",
        [(first, None, 0, 0, 0), (own_x, None, 0, 1, 0), (own_y, None, 0, 2, 0), (own_d, None, 0, 3, 0)]
        + [(one, None, 1, 0, 0), (three, None, 3, 0, 0)],
        None,
    )
    one_x, one_y, three_x, three_y, two, small, small_got, second, *attn = together(
        one_x, one_y, three_x, three_y, two, small, small_got, second, *attn
    )
    small = small + small_got
    one_d, three_d = over_y(one_x), over_x(three_y)
    two_x, two_y = over_x(two), over_y(two)
    small_got = lax.ppermute(small, "dp", pairs(lambda z, y, x: (z ^ 1, y, x)))
    second_one, second_three = up_z(second, 1), up_z(second, 3)
    attn = put(
        "place_1",
        [(one_x, None, 1, 1, 0), (one_y, None, 1, 2, 0), (three_x, None, 3, 1, 0), (three_y, None, 3, 2, 0)]
        + [(two, None, 2, 0, 0)],
        attn,
    )
    two_top, two_rest = cut_out("cut_two", (two_x, 0, cut), (two_y, cut, 3 * share))
    two_x, two_y, two_top, two_rest, one_d, three_d, small, small_got, second, second_one, second_three, *attn = together(
        two_x, two_y, two_top, two_rest, one_d, three_d, small, small_got, second, second_one, second_three, *attn
    )
    small = small + small_got
    two_a, two_b = over_y(two_top), over_x(two_rest)
    small_got = up_z(small, 2)
    second_two = up_z(second, 2)
    attn = put(
        "place_2",
        [(one_d, None, 1, 3, 0), (three_d, None, 3, 3, 0), (two_x, None, 2, 1, 0), (two_y, None, 2, 2, 0)],
        attn,
    )
    two_a, two_b, small, small_got, *attn = together(two_a, two_b, small, small_got, *attn)
    small = small + small_got
    wq, wk, wv = put("place_3", [(two_a, None, 2, 3, 0), (two_b, None, 2, 3, cut)], attn)
    normed_one, queries, keys, values = project(tokens, tables, small, wq, wk, wv)

    def by_weight(ins, outs):
        for k in range(4):
            outs[0][k] = ins[k][:share]
            outs[1][k] = ins[k][share:]

    output_lines, mlp_lines = combine(
        "stack_lines",
        by_weight,
        [second, second_one, second_two, second_three],
        [shape((4, share, cols), BF), shape((4, 2 * share, cols), BF)],
    )
    output_lines, mlp_lines, queries = together(output_lines, mlp_lines, queries)
    output_x, output_y = over_x(output_lines), over_y(output_lines)
    mlp_x, mlp_y = over_x(mlp_lines), over_y(mlp_lines)
    probs, mixture = attend(info, coderow, queries, keys, values, heads)
    down_low, down_bias_sum = weigh_cotangent(cotangent, info, small)
    output_x, output_y, mlp_x, mlp_y, mixture, down_low = together(
        output_x, output_y, mlp_x, mlp_y, mixture, down_low
    )
    output_a, output_b, mlp_a, mlp_b = cut_out(
        "cut_lines", (output_x, 0, 2), (output_y, 2, 4), (mlp_x, 0, 2), (mlp_y, 2, 4)
    )
    output_a, output_b = over_y(output_a), over_x(output_b)
    mlp_a, mlp_b = over_y(mlp_a), over_x(mlp_b)
    lines = lambda arrays: [(a, k, k, s, 0) for s, a in enumerate(arrays) for k in range(4)]
    diagonal = lambda a, b: [((a, b)[k // 2], k % 2, k, 3, 0) for k in range(4)]
    wo = place("place_output", order, lines((output_lines, output_x, output_y)), 1, share)
    mlp = place("place_mlp", order, lines((mlp_lines, mlp_x, mlp_y)), 2, share)
    (wo,) = place("place_output_end", order, diagonal(output_a, output_b), 1, share, wo)
    attn_part = project_back("attention_out", [mixture], [wo])
    attn_other = over_mp(attn_part)
    wu, wd = place("place_mlp_end", order, diagonal(mlp_a, mlp_b), 2, share, mlp)
    hidden, normed_two, activated, slope = mlp_up(tokens, attn_part, attn_other, small, up_bias, wu)

    grads_of = lambda name, left, right: weight_grads(name, order, left, right, share, "square")
    d_own, d_x, d_y, d_a, d_b = grads_of("down_grads", down_low, [activated])
    d_a, d_b = over_x(d_a), over_y(d_b)
    pre_grad, normed_two_part, up_bias_sum = mlp_back(down_low, slope, wd, wu)
    d_a, d_b, pre_grad, normed_two_part = together(d_a, d_b, pre_grad, normed_two_part)

    normed_two_other = over_mp(normed_two_part)
    d_x, d_y = relay("relay_down", d_x, d_y, d_a, d_b, 2)
    d_x, d_y = over_x(d_x), over_y(d_y)
    u_own, u_x, u_y, u_a, u_b = grads_of("up_grads", normed_two, [pre_grad])
    down_part = project_back("mlp_down", [activated], [wd])
    normed_two_other, d_x, d_y, u_a, u_b, down_part = together(normed_two_other, d_x, d_y, u_a, u_b, down_part)

    down_other = over_mp(down_part)
    u_a, u_b = over_x(u_a), over_y(u_b)
    down_sums = square_sums("sums_down", d_own, d_x, d_y)
    down_got = [to_line(down_sums[k], k) for k in (1, 2, 3)]
    hidden_grad, attn_low, mixture_grad, mlp_gain_sum = hidden_back(
        hidden, normed_two_part, normed_two_other, cotangent, info, small, wo
    )
    o_own, o_x, o_y, o_a, o_b = grads_of("output_grads", attn_low, [mixture])
    u_a, u_b, mixture_grad, o_a, o_b, down_other, *down_got = together(
        u_a, u_b, mixture_grad, o_a, o_b, down_other, *down_got
    )

    u_x, u_y = relay("relay_up", u_x, u_y, u_a, u_b, 2)
    u_x, u_y = over_x(u_x), over_y(u_y)
    o_a, o_b = over_x(o_a), over_y(o_b)
    dq, dk, dv = attention_backward(queries, keys, values, probs, mixture_grad, tables, heads)
    u_x, u_y, o_a, o_b, dq, dk, dv = together(u_x, u_y, o_a, o_b, dq, dk, dv)

    up_sums = square_sums("sums_up", u_own, u_x, u_y)
    up_got = [to_line(up_sums[k], k) for k in (1, 2, 3)]
    o_x, o_y = relay("relay_output", o_x, o_y, o_a, o_b, 2)
    o_x, o_y = over_x(o_x), over_y(o_y)
    pieces = weight_grads("attention_grads", order, normed_one, [dq, dk, dv], share, "line")
    normed_one_part = project_back("attention_in_back", [dq, dk, dv], [wq, wk, wv])
    o_x, o_y, normed_one_part, *rest_of = together(o_x, o_y, normed_one_part, *pieces, *up_got)
    pieces, up_got = rest_of[:20], rest_of[20:]

    normed_one_other = over_mp(normed_one_part)
    lines_of = [pieces[5 * k : 5 * k + 5] for k in range(4)]
    (g0, gx0, gy0, own_a, own_b), (g1, gx1, gy1, *gd1), (g2, gx2, gy2, two_a, two_b), (g3, gx3, gy3, *gd3) = lines_of
    two_a, two_b = over_x(two_a), over_y(two_b)
    own_a, own_b = over_x(own_a), over_y(own_b)
    output_sums = square_sums("sums_output", o_own, o_x, o_y)
    output_got = [to_line(output_sums[k], k) for k in (1, 2, 3)]
    two_a, two_b, own_a, own_b, normed_one_other, *others = together(
        two_a, two_b, own_a, own_b, normed_one_other, *gd1, *gd3
    )
    gd1, gd3 = others[:2], others[2:]

    gx2, gy2 = relay("relay_two", gx2, gy2, two_a, two_b, cut)
    gx2, gy2 = over_x(gx2), over_y(gy2)
    one_a, one_b, three_a, three_b = over_x(gd1[0]), over_y(gd1[1]), over_x(gd3[0]), over_y(gd3[1])
    input_grad, attn_gain_sum = input_back(tokens, normed_one_part, normed_one_other, hidden_grad, small)
    sums = small_sums(attn_gain_sum, mlp_gain_sum, down_bias_sum, up_bias_sum)
    gx2, gy2, one_a, one_b, three_a, three_b, sums, *output_got = together(
        gx2, gy2, one_a, one_b, three_a, three_b, sums, *output_got
    )

    def second_step(ins, outs):
        outs[0][...] = plus(*(r[...] for r in ins[:3])).astype(BF)
        put_relay(*ins[3:7], *outs[1:3], cut)
        put_relay(*ins[7:11], *outs[3:5], cut)

    like = shape(g2.shape, BF)
    two_sum, gx1, gy1, gx3, gy3 = combine(
        "sums_two", second_step, [g2, gx2, gy2, gx1, gy1, one_a, one_b, gx3, gy3, three_a, three_b], [like] * 5
    )
    two_got = to_line(two_sum, 2)
    gx1, gy1, gx3, gy3 = over_x(gx1), over_y(gy1), over_x(gx3), over_y(gy3)
    sums = small_over_square(sums)
    layer_out = finish_output(hidden, down_part, down_other, small)
    gx1, gy1, gx3, gy3, sums, layer_out, own_a, own_b = together(gx1, gy1, gx3, gy3, sums, layer_out, own_a, own_b)

    def third_step(ins, outs):
        outs[0][...] = plus(*(r[...] for r in ins[:3])).astype(BF)
        outs[1][...] = plus(*(r[...] for r in ins[3:6])).astype(BF)
        put_relay(*ins[6:10], *outs[2:4], cut)

    one_sum, three_sum, gx0, gy0 = combine(
        "sums_one_three", third_step, [g1, gx1, gy1, g3, gx3, gy3, gx0, gy0, own_a, own_b], [like] * 4
    )
    one_got, three_got = to_line(one_sum, 1), to_line(three_sum, 3)
    gx0, gy0 = over_x(gx0), over_y(gy0)
    sums = small_over_line(sums)
    output_grad, up_grad, down_grad = line_sums(
        "sums_mlp", [[own[0], *got] for own, got in ((output_sums, output_got), (up_sums, up_got), (down_sums, down_got))]
    )

    def last_step(ins, outs):
        for n in range(3):
            rows = slice(n * share, (n + 1) * share)
            outs[n][...] = plus(*(r[rows] for r in ins))

    grads = combine(
        "sums_attention", last_step, [g0, gx0, gy0, one_got, two_got, three_got], [shape((share, cols), F32)] * 3
    )
    sums = own_parts(me, sums, share)
    return layer_out, input_grad, [*grads, output_grad, up_grad, down_grad], sums


def solution(mesh):
    rows = P("dp", None)
    wide = P("dp", "mp")
    tall = P("mp", "dp")
    return jax.shard_map(
        local,
        mesh=mesh,
        in_specs=(rows,) * 5
        + (wide, wide, wide, tall, P("dp"), P("dp"), wide, P("mp"), tall, P("dp")),
        out_specs=(rows, rows, wide, wide, wide, tall, P("dp"), P("dp"), wide, P("mp"), tall, P("dp")),
        check_vma=False,
    )
```

```python
import math

import jax
import jax.numpy as jnp
import numpy as np
from jax import lax
from jax.experimental import pallas as pl
from jax.experimental.pallas import tpu as pltpu
from jax.sharding import PartitionSpec as P

HD = 80
NCLASS = 3
PATCHES = 16
TILE = 352
LANES = 128
BF = jnp.bfloat16
F32 = jnp.float32
ROOT = math.sqrt(HD)
ROOM = 6 * 1024 * 1024
SMALL = 8


def pairs(move):
    out = []
    for z in range(4):
        for y in range(2):
            for x in range(2):
                a, b, c = move(z, y, x)
                out.append(((z * 2 + y) * 2 + x, (a * 2 + b) * 2 + c))
    return out


def over_x(field):
    return lax.ppermute(field, "dp", pairs(lambda z, y, x: (z, y, 1 - x)))


def over_y(field):
    return lax.ppermute(field, "dp", pairs(lambda z, y, x: (z, 1 - y, x)))


def up_z(field, k):
    return lax.ppermute(field, "dp", pairs(lambda z, y, x: ((z + k) % 4, y, x)))


def over_mp(field):
    return lax.ppermute(field, "mp", [(0, 1), (1, 0)])


def gridded():
    return lax.axis_size("dp") == 16


def chip_order():
    me = lax.axis_index("dp")
    z, y, x = me // 4, (me // 2) % 2, me % 2
    k = jnp.arange(16, dtype=jnp.int32)
    line, square = k // 4, k % 4
    return ((z - line + 4) % 4) * 4 + (y ^ (square // 2)) * 2 + (x ^ (square % 2))


def together(*values):
    return lax.optimization_barrier(values)


def halves(rows):
    cut = (rows // 2 + 15) // 16 * 16
    return slice(0, cut), slice(cut, rows)


def to_line(field, k):
    return up_z(field, 4 - k)


COST = 1.0

NN = (((1,), (0,)), ((), ()))
NT = (((1,), (1,)), ((), ()))
TN = (((0,), (0,)), ((), ()))
shape = jax.ShapeDtypeStruct


def dot(a, b, dims=NN):
    return lax.dot_general(a, b, dims, preferred_element_type=F32)


def run(name, body, inputs, outs, scratch=(), flops=0, order=None, aliases=None):
    specs = [pl.BlockSpec(memory_space=pltpu.VMEM)] * len(inputs)
    if order is not None:
        inputs, specs = [order, *inputs], [pl.BlockSpec(memory_space=pltpu.SMEM), *specs]
    moved = sum(math.prod(a.shape) * a.dtype.itemsize for a in [*inputs, *outs])
    return pl.pallas_call(
        body,
        name=name,
        in_specs=specs,
        out_specs=[pl.BlockSpec(memory_space=pltpu.VMEM)] * len(outs),
        out_shape=outs,
        scratch_shapes=list(scratch),
        input_output_aliases=aliases or {},
        compiler_params=pltpu.CompilerParams(
            vmem_limit_bytes=ROOM + moved + sum(math.prod(f.shape) * f.dtype.itemsize for f in scratch)
        ),
        cost_estimate=pl.CostEstimate(flops=int(COST * flops), bytes_accessed=int(COST * moved), transcendentals=0),
    )(*inputs)


def tiles(count, size=TILE):
    return [slice(start, start + size) for start in range(0, count, size)]


def pair_columns(p):
    first = 2 * p * HD // LANES * LANES
    return slice(first, first + 2 * LANES)


def apart(p, field):
    lane = lax.broadcasted_iota(jnp.int32, (1, 2 * LANES), 1) + pair_columns(p).start
    zero = jnp.zeros((), field.dtype)
    heads = [jnp.where((lane >= h * HD) & (lane < h * HD + HD), field, zero) for h in (2 * p, 2 * p + 1)]
    return jnp.concatenate(heads, axis=0)


def add_pair(sums, p, part):
    first = pair_columns(p).start // LANES
    for c in range(2):
        piece = part[:, c * LANES : (c + 1) * LANES]
        sums[first + c] = piece if sums[first + c] is None else sums[first + c] + piece


def sideways(field, size):
    return jnp.concatenate([field[:, :size].T, field[:, size:].T], axis=1)


def rope(v, cos, left_sin, right_sin):
    rows, cols = v.shape
    left = pltpu.roll(v, cols - HD // 2, 1)
    right = pltpu.roll(v, HD // 2, 1)
    three = lambda f: f.reshape(rows // PATCHES, PATCHES, cols)
    out = three(v) * cos + three(left) * left_sin + three(right) * right_sin
    return out.reshape(rows, cols)


def rope_tables(heads):
    half = HD // 2
    i = np.arange(half, dtype=np.float32)
    rates = np.exp(np.float32(-math.log(10000.0)) * (np.float32(2.0) * i / np.float32(HD))).astype(np.float32)
    angle = np.arange(PATCHES, dtype=np.float32)[:, None] * rates[None, :]
    cos, sin = np.cos(angle).astype(np.float32), np.sin(angle).astype(np.float32)
    zero = np.zeros_like(sin)
    full = lambda a, b: np.tile(np.concatenate([a, b], 1), (1, heads))
    return full(cos, cos), full(-sin, zero), full(zero, sin)


def row_of(small, at):
    return jnp.concatenate([small[at : at + 1, :], small[at + 1 : at + 2, :]], axis=1)


def token_weight(info, rows, small):
    counts = [small[6:7, c : c + 1] for c in range(NCLASS)]
    total = counts[0] + counts[1] + counts[2]
    return sum(info[rows, 1 + c : 2 + c] * (total / (NCLASS * counts[c])) for c in range(NCLASS))


def scale_of(field):
    return lax.rsqrt(jnp.mean(field * field, axis=-1, keepdims=True) + 1e-06)


def upper(rows):
    return rows // 2 // 16 * 16 + 16


def query_blocks(count, do):
    full = count // LANES

    def body(b, carry):
        do(b, pl.ds(pl.multiple_of(b * LANES, LANES), LANES), LANES)
        return carry

    lax.fori_loop(0, full, body, 0)
    if count % LANES:
        do(full, slice(full * LANES, count), count % LANES)


def combine(name, body, inputs, outs):
    return run(name, lambda *refs: body(refs[: len(inputs)], refs[len(inputs) :]), inputs, outs)


def stacked(name, *fields):
    def body(ins, outs):
        for n, ref in enumerate(ins):
            outs[0][n] = ref[...]

    return combine(name, body, fields, [shape((len(fields), *fields[0].shape), fields[0].dtype)])[0]


def cut_out(name, *wanted):
    def body(ins, outs):
        for ref, out, (_, first, end) in zip(ins, outs, wanted):
            out[...] = ref[first:end]

    outs = [shape((end - first, *f.shape[1:]), f.dtype) for f, first, end in wanted]
    return combine(name, body, [f for f, _, _ in wanted], outs)


def two_terms(field):
    high = field.astype(BF).astype(F32)
    return jnp.concatenate([high, field - high], axis=0).astype(BF)


def one_term(pair):
    pair = pair.astype(F32)
    return pair[:SMALL] + pair[SMALL:]


def plus(*fields):
    return sum(f.astype(F32) for f in fields)


def put_relay(gx, gy, via_x, via_y, to_x, to_y, top):
    to_x[:top] = gx[:top]
    to_x[top:] = plus(gx[top:], via_y[...]).astype(BF)
    to_y[:top] = plus(gy[:top], via_x[...]).astype(BF)
    to_y[top:] = gy[top:]


def relay(name, gx, gy, via_x, via_y, top):
    body = lambda ins, outs: put_relay(*ins, *outs, top)
    return combine(name, body, [gx, gy, via_x, via_y], [shape(gx.shape, BF)] * 2)


def place(name, order, gathered, names, share, into=None):
    arrays = []
    for array, *_ in gathered:
        if not any(array is a for a in arrays):
            arrays.append(array)
    cols = arrays[0].shape[-1]
    into = list(into or ())

    def body(order, *refs):
        out = refs[len(arrays) + len(into) :]
        for array, index, line, square, start in gathered:
            ref = refs[[a is array for a in arrays].index(True)]
            chip = order[line * 4 + square] * share
            for n in range(names):
                low, high = max(start, n * share), min(start + array.shape[-2], (n + 1) * share)
                if low < high:
                    to = pl.ds(pl.multiple_of(chip + (low - n * share), 16), high - low)
                    rows = slice(low - start, high - start)
                    out[n][to, :] = ref[rows, :] if index is None else ref[index, rows, :]

    aliases = {1 + len(arrays) + n: n for n in range(len(into))}
    return run(
        name, body, [*arrays, *into], [shape((16 * share, cols), BF)] * names, order=order, aliases=aliases
    )


def project(tokens, tables, small, wq, wk, wv):
    count, width = tokens.shape
    cols = wq.shape[1]

    def body(tokens, cos, left_sin, right_sin, small, wq, wk, wv, normed, q_out, k_out, v_out):
        turn = cos[...], left_sin[...], right_sin[...]
        for rows in tiles(count):
            x = tokens[rows, :].astype(F32)
            low = (x * scale_of(x) * row_of(small, 0)).astype(BF)
            normed[rows, :] = low
            q_out[rows, :] = rope(dot(low, wq[...]), *turn).astype(BF)
            k_out[rows, :] = rope(dot(low, wk[...]), *turn).astype(BF)
            v_out[rows, :] = dot(low, wv[...]).astype(BF)

    return run(
        "project",
        body,
        [tokens, *tables, small, wq, wk, wv],
        [shape((count, width), BF)] + [shape((count, cols), BF)] * 3,
        flops=6 * count * width * cols,
    )


def attend(info, coderow, queries, keys, values, heads):
    count, cols = queries.shape

    def body(info, coderow, q, k, v, probs, mixture):
        def one_block(b, rows, size):
            key_at = lax.broadcasted_iota(jnp.int32, (size, 2 * size), 0)
            query_at = lax.broadcasted_iota(jnp.int32, (size, 2 * size), 1)
            query_at = jnp.where(query_at < size, query_at, query_at - size)
            code = coderow[b][:, :size]
            same = info[rows, 0:1] == jnp.concatenate([code, code], axis=1)
            allowed = (same & (key_at < query_at)) | (key_at == query_at)
            sums = [None] * (cols // LANES)
            for p in range(heads // 2):
                here = pair_columns(p)
                scores = dot(k[rows, here], apart(p, q[rows, here]), NT) * (1.0 / ROOT)
                scores = jnp.where(allowed, scores, -1e30)
                exponent = jnp.exp(scores - jnp.max(scores, axis=0, keepdims=True))
                soft = exponent * (1.0 / jnp.sum(exponent, axis=0, keepdims=True))
                probs[p, rows, 0 : 2 * size] = soft
                add_pair(sums, p, dot(sideways(soft.astype(BF), size), apart(p, v[rows, here])))
            mixture[rows, :] = jnp.concatenate(sums, axis=1).astype(BF)

        query_blocks(count, one_block)

    return run(
        "attend",
        body,
        [info, coderow, queries, keys, values],
        [shape((heads // 2, count, 2 * LANES), F32), shape((count, cols), BF)],
        flops=40 * count * LANES * cols,
    )


def attention_backward(q, k, v, probs, mixture_grad, tables, heads):
    count, cols = q.shape

    def body(q, k, v, probs, mg, cos, left_sin, right_sin, dq_out, dk_out, dv_out, dq, dk):
        def back(b, rows, size):
            sums = [[None] * (cols // LANES) for _ in range(3)]
            for p in range(heads // 2):
                here = pair_columns(p)
                soft = probs[p, rows, 0 : 2 * size]
                grad = apart(p, mg[rows, here])
                soft_grad = dot(v[rows, here], grad, NT)
                inner = jnp.sum(soft * soft_grad, axis=0, keepdims=True)
                score_grad = (soft * (soft_grad - inner)).astype(BF)
                add_pair(sums[2], p, dot(soft.astype(BF), grad))
                add_pair(sums[0], p, dot(sideways(score_grad, size), apart(p, k[rows, here])))
                add_pair(sums[1], p, dot(score_grad, apart(p, q[rows, here])))
            dv_out[rows, :] = jnp.concatenate(sums[2], axis=1).astype(BF)
            dq[rows, :] = jnp.concatenate(sums[0], axis=1)
            dk[rows, :] = jnp.concatenate(sums[1], axis=1)

        query_blocks(count, back)
        turn = cos[...], -left_sin[...], -right_sin[...]
        for grad, out in ((dq, dq_out), (dk, dk_out)):
            for rows in tiles(count):
                out[rows, :] = rope(grad[rows, :] * (1.0 / ROOT), *turn).astype(BF)

    return run(
        "attention_backward",
        body,
        [q, k, v, probs, mixture_grad, *tables],
        [shape((count, cols), BF)] * 3,
        [pltpu.VMEM((count, cols), F32)] * 2,
        flops=12 * count * LANES * cols,
    )


def project_back(name, fields, weights):
    count, cols = fields[0].shape
    width, n = weights[0].shape[0], len(fields)

    def body(*refs):
        out = refs[-1]
        for rows in tiles(count):
            total = dot(refs[0][rows, :], refs[n][...], NT)
            for f in range(1, n):
                total = total + dot(refs[f][rows, :], refs[n + f][...], NT)
            out[rows, :] = total.astype(BF)

    return run(
        name, body, [*fields, *weights], [shape((count, width), BF)], flops=2 * n * count * width * cols
    )[0]


def attention_in_back(fields, weights, tokens):
    count, cols = fields[0].shape
    width, n = weights[0].shape[0], len(fields)

    def body(*refs):
        tokens, out = refs[2 * n :]
        parts = []
        for rows in tiles(count):
            total = dot(refs[0][rows, :], refs[n][...], NT)
            for f in range(1, n):
                total = total + dot(refs[f][rows, :], refs[n + f][...], NT)
            out[rows, :] = total.astype(BF)
            field = tokens[rows, :].astype(F32)
            parts.append(jnp.sum(total * field * scale_of(field), axis=0, keepdims=True))
        gain = sum(parts)
        high = gain.astype(BF).astype(F32)
        row = lax.broadcasted_iota(jnp.int32, (2 * SMALL, width), 0)
        out[count:, :] = jnp.where(row == 0, high, jnp.where(row == 1, gain - high, 0.0)).astype(BF)

    return run(
        "attention_in_back",
        body,
        [*fields, *weights, tokens],
        [shape((count + 2 * SMALL, width), BF)],
        flops=2 * n * count * width * cols,
    )[0]


def weigh_cotangent(cotangent, info, small):
    count, width = cotangent.shape

    def body(cot, info, small, low, total):
        parts = []
        for rows in tiles(count):
            low[rows, :] = (cot[rows, :].astype(F32) * token_weight(info, rows, small)).astype(BF)
            parts.append(jnp.sum(low[rows, :].astype(F32), axis=0, keepdims=True))
        total[...] = sum(parts)

    return run(
        "weigh_cotangent",
        body,
        [cotangent, info, small],
        [shape((count, width), BF), shape((1, width), F32)],
    )


def mlp_up(tokens, mine, other, small, up_bias, weight):
    count, width = tokens.shape
    cols = up_bias.shape[1]

    def body(tokens, mine, other, small, bias, w, hidden, normed, act, slope):
        for rows in tiles(count):
            field = tokens[rows, :].astype(F32) + (mine[rows, :].astype(F32) + other[rows, :].astype(F32))
            hidden[rows, :] = field
            low = (field * scale_of(field) * row_of(small, 2)).astype(BF)
            normed[rows, :] = low
            pre = dot(low, w[...]) + bias[...].astype(F32)
            sig = 1.0 / (1.0 + jnp.exp(-pre))
            act[rows, :] = (pre * sig).astype(BF)
            slope[rows, :] = sig * (1.0 + pre * (1.0 - sig))

    return run(
        "mlp_up",
        body,
        [tokens, mine, other, small, up_bias, weight],
        [shape((count, width), F32), shape((count, width), BF), shape((count, cols), BF), shape((count, cols), F32)],
        flops=2 * count * width * cols,
    )


def mlp_back(low, slope, down, up):
    count, width = low.shape
    cols = slope.shape[1]

    def body(low, slope, down, up, pre_grad, part, total):
        sums = []
        for rows in tiles(count):
            grad = (dot(low[rows, :], down[...]) * slope[rows, :]).astype(BF)
            pre_grad[rows, :] = grad
            sums.append(jnp.sum(grad.astype(F32), axis=0, keepdims=True))
            part[rows, :] = dot(grad, up[...], NT).astype(BF)
        total[...] = sum(sums)

    return run(
        "mlp_back",
        body,
        [low, slope, down, up],
        [shape((count, cols), BF), shape((count, width), BF), shape((1, cols), F32)],
        flops=4 * count * width * cols,
    )


def finish_output(hidden, mine, other, small):
    def body(hidden, mine, other, small, out):
        for rows in tiles(hidden.shape[0]):
            down = mine[rows, :].astype(F32) + other[rows, :].astype(F32)
            out[rows, :] = (hidden[rows, :] + (down + row_of(small, 4))).astype(BF)

    return run("finish_output", body, [hidden, mine, other, small], [shape(hidden.shape, BF)])[0]


def norm_back(field, scale, gain, grad):
    scaled = grad * gain
    inner = jnp.mean(scaled * field, axis=-1, keepdims=True)
    return scale * scaled - field * (scale * scale * scale * inner)


def hidden_back(hidden, mine, other, cotangent, info, small, weight):
    count, width = hidden.shape
    cols = weight.shape[1]

    def body(hidden, mine, other, cot, info, small, w, grad_out, low, mg, total):
        parts = []
        for rows in tiles(count):
            field = hidden[rows, :]
            grad = mine[rows, :].astype(F32) + other[rows, :].astype(F32)
            scale = scale_of(field)
            parts.append(jnp.sum(grad * field * scale, axis=0, keepdims=True))
            through = norm_back(field, scale, row_of(small, 2), grad)
            result = cot[rows, :].astype(F32) * token_weight(info, rows, small) + through
            grad_out[rows, :] = result
            low[rows, :] = result.astype(BF)
            mg[rows, :] = dot(result.astype(BF), w[...]).astype(BF)
        total[...] = sum(parts)

    return run(
        "hidden_back",
        body,
        [hidden, mine, other, cotangent, info, small, weight],
        [shape((count, width), F32), shape((count, width), BF), shape((count, cols), BF), shape((1, width), F32)],
        flops=2 * count * width * cols,
    )


def input_back(tokens, mine, other, hidden_grad, small):
    count, width = tokens.shape

    def body(tokens, mine, other, hidden_grad, small, out):
        for rows in tiles(count):
            field = tokens[rows, :].astype(F32)
            grad = mine[rows, :].astype(F32) + other[rows, :].astype(F32)
            out[rows, :] = hidden_grad[rows, :] + norm_back(field, scale_of(field), row_of(small, 0), grad)

    return run(
        "input_back", body, [tokens, mine, other, hidden_grad, small], [shape((count, width), F32)]
    )[0]


def weight_grads(name, order, left, rights, share, kind):
    count, width = left.shape
    cols = rights[0].shape[1]
    n = len(rights)
    rows = n * share
    if kind == "whole":
        outs = [shape((width, cols), BF)] * n
    elif kind == "ring":
        outs = [shape((4, rows, cols), BF)] * 4
    elif kind == "square":
        outs = [shape((4, rows, cols), BF)] * 3 + [shape((2, rows, cols), BF)] * 2
    else:
        cut = upper(rows)
        outs = [shape((rows, cols), BF)] * 12
        outs += [shape((2 * cut, cols), BF), shape((2 * (rows - cut), cols), BF)] * 2

    def body(*refs):
        order, refs = (None, refs) if kind == "whole" else (refs[0], refs[1:])
        left, right, out = refs[0], refs[1 : n + 1], refs[n + 1 : n + 1 + len(outs)]
        whole = out if kind == "whole" else [refs[-1].at[r] for r in range(n)]
        for at in tiles(width, width // 2):
            for r in range(n):
                whole[r][at, :] = dot(left[:, at], right[r][...], TN).astype(BF)
        if kind == "whole":
            return
        for line in range(4):
            for square in range(4):
                chip = order[line * 4 + square]
                for r in range(n):
                    block = whole[r][pl.ds(pl.multiple_of(chip * share, 16), share), :]
                    to = slice(r * share, (r + 1) * share)
                    if kind == "ring":
                        out[line][square, to, :] = block
                    elif kind == "line" and square < 3:
                        out[line * 3 + square][to, :] = block
                    elif kind == "line":
                        top, rest = out[12:14] if line % 2 == 0 else out[14:16]
                        second = line in (0, 3)
                        start, end = r * share, (r + 1) * share
                        mid = min(max(cut, start), end)
                        if start < mid:
                            at = cut * second
                            top[at + start : at + mid, :] = block[: mid - start]
                        if mid < end:
                            at = (rows - cut) * second - cut
                            rest[at + mid : at + end, :] = block[mid - start :]
                    elif square < 3:
                        out[square][line, to, :] = block
                    else:
                        out[3 + line // 2][line % 2, to, :] = block

    return run(
        name,
        body,
        [left, *rights],
        outs,
        [] if kind == "whole" else [pltpu.VMEM((n, width, cols), BF)],
        flops=2 * n * count * width * cols,
        order=order,
    )


def local(
    tokens,
    cotangent,
    segment_ids,
    valid_mask,
    frequency,
    query_weight,
    key_weight,
    value_weight,
    output_weight,
    attn_gain,
    mlp_gain,
    up_weight,
    up_bias,
    down_weight,
    down_bias,
):
    dp = lax.axis_size("dp")
    me = lax.axis_index("dp")
    block_rows, patches = segment_ids.shape
    count, width = tokens.shape
    share, cols = query_weight.shape
    heads = cols // HD
    member = (frequency == jnp.arange(NCLASS, dtype=jnp.int32)[None, :]).astype(jnp.int32)
    row_valid = jnp.sum(valid_mask, axis=1)
    local_counts = jnp.sum(member * row_valid[:, None], axis=0)
    here = (jnp.arange(dp, dtype=jnp.int32) == me)[:, None]
    vectors = jnp.stack([attn_gain, mlp_gain, down_bias]).astype(F32)
    vectors = jnp.where(here[None], vectors[:, None, :], 0.0).reshape(6, cols)
    count_row = jnp.pad(local_counts.astype(F32)[None], ((0, 1), (0, cols - NCLASS)))
    small = jnp.concatenate([vectors, count_row])

    code = (jnp.arange(block_rows, dtype=jnp.int32)[:, None] * PATCHES + segment_ids).astype(F32)
    of_class = (valid_mask[:, :, None] * member[:, None, :]).astype(F32).reshape(count, NCLASS)
    key_code = jnp.where(valid_mask == 1, code, -1.0).reshape(count, 1)
    info = jnp.pad(jnp.concatenate([key_code, of_class], 1), ((0, 0), (0, 7 - NCLASS)))
    coderow = jnp.pad(code.reshape(1, count), ((0, 0), (0, -count % LANES))).reshape(-1, 1, LANES)

    weights = (query_weight, key_weight, value_weight, output_weight.T, up_weight, down_weight.T)
    layer = on_grid if gridded() else off_grid
    layer_out, input_grad, grads, sums = layer(
        tokens, cotangent, info, coderow, rope_tables(heads), small, weights, up_bias[None], heads
    )
    query_grad, key_grad, value_grad, output_grad, up_grad, down_grad = grads
    attn_gain_grad, mlp_gain_grad, down_bias_grad, up_bias_grad = sums
    return (
        layer_out,
        input_grad,
        query_grad,
        key_grad,
        value_grad,
        output_grad.T,
        attn_gain_grad.reshape(share),
        mlp_gain_grad.reshape(share),
        up_grad,
        up_bias_grad.reshape(cols),
        down_grad.T,
        down_bias_grad.reshape(share),
    )


def small_sums(mine, other, *vectors):
    cols = vectors[-1].shape[1]
    count = mine.shape[0] - 2 * SMALL

    def body(ins, outs):
        outs[0][...] = jnp.zeros_like(outs[0])
        ends = plus(ins[0][count:, :], ins[1][count:, :])
        row = 0
        for total in [ends[0:1] + ends[1:2]] + [r[...] for r in ins[2:]]:
            for start in range(0, total.shape[1], cols):
                outs[0][row : row + 1, :] = total[:, start : start + cols]
                row += 1

    return combine("small_sums", body, [mine, other, *vectors], [shape((SMALL, cols), F32)])[0]


def own_parts(me, sums, share):
    cols = sums.shape[1]
    chips = 2 * cols // share

    def body(me, sums, *outs):
        for n in range(3):
            row = row_of(sums, 2 * n)
            part = jnp.zeros((1, share), F32)
            for c in range(chips):
                part = jnp.where(me[0] == c, row[:, c * share : (c + 1) * share], part)
            outs[n][...] = part
        outs[3][...] = sums[6:7, :]

    outs = [shape((1, share), F32)] * 3 + [shape((1, cols), F32)]
    return run("own_parts", body, [sums], outs, order=me.astype(jnp.int32).reshape(1))


def off_grid(tokens, cotangent, info, coderow, tables, small, weights, up_bias, heads):
    small = lax.psum(small, "dp")
    share = weights[0].shape[0]
    wq, wk, wv, wo, wu, wd = (lax.all_gather(w, "dp", axis=0, tiled=True) for w in weights)
    normed_one, queries, keys, values = project(tokens, tables, small, wq, wk, wv)
    probs, mixture = attend(info, coderow, queries, keys, values, heads)
    attn_part = project_back("attention_out", [mixture], [wo])
    attn_other = over_mp(attn_part)
    down_low, down_bias_sum = weigh_cotangent(cotangent, info, small)
    hidden, normed_two, activated, slope = mlp_up(tokens, attn_part, attn_other, small, up_bias, wu)
    pre_grad, normed_two_part, up_bias_sum = mlp_back(down_low, slope, wd, wu)
    normed_two_other = over_mp(normed_two_part)
    down_part = project_back("mlp_down", [activated], [wd])
    layer_out = finish_output(hidden, down_part, over_mp(down_part), small)
    hidden_grad, attn_low, mixture_grad, mlp_gain_sum = hidden_back(
        hidden, normed_two_part, normed_two_other, cotangent, info, small, wo
    )
    dq, dk, dv = attention_backward(queries, keys, values, probs, mixture_grad, tables, heads)
    normed_one_part = attention_in_back([dq, dk, dv], [wq, wk, wv], tokens)
    normed_one_other = over_mp(normed_one_part)
    input_grad = input_back(tokens, normed_one_part, normed_one_other, hidden_grad, small)
    locals_ = weight_grads("attention_grads", None, normed_one, [dq, dk, dv], share, "whole")
    for left, right in ((attn_low, mixture), (normed_two, pre_grad), (down_low, activated)):
        locals_ += weight_grads("weight_grads", None, left, [right], share, "whole")
    grads = [lax.psum_scatter(g.astype(F32), "dp", scatter_dimension=0, tiled=True) for g in locals_]
    sums = small_sums(normed_one_part, normed_one_other, mlp_gain_sum, down_bias_sum, up_bias_sum)
    sums = own_parts(lax.axis_index("dp"), lax.psum(sums, "dp"), share)
    return layer_out, input_grad, grads, sums


def from_hbm(name, groups):
    flat = [f for g in groups for f in g]
    outs = [shape((sum(f.shape[0] for f in g), g[0].shape[1]), g[0].dtype) for g in groups]

    def body(*refs):
        ins, out, sem = refs[: len(flat)], refs[len(flat) : -1], refs[-1]
        copies, at = [], 0
        for g, group in enumerate(groups):
            row = 0
            for field in group:
                copies.append(pltpu.make_async_copy(ins[at], out[g].at[pl.ds(row, field.shape[0])], sem.at[at]))
                row, at = row + field.shape[0], at + 1
        for copy in copies:
            copy.start()
        for copy in copies:
            copy.wait()

    moved = sum(math.prod(o.shape) * o.dtype.itemsize for o in outs)
    return pl.pallas_call(
        body,
        name=name,
        in_specs=[pl.BlockSpec(memory_space=pl.ANY)] * len(flat),
        out_specs=[pl.BlockSpec(memory_space=pltpu.VMEM)] * len(outs),
        out_shape=outs,
        scratch_shapes=[pltpu.SemaphoreType.DMA((len(flat),))],
        compiler_params=pltpu.CompilerParams(vmem_limit_bytes=ROOM + moved),
        cost_estimate=pl.CostEstimate(flops=0, bytes_accessed=2 * moved, transcendentals=0),
    )(*flat)


def on_grid(tokens, cotangent, info, coderow, tables, small, weights, up_bias, heads):
    order, me = chip_order(), lax.axis_index("dp")
    share, cols = weights[0].shape
    rows = 3 * share
    q, k, v, o, u, d = weights
    first, four = from_hbm("stack_first", [(q, k, v), (q, k, v, d)])
    cut, low, mid = upper(rows), rows - upper(rows), 2 * share
    block = shape((share, cols), BF)
    fourfold = shape((4, share, cols), BF)
    put = lambda name, pieces, into: place(name, order, pieces, 3, share, into)
    put_one = lambda name, pieces, into=None: place(name, order, pieces, 1, share, into)

    one, three = up_z(first, 1), up_z(first, 3)
    own_x, own_y = over_x(four), over_y(four)
    small_got = lax.ppermute(small, "dp", pairs(lambda z, y, x: (z ^ 1, y, x)))

    def cut_own(ins, outs):
        outs[0][...] = ins[0][:mid]
        outs[1][...] = ins[1][mid:]

    own_a, own_b = combine("cut_own", cut_own, [own_x, own_y], [shape((mid, cols), BF)] * 2)
    own_a, own_b = over_y(own_a), over_x(own_b)
    four, own_x, own_y, one, three, own_a, own_b, small, small_got, info, coderow, order, me, up_bias, o, u = together(
        four, own_x, own_y, one, three, own_a, own_b, small, small_got, info, coderow, order, me, up_bias, o, u
    )
    small = small + small_got
    two = up_z(first, 2)
    both = stacked("stack_one_three", one, three)
    both_x, both_y = over_x(both), over_y(both)
    small_got = up_z(small, 2)

    def stack_down(ins, outs):
        four, own_x, own_y, own_b = ins
        outs[0][0] = four[rows:]
        outs[0][1] = own_x[rows:]
        outs[0][2] = own_y[rows:]
        outs[0][3] = own_b[rows - mid :]

    (down_0,) = combine("stack_down", stack_down, [four, own_x, own_y, own_b], [fourfold])
    (mlp_0,) = from_hbm("stack_mlp", [(o, u)])
    attn = put(
        "place_0",
        [(four, None, 0, 0, 0), (own_x, None, 0, 1, 0), (own_y, None, 0, 2, 0), (own_a, None, 0, 3, 0)]
        + [(own_b, None, 0, 3, mid), (one, None, 1, 0, 0), (three, None, 3, 0, 0)],
        None,
    )
    both_x, both_y, two, small, small_got, mlp_0, down_0, *attn = together(
        both_x, both_y, two, small, small_got, mlp_0, down_0, *attn
    )
    small = small + small_got

    def next_step(ins, outs):
        outs[0][0] = ins[0][...]
        outs[0][1] = ins[2][1]
        outs[1][0] = ins[0][...]
        outs[1][1] = ins[1][0]

    by_x, by_y = combine("stack_two", next_step, [two, both_x, both_y], [shape(both.shape, BF)] * 2)
    mlp_1, down_1 = up_z(mlp_0, 1), up_z(down_0, 1)
    by_x, by_y = over_x(by_x), over_y(by_y)
    small_got = over_x(small)
    attn = put(
        "place_1",
        [(both_x, 0, 1, 1, 0), (both_y, 0, 1, 2, 0), (both_x, 1, 3, 1, 0), (both_y, 1, 3, 2, 0), (two, None, 2, 0, 0)],
        attn,
    )
    by_x, by_y, small, small_got, mlp_0, mlp_1, down_0, down_1, *attn = together(
        by_x, by_y, small, small_got, mlp_0, mlp_1, down_0, down_1, *attn
    )

    def halves(ins, outs):
        outs[0][...] = ins[0][0, :cut]
        outs[1][...] = ins[1][0, cut:]

    two_a, two_b = combine("cut_two", halves, [by_x, by_y], [shape((cut, cols), BF), shape((low, cols), BF)])
    small = small + small_got
    two_a, two_b = over_y(two_a), over_x(two_b)
    small_got = over_y(small)
    mlp_2 = up_z(mlp_1, 1)
    attn = put(
        "place_2",
        [(by_y, 1, 1, 3, 0), (by_x, 1, 3, 3, 0), (by_x, 0, 2, 1, 0), (by_y, 0, 2, 2, 0)],
        attn,
    )
    two_a, two_b, small, small_got, mlp_2, down_1, *attn = together(
        two_a, two_b, small, small_got, mlp_2, down_1, *attn
    )
    small = small + small_got
    mlp_3, down_2 = up_z(mlp_2, 1), up_z(down_1, 1)
    wq, wk, wv = put("place_3", [(two_a, None, 2, 3, 0), (two_b, None, 2, 3, cut)], attn)
    normed_one, queries, keys, values = project(tokens, tables, small, wq, wk, wv)
    mlp_3, queries = together(mlp_3, queries)

    def by_weight(ins, outs):
        for n in range(2):
            for k in range(4):
                outs[n][k] = ins[k][n * share : (n + 1) * share]

    wo_own, wu_own = combine("stack_lines", by_weight, [mlp_0, mlp_1, mlp_2, mlp_3], [fourfold] * 2)
    lines = lambda *arrays: [(a, k, k, s, 0) for s, a in enumerate(arrays) for k in range(4)]
    diagonal = lambda a, b: [((a, b)[k // 2], k % 2, k, 3, 0) for k in range(4)]
    wo_x, wo_y = over_x(wo_own), over_y(wo_own)
    probs, mixture = attend(info, coderow, queries, keys, values, heads)
    wo_x, wo_y, mixture, wo_own, wu_own, down_0, down_1, down_2 = together(
        wo_x, wo_y, mixture, wo_own, wu_own, down_0, down_1, down_2
    )

    wo_a, wo_b = cut_out("cut_output", (wo_x, 0, 2), (wo_y, 2, 4))
    wo_a, wo_b = over_y(wo_a), over_x(wo_b)
    wu_x, wu_y = over_x(wu_own), over_y(wu_own)
    down_3 = up_z(down_2, 1)
    wo = put_one("place_output", lines(wo_own, wo_x, wo_y))
    down_low, down_bias_sum = weigh_cotangent(cotangent, info, small)
    (wo,) = put_one("place_output_end", diagonal(wo_a, wo_b), wo)
    attn_part = project_back("attention_out", [mixture], [wo])
    wu_x, wu_y, attn_part, down_low, down_3 = together(wu_x, wu_y, attn_part, down_low, down_3)

    attn_other = over_mp(attn_part)
    wu_a, wu_b = cut_out("cut_up", (wu_x, 0, 2), (wu_y, 2, 4))
    wu_a, wu_b = over_y(wu_a), over_x(wu_b)
    wu = put_one("place_up", lines(wu_own, wu_x, wu_y))
    (wd,) = put_one(
        "place_down", [(a, s, k, s, 0) for k, a in enumerate((down_0, down_1, down_2, down_3)) for s in range(4)]
    )
    attn_other, wu_a, wu_b, wd, *wu = together(attn_other, wu_a, wu_b, wd, *wu)
    (wu,) = put_one("place_up_end", diagonal(wu_a, wu_b), wu)
    hidden, normed_two, activated, slope = mlp_up(tokens, attn_part, attn_other, small, up_bias, wu)

    grads_of = lambda name, left, right, kind: weight_grads(name, order, left, right, share, kind)
    d_0, d_1, d_2, d_3 = grads_of("down_grads", down_low, [activated], "ring")
    d_1, d_2, activated, down_low = together(d_1, d_2, activated, down_low)
    d_got = up_z(d_1, 1)
    pre_grad, normed_two_part, up_bias_sum = mlp_back(down_low, slope, wd, wu)
    normed_two_other = over_mp(normed_two_part)
    u_own, u_x, u_y, u_a, u_b = grads_of("up_grads", normed_two, [pre_grad], "square")
    u_a, u_b = over_x(u_a), over_y(u_b)
    down_part = project_back("mlp_down", [activated], [wd])
    hidden_grad, attn_low, mixture_grad, mlp_gain_sum = hidden_back(
        hidden, normed_two_part, normed_two_other, cotangent, info, small, wo
    )
    u_a, u_b, down_part, mixture_grad, attn_low, d_got = together(u_a, u_b, down_part, mixture_grad, attn_low, d_got)

    def ring_step(name, mine, got):
        def body(ins, outs):
            for s in range(4):
                outs[0][s] = plus(ins[0][s], ins[1][s]).astype(BF)

        return up_z(combine(name, body, [mine, got], [fourfold])[0], 1)

    d_got = ring_step("ring_two", d_2, d_got)
    u_x, u_y = relay("relay_up", u_x, u_y, u_a, u_b, 2)
    u_x, u_y = over_x(u_x), over_y(u_y)
    o_own, o_x, o_y, o_a, o_b = grads_of("output_grads", attn_low, [mixture], "square")
    o_a, o_b = over_x(o_a), over_y(o_b)
    dq, dk, dv = attention_backward(queries, keys, values, probs, mixture_grad, tables, heads)
    u_x, u_y, o_a, o_b, dq, dk, dv, down_part, d_got = together(u_x, u_y, o_a, o_b, dq, dk, dv, down_part, d_got)

    d_got = ring_step("ring_three", d_3, d_got)
    down_other = over_mp(down_part)
    o_x, o_y = relay("relay_output", o_x, o_y, o_a, o_b, 2)
    o_x, o_y = over_x(o_x), over_y(o_y)
    pieces = weight_grads("attention_grads", order, normed_one, [dq, dk, dv], share, "line")
    normed_one_part = attention_in_back([dq, dk, dv], [wq, wk, wv], tokens)
    o_x, o_y, normed_one_part, d_got, down_other, *pieces = together(
        o_x, o_y, normed_one_part, d_got, down_other, *pieces
    )

    g0, gx0, gy0, g1, gx1, gy1, g2, gx2, gy2, g3, gx3, gy3, even_x, even_y, odd_x, odd_y = pieces
    like = shape((rows, cols), BF)
    d_cut = upper(share)

    def pack_even(ins, outs):
        even_x, even_y, d_0, d_got = ins
        outs[0][: 2 * cut] = even_x[...]
        outs[1][: 2 * low] = even_y[...]
        diagonal = plus(d_0[3], d_got[3]).astype(BF)
        outs[0][2 * cut :] = diagonal[:d_cut]
        outs[1][2 * low :] = diagonal[d_cut:]
        for s in range(3):
            outs[2 + s][...] = plus(d_0[s], d_got[s]).astype(BF)

    even_x, even_y, d_own, d_x, d_y = combine(
        "pack_even",
        pack_even,
        [even_x, even_y, d_0, d_got],
        [shape((2 * cut + d_cut, cols), BF), shape((2 * low + share - d_cut, cols), BF)] + [block] * 3,
    )
    even_x, even_y = over_x(even_x), over_y(even_y)

    def square_sums(ins, outs):
        for n in range(2):
            at = slice(n * share, (n + 1) * share)
            for k in range(4):
                outs[k][at] = plus(*(r[k] for r in ins[3 * n : 3 * n + 3])).astype(outs[k].dtype)

    mlp_sums = combine(
        "sums_square",
        square_sums,
        [o_own, o_x, o_y, u_own, u_x, u_y],
        [shape((2 * share, cols), F32)] + [shape((2 * share, cols), BF)] * 3,
    )
    mlp_got = [to_line(mlp_sums[k], k) for k in (1, 3)]
    normed_one_other = over_mp(normed_one_part)
    even_x, even_y, normed_one_other, mlp_two, *mlp_got = together(
        even_x, even_y, normed_one_other, mlp_sums[2], *mlp_got
    )

    sums = small_sums(normed_one_part, normed_one_other, mlp_gain_sum, down_bias_sum, up_bias_sum)
    x_rows, y_rows = rows + 2 * cut, rows + 2 * low

    def first_step(ins, outs):
        gx2, gy2, even_x, even_y, odd_x, odd_y, d_x, d_y, sums = ins
        put_relay(gx2, gy2, even_x.at[:cut], even_y.at[:low], outs[0].at[:rows], outs[1].at[:rows], cut)
        outs[0][rows:x_rows] = odd_x[...]
        outs[1][rows:y_rows] = odd_y[...]
        put_relay(
            d_x,
            d_y,
            even_x.at[2 * cut :],
            even_y.at[2 * low :],
            outs[0].at[x_rows : x_rows + share],
            outs[1].at[y_rows:],
            d_cut,
        )
        outs[0][x_rows + share :] = two_terms(sums[...])

    by_x, by_y = combine(
        "relay_two",
        first_step,
        [gx2, gy2, even_x, even_y, odd_x, odd_y, d_x, d_y, sums],
        [shape((x_rows + share + 2 * SMALL, cols), BF), shape((y_rows + share, cols), BF)],
    )
    by_x, by_y = over_x(by_x), over_y(by_y)
    mlp_two = to_line(mlp_two, 2)
    input_grad = input_back(tokens, normed_one_part, normed_one_other, hidden_grad, small)
    by_x, by_y, mlp_two, input_grad = together(by_x, by_y, mlp_two, input_grad)

    wider = shape((rows + 2 * SMALL, cols), BF)

    def second_step(ins, outs):
        g2, by_x, by_y, gx1, gy1, gx3, gy3, d_own, sums = ins
        two, to_x, to_y, d_grad, new_sums = outs
        two[:rows] = plus(g2[...], by_x[:rows], by_y[:rows]).astype(BF)
        for n, (gx, gy) in enumerate(((gx1, gy1), (gx3, gy3))):
            via_x = by_x.at[rows + n * cut : rows + (n + 1) * cut]
            via_y = by_y.at[rows + n * low : rows + (n + 1) * low]
            at = slice(n * rows, (n + 1) * rows)
            put_relay(gx, gy, via_x, via_y, to_x.at[at], to_y.at[at], cut)
        d_grad[...] = plus(d_own[...], by_x[x_rows : x_rows + share], by_y[y_rows:])
        total = sums[...] + one_term(by_x[x_rows + share :])
        new_sums[...] = total
        two[rows:] = two_terms(total)
        to_y[2 * rows :] = two_terms(total)

    two_sum, by_x, by_y, down_grad, sums = combine(
        "sums_two",
        second_step,
        [g2, by_x, by_y, gx1, gy1, gx3, gy3, d_own, sums],
        [wider, shape((2 * rows, cols), BF), shape((2 * rows + 2 * SMALL, cols), BF)]
        + [shape((share, cols), F32), shape((SMALL, cols), F32)],
    )
    two_got = to_line(two_sum, 2)
    by_x, by_y = over_x(by_x), over_y(by_y)
    layer_out = finish_output(hidden, down_part, down_other, small)
    by_x, by_y, layer_out, two_got = together(by_x, by_y, layer_out, two_got)

    def third_step(ins, outs):
        g1, g3, by_x, by_y, gx0, gy0, even_x, even_y, two_got, sums = ins
        one, three, to_x, to_y, new_sums = outs
        for n, (own, to) in enumerate(((g1, one), (g3, three))):
            at = slice(n * rows, (n + 1) * rows)
            to[:rows] = plus(own[...], by_x[at], by_y[at]).astype(BF)
        put_relay(
            gx0, gy0, even_x.at[cut : 2 * cut], even_y.at[low : 2 * low], to_x, to_y.at[:rows], cut
        )
        total = sums[...] + one_term(by_y[2 * rows :])
        one[rows:] = two_terms(total)
        three[rows:] = two_terms(total)
        to_y[rows:] = two_got[rows:]
        new_sums[...] = total + one_term(two_got[rows:])

    one_sum, three_sum, gx0, gy0, sums = combine(
        "sums_one_three",
        third_step,
        [g1, g3, by_x, by_y, gx0, gy0, even_x, even_y, two_got, sums],
        [wider, wider, like, wider, shape((SMALL, cols), F32)],
    )
    one_got, three_got = to_line(one_sum, 1), to_line(three_sum, 3)
    gx0, gy0 = over_x(gx0), over_y(gy0)

    def sum_parts(ins, outs):
        for n, out in enumerate(outs):
            out[...] = plus(*(r[n * share : (n + 1) * share] for r in ins))

    result = shape((share, cols), F32)
    output_grad, up_grad = combine("sums_mlp", sum_parts, [mlp_sums[0], *mlp_got, mlp_two], [result] * 2)

    def last_step(ins, outs):
        sum_parts(ins[:-1], outs[:3])
        sums, gy0, one_got, three_got = ins[-1], ins[2], ins[3], ins[5]
        outs[3][...] = sums[...] + (one_term(gy0[rows:]) + one_term(one_got[rows:]) + one_term(three_got[rows:]))

    *grads, sums = combine(
        "sums_attention",
        last_step,
        [g0, gx0, gy0, one_got, two_got, three_got, sums],
        [result] * 3 + [shape((SMALL, cols), F32)],
    )
    sums = own_parts(me, sums, share)
    return layer_out, input_grad, [*grads, output_grad, up_grad, down_grad], sums


def solution(mesh):
    rows = P("dp", None)
    wide = P("dp", "mp")
    tall = P("mp", "dp")
    return jax.shard_map(
        local,
        mesh=mesh,
        in_specs=(rows,) * 5
        + (wide, wide, wide, tall, P("dp"), P("dp"), wide, P("mp"), tall, P("dp")),
        out_specs=(rows, rows, wide, wide, wide, tall, P("dp"), P("dp"), wide, P("mp"), tall, P("dp")),
        check_vma=False,
    )
```

```python
import math

import jax
import jax.numpy as jnp
import numpy as np
from jax import lax
from jax.experimental import pallas as pl
from jax.experimental.pallas import tpu as pltpu
from jax.sharding import PartitionSpec as P

HD = 80
NCLASS = 3
PATCHES = 16
TILE = 352
LANES = 128
BF = jnp.bfloat16
F32 = jnp.float32
ROOT = math.sqrt(HD)
ROOM = 6 * 1024 * 1024
SMALL = 8


def pairs(move):
    out = []
    for z in range(4):
        for y in range(2):
            for x in range(2):
                a, b, c = move(z, y, x)
                out.append(((z * 2 + y) * 2 + x, (a * 2 + b) * 2 + c))
    return out


def over_x(field):
    return lax.ppermute(field, "dp", pairs(lambda z, y, x: (z, y, 1 - x)))


def over_y(field):
    return lax.ppermute(field, "dp", pairs(lambda z, y, x: (z, 1 - y, x)))


def up_z(field, k):
    return lax.ppermute(field, "dp", pairs(lambda z, y, x: ((z + k) % 4, y, x)))


def over_mp(field):
    return lax.ppermute(field, "mp", [(0, 1), (1, 0)])


def gridded():
    return lax.axis_size("dp") == 16


def chip_order():
    me = lax.axis_index("dp")
    z, y, x = me // 4, (me // 2) % 2, me % 2
    k = jnp.arange(16, dtype=jnp.int32)
    line, square = k // 4, k % 4
    return ((z - line + 4) % 4) * 4 + (y ^ (square // 2)) * 2 + (x ^ (square % 2))


def together(*values):
    return lax.optimization_barrier(values)


def halves(rows):
    cut = (rows // 2 + 15) // 16 * 16
    return slice(0, cut), slice(cut, rows)


def to_line(field, k):
    return up_z(field, 4 - k)


COST = 1.0

NN = (((1,), (0,)), ((), ()))
NT = (((1,), (1,)), ((), ()))
TN = (((0,), (0,)), ((), ()))
shape = jax.ShapeDtypeStruct


def dot(a, b, dims=NN):
    return lax.dot_general(a, b, dims, preferred_element_type=F32)


def run(name, body, inputs, outs, scratch=(), flops=0, order=None, aliases=None):
    specs = [pl.BlockSpec(memory_space=pltpu.VMEM)] * len(inputs)
    if order is not None:
        inputs, specs = [order, *inputs], [pl.BlockSpec(memory_space=pltpu.SMEM), *specs]
    moved = sum(math.prod(a.shape) * a.dtype.itemsize for a in [*inputs, *outs])
    return pl.pallas_call(
        body,
        name=name,
        in_specs=specs,
        out_specs=[pl.BlockSpec(memory_space=pltpu.VMEM)] * len(outs),
        out_shape=outs,
        scratch_shapes=list(scratch),
        input_output_aliases=aliases or {},
        compiler_params=pltpu.CompilerParams(
            vmem_limit_bytes=ROOM + moved + sum(math.prod(f.shape) * f.dtype.itemsize for f in scratch)
        ),
        cost_estimate=pl.CostEstimate(flops=int(COST * flops), bytes_accessed=int(COST * moved), transcendentals=0),
    )(*inputs)


def tiles(count, size=TILE):
    return [slice(start, start + size) for start in range(0, count, size)]


def pair_columns(p):
    first = 2 * p * HD // LANES * LANES
    return slice(first, first + 2 * LANES)


def apart(p, field):
    lane = lax.broadcasted_iota(jnp.int32, (1, 2 * LANES), 1) + pair_columns(p).start
    zero = jnp.zeros((), field.dtype)
    heads = [jnp.where((lane >= h * HD) & (lane < h * HD + HD), field, zero) for h in (2 * p, 2 * p + 1)]
    return jnp.concatenate(heads, axis=0)


def add_pair(sums, p, part):
    first = pair_columns(p).start // LANES
    for c in range(2):
        piece = part[:, c * LANES : (c + 1) * LANES]
        sums[first + c] = piece if sums[first + c] is None else sums[first + c] + piece


def sideways(field, size):
    return jnp.concatenate([field[:, :size].T, field[:, size:].T], axis=1)


def rope(v, cos, left_sin, right_sin):
    rows, cols = v.shape
    left = pltpu.roll(v, cols - HD // 2, 1)
    right = pltpu.roll(v, HD // 2, 1)
    three = lambda f: f.reshape(rows // PATCHES, PATCHES, cols)
    out = three(v) * cos + three(left) * left_sin + three(right) * right_sin
    return out.reshape(rows, cols)


def rope_tables(heads):
    half = HD // 2
    i = np.arange(half, dtype=np.float32)
    rates = np.exp(np.float32(-math.log(10000.0)) * (np.float32(2.0) * i / np.float32(HD))).astype(np.float32)
    angle = np.arange(PATCHES, dtype=np.float32)[:, None] * rates[None, :]
    cos, sin = np.cos(angle).astype(np.float32), np.sin(angle).astype(np.float32)
    zero = np.zeros_like(sin)
    full = lambda a, b: np.tile(np.concatenate([a, b], 1), (1, heads))
    return full(cos, cos), full(-sin, zero), full(zero, sin)


def row_of(small, at):
    return jnp.concatenate([small[at : at + 1, :], small[at + 1 : at + 2, :]], axis=1)


def token_weight(info, rows, small):
    counts = [small[6:7, c : c + 1] for c in range(NCLASS)]
    total = counts[0] + counts[1] + counts[2]
    return sum(info[rows, 1 + c : 2 + c] * (total / (NCLASS * counts[c])) for c in range(NCLASS))


def scale_of(field):
    return lax.rsqrt(jnp.mean(field * field, axis=-1, keepdims=True) + 1e-06)


def upper(rows):
    return rows // 2 // 16 * 16 + 16


def query_blocks(count, do):
    full = count // LANES

    def body(b, carry):
        do(b, pl.ds(pl.multiple_of(b * LANES, LANES), LANES), LANES)
        return carry

    lax.fori_loop(0, full, body, 0)
    if count % LANES:
        do(full, slice(full * LANES, count), count % LANES)


def combine(name, body, inputs, outs):
    return run(name, lambda *refs: body(refs[: len(inputs)], refs[len(inputs) :]), inputs, outs)


def stacked(name, *fields):
    def body(ins, outs):
        for n, ref in enumerate(ins):
            outs[0][n] = ref[...]

    return combine(name, body, fields, [shape((len(fields), *fields[0].shape), fields[0].dtype)])[0]


def cut_out(name, *wanted):
    def body(ins, outs):
        for ref, out, (_, first, end) in zip(ins, outs, wanted):
            out[...] = ref[first:end]

    outs = [shape((end - first, *f.shape[1:]), f.dtype) for f, first, end in wanted]
    return combine(name, body, [f for f, _, _ in wanted], outs)


def two_terms(field):
    high = field.astype(BF).astype(F32)
    return jnp.concatenate([high, field - high], axis=0).astype(BF)


def one_term(pair):
    pair = pair.astype(F32)
    return pair[:SMALL] + pair[SMALL:]


def plus(*fields):
    return sum(f.astype(F32) for f in fields)


def put_relay(gx, gy, via_x, via_y, to_x, to_y, top):
    to_x[:top] = gx[:top]
    to_x[top:] = plus(gx[top:], via_y[...]).astype(BF)
    to_y[:top] = plus(gy[:top], via_x[...]).astype(BF)
    to_y[top:] = gy[top:]


def relay(name, gx, gy, via_x, via_y, top):
    body = lambda ins, outs: put_relay(*ins, *outs, top)
    return combine(name, body, [gx, gy, via_x, via_y], [shape(gx.shape, BF)] * 2)


def place(name, order, gathered, names, share, into=None):
    arrays = []
    for array, *_ in gathered:
        if not any(array is a for a in arrays):
            arrays.append(array)
    cols = arrays[0].shape[-1]
    into = list(into or ())

    def body(order, *refs):
        out = refs[len(arrays) + len(into) :]
        for array, index, line, square, start in gathered:
            ref = refs[[a is array for a in arrays].index(True)]
            chip = order[line * 4 + square] * share
            for n in range(names):
                low, high = max(start, n * share), min(start + array.shape[-2], (n + 1) * share)
                if low < high:
                    to = pl.ds(pl.multiple_of(chip + (low - n * share), 16), high - low)
                    rows = slice(low - start, high - start)
                    out[n][to, :] = ref[rows, :] if index is None else ref[index, rows, :]

    aliases = {1 + len(arrays) + n: n for n in range(len(into))}
    return run(
        name, body, [*arrays, *into], [shape((16 * share, cols), BF)] * names, order=order, aliases=aliases
    )


def project(tokens, tables, small, wq, wk, wv):
    count, width = tokens.shape
    cols = wq.shape[1]

    def body(tokens, cos, left_sin, right_sin, small, wq, wk, wv, normed, q_out, k_out, v_out):
        turn = cos[...], left_sin[...], right_sin[...]
        for rows in tiles(count):
            x = tokens[rows, :].astype(F32)
            low = (x * scale_of(x) * row_of(small, 0)).astype(BF)
            normed[rows, :] = low
            q_out[rows, :] = rope(dot(low, wq[...]), *turn).astype(BF)
            k_out[rows, :] = rope(dot(low, wk[...]), *turn).astype(BF)
            v_out[rows, :] = dot(low, wv[...]).astype(BF)

    return run(
        "project",
        body,
        [tokens, *tables, small, wq, wk, wv],
        [shape((count, width), BF)] + [shape((count, cols), BF)] * 3,
        flops=6 * count * width * cols,
    )


def attend(info, coderow, queries, keys, values, heads):
    count, cols = queries.shape

    def body(info, coderow, q, k, v, probs, mixture):
        def one_block(b, rows, size):
            key_at = lax.broadcasted_iota(jnp.int32, (size, 2 * size), 0)
            query_at = lax.broadcasted_iota(jnp.int32, (size, 2 * size), 1)
            query_at = jnp.where(query_at < size, query_at, query_at - size)
            code = coderow[b][:, :size]
            same = info[rows, 0:1] == jnp.concatenate([code, code], axis=1)
            allowed = (same & (key_at < query_at)) | (key_at == query_at)
            sums = [None] * (cols // LANES)
            for p in range(heads // 2):
                here = pair_columns(p)
                scores = dot(k[rows, here], apart(p, q[rows, here]), NT) * (1.0 / ROOT)
                scores = jnp.where(allowed, scores, -1e30)
                exponent = jnp.exp(scores - jnp.max(scores, axis=0, keepdims=True))
                soft = exponent * (1.0 / jnp.sum(exponent, axis=0, keepdims=True))
                probs[p, rows, 0 : 2 * size] = soft
                add_pair(sums, p, dot(sideways(soft.astype(BF), size), apart(p, v[rows, here])))
            mixture[rows, :] = jnp.concatenate(sums, axis=1).astype(BF)

        query_blocks(count, one_block)

    return run(
        "attend",
        body,
        [info, coderow, queries, keys, values],
        [shape((heads // 2, count, 2 * LANES), F32), shape((count, cols), BF)],
        flops=40 * count * LANES * cols,
    )


def attention_backward(q, k, v, probs, mixture_grad, tables, heads):
    count, cols = q.shape

    def body(q, k, v, probs, mg, cos, left_sin, right_sin, dq_out, dk_out, dv_out, dq, dk):
        def back(b, rows, size):
            sums = [[None] * (cols // LANES) for _ in range(3)]
            for p in range(heads // 2):
                here = pair_columns(p)
                soft = probs[p, rows, 0 : 2 * size]
                grad = apart(p, mg[rows, here])
                soft_grad = dot(v[rows, here], grad, NT)
                inner = jnp.sum(soft * soft_grad, axis=0, keepdims=True)
                score_grad = (soft * (soft_grad - inner)).astype(BF)
                add_pair(sums[2], p, dot(soft.astype(BF), grad))
                add_pair(sums[0], p, dot(sideways(score_grad, size), apart(p, k[rows, here])))
                add_pair(sums[1], p, dot(score_grad, apart(p, q[rows, here])))
            dv_out[rows, :] = jnp.concatenate(sums[2], axis=1).astype(BF)
            dq[rows, :] = jnp.concatenate(sums[0], axis=1)
            dk[rows, :] = jnp.concatenate(sums[1], axis=1)

        query_blocks(count, back)
        turn = cos[...], -left_sin[...], -right_sin[...]
        for grad, out in ((dq, dq_out), (dk, dk_out)):
            for rows in tiles(count):
                out[rows, :] = rope(grad[rows, :] * (1.0 / ROOT), *turn).astype(BF)

    return run(
        "attention_backward",
        body,
        [q, k, v, probs, mixture_grad, *tables],
        [shape((count, cols), BF)] * 3,
        [pltpu.VMEM((count, cols), F32)] * 2,
        flops=12 * count * LANES * cols,
    )


def project_back(name, fields, weights):
    count, cols = fields[0].shape
    width, n = weights[0].shape[0], len(fields)

    def body(*refs):
        out = refs[-1]
        for rows in tiles(count):
            total = dot(refs[0][rows, :], refs[n][...], NT)
            for f in range(1, n):
                total = total + dot(refs[f][rows, :], refs[n + f][...], NT)
            out[rows, :] = total.astype(BF)

    return run(
        name, body, [*fields, *weights], [shape((count, width), BF)], flops=2 * n * count * width * cols
    )[0]


def attention_in_back(fields, weights, tokens):
    count, cols = fields[0].shape
    width, n = weights[0].shape[0], len(fields)

    def body(*refs):
        tokens, out = refs[2 * n :]
        parts = []
        for rows in tiles(count):
            total = dot(refs[0][rows, :], refs[n][...], NT)
            for f in range(1, n):
                total = total + dot(refs[f][rows, :], refs[n + f][...], NT)
            out[rows, :] = total.astype(BF)
            field = tokens[rows, :].astype(F32)
            parts.append(jnp.sum(total * field * scale_of(field), axis=0, keepdims=True))
        gain = sum(parts)
        high = gain.astype(BF).astype(F32)
        row = lax.broadcasted_iota(jnp.int32, (2 * SMALL, width), 0)
        out[count:, :] = jnp.where(row == 0, high, jnp.where(row == 1, gain - high, 0.0)).astype(BF)

    return run(
        "attention_in_back",
        body,
        [*fields, *weights, tokens],
        [shape((count + 2 * SMALL, width), BF)],
        flops=2 * n * count * width * cols,
    )[0]


def weigh_cotangent(cotangent, info, small):
    count, width = cotangent.shape

    def body(cot, info, small, low, total):
        parts = []
        for rows in tiles(count):
            low[rows, :] = (cot[rows, :].astype(F32) * token_weight(info, rows, small)).astype(BF)
            parts.append(jnp.sum(low[rows, :].astype(F32), axis=0, keepdims=True))
        total[...] = sum(parts)

    return run(
        "weigh_cotangent",
        body,
        [cotangent, info, small],
        [shape((count, width), BF), shape((1, width), F32)],
    )


def mlp_up(tokens, mine, other, small, up_bias, weight):
    count, width = tokens.shape
    cols = up_bias.shape[1]

    def body(tokens, mine, other, small, bias, w, hidden, normed, act, slope):
        for rows in tiles(count):
            field = tokens[rows, :].astype(F32) + (mine[rows, :].astype(F32) + other[rows, :].astype(F32))
            hidden[rows, :] = field
            low = (field * scale_of(field) * row_of(small, 2)).astype(BF)
            normed[rows, :] = low
            pre = dot(low, w[...]) + bias[...].astype(F32)
            sig = 1.0 / (1.0 + jnp.exp(-pre))
            act[rows, :] = (pre * sig).astype(BF)
            slope[rows, :] = sig * (1.0 + pre * (1.0 - sig))

    return run(
        "mlp_up",
        body,
        [tokens, mine, other, small, up_bias, weight],
        [shape((count, width), F32), shape((count, width), BF), shape((count, cols), BF), shape((count, cols), F32)],
        flops=2 * count * width * cols,
    )


def mlp_back(low, slope, down, up):
    count, width = low.shape
    cols = slope.shape[1]

    def body(low, slope, down, up, pre_grad, part, total):
        sums = []
        for rows in tiles(count):
            grad = (dot(low[rows, :], down[...]) * slope[rows, :]).astype(BF)
            pre_grad[rows, :] = grad
            sums.append(jnp.sum(grad.astype(F32), axis=0, keepdims=True))
            part[rows, :] = dot(grad, up[...], NT).astype(BF)
        total[...] = sum(sums)

    return run(
        "mlp_back",
        body,
        [low, slope, down, up],
        [shape((count, cols), BF), shape((count, width), BF), shape((1, cols), F32)],
        flops=4 * count * width * cols,
    )


def finish_output(hidden, mine, other, small):
    def body(hidden, mine, other, small, out):
        for rows in tiles(hidden.shape[0]):
            down = mine[rows, :].astype(F32) + other[rows, :].astype(F32)
            out[rows, :] = (hidden[rows, :] + (down + row_of(small, 4))).astype(BF)

    return run("finish_output", body, [hidden, mine, other, small], [shape(hidden.shape, BF)])[0]


def norm_back(field, scale, gain, grad):
    scaled = grad * gain
    inner = jnp.mean(scaled * field, axis=-1, keepdims=True)
    return scale * scaled - field * (scale * scale * scale * inner)


def hidden_back(hidden, mine, other, cotangent, info, small, weight):
    count, width = hidden.shape
    cols = weight.shape[1]

    def body(hidden, mine, other, cot, info, small, w, grad_out, low, mg, total):
        parts = []
        for rows in tiles(count):
            field = hidden[rows, :]
            grad = mine[rows, :].astype(F32) + other[rows, :].astype(F32)
            scale = scale_of(field)
            parts.append(jnp.sum(grad * field * scale, axis=0, keepdims=True))
            through = norm_back(field, scale, row_of(small, 2), grad)
            result = cot[rows, :].astype(F32) * token_weight(info, rows, small) + through
            grad_out[rows, :] = result
            low[rows, :] = result.astype(BF)
            mg[rows, :] = dot(result.astype(BF), w[...]).astype(BF)
        total[...] = sum(parts)

    return run(
        "hidden_back",
        body,
        [hidden, mine, other, cotangent, info, small, weight],
        [shape((count, width), F32), shape((count, width), BF), shape((count, cols), BF), shape((1, width), F32)],
        flops=2 * count * width * cols,
    )


def input_back(tokens, mine, other, hidden_grad, small):
    count, width = tokens.shape

    def body(tokens, mine, other, hidden_grad, small, out):
        for rows in tiles(count):
            field = tokens[rows, :].astype(F32)
            grad = mine[rows, :].astype(F32) + other[rows, :].astype(F32)
            out[rows, :] = hidden_grad[rows, :] + norm_back(field, scale_of(field), row_of(small, 0), grad)

    return run(
        "input_back", body, [tokens, mine, other, hidden_grad, small], [shape((count, width), F32)]
    )[0]


def weight_grads(name, order, left, rights, share, kind):
    count, width = left.shape
    cols = rights[0].shape[1]
    n = len(rights)
    rows = n * share
    if kind == "whole":
        outs = [shape((width, cols), BF)] * n
    elif kind == "ring":
        outs = [shape((4, rows, cols), BF)] * 4
    elif kind == "square":
        outs = [shape((4, rows, cols), BF)] * 3 + [shape((2, rows, cols), BF)] * 2
    else:
        cut = upper(rows)
        outs = [shape((rows, cols), BF)] * 12
        outs += [shape((2 * cut, cols), BF), shape((2 * (rows - cut), cols), BF)] * 2

    def body(*refs):
        order, refs = (None, refs) if kind == "whole" else (refs[0], refs[1:])
        left, right, out = refs[0], refs[1 : n + 1], refs[n + 1 : n + 1 + len(outs)]
        whole = out if kind == "whole" else [refs[-1].at[r] for r in range(n)]
        for at in tiles(width, width // 2):
            for r in range(n):
                whole[r][at, :] = dot(left[:, at], right[r][...], TN).astype(BF)
        if kind == "whole":
            return
        for line in range(4):
            for square in range(4):
                chip = order[line * 4 + square]
                for r in range(n):
                    block = whole[r][pl.ds(pl.multiple_of(chip * share, 16), share), :]
                    to = slice(r * share, (r + 1) * share)
                    if kind == "ring":
                        out[line][square, to, :] = block
                    elif kind == "line" and square < 3:
                        out[line * 3 + square][to, :] = block
                    elif kind == "line":
                        top, rest = out[12:14] if line % 2 == 0 else out[14:16]
                        second = line in (0, 3)
                        start, end = r * share, (r + 1) * share
                        mid = min(max(cut, start), end)
                        if start < mid:
                            at = cut * second
                            top[at + start : at + mid, :] = block[: mid - start]
                        if mid < end:
                            at = (rows - cut) * second - cut
                            rest[at + mid : at + end, :] = block[mid - start :]
                    elif square < 3:
                        out[square][line, to, :] = block
                    else:
                        out[3 + line // 2][line % 2, to, :] = block

    return run(
        name,
        body,
        [left, *rights],
        outs,
        [] if kind == "whole" else [pltpu.VMEM((n, width, cols), BF)],
        flops=2 * n * count * width * cols,
        order=order,
    )


def local(
    tokens,
    cotangent,
    segment_ids,
    valid_mask,
    frequency,
    query_weight,
    key_weight,
    value_weight,
    output_weight,
    attn_gain,
    mlp_gain,
    up_weight,
    up_bias,
    down_weight,
    down_bias,
):
    dp = lax.axis_size("dp")
    me = lax.axis_index("dp")
    block_rows, patches = segment_ids.shape
    count, width = tokens.shape
    share, cols = query_weight.shape
    heads = cols // HD
    member = (frequency == jnp.arange(NCLASS, dtype=jnp.int32)[None, :]).astype(jnp.int32)
    row_valid = jnp.sum(valid_mask, axis=1)
    local_counts = jnp.sum(member * row_valid[:, None], axis=0)
    here = (jnp.arange(dp, dtype=jnp.int32) == me)[:, None]
    vectors = jnp.stack([attn_gain, mlp_gain, down_bias]).astype(F32)
    vectors = jnp.where(here[None], vectors[:, None, :], 0.0).reshape(6, cols)
    count_row = jnp.pad(local_counts.astype(F32)[None], ((0, 1), (0, cols - NCLASS)))
    small = jnp.concatenate([vectors, count_row])

    code = (jnp.arange(block_rows, dtype=jnp.int32)[:, None] * PATCHES + segment_ids).astype(F32)
    of_class = (valid_mask[:, :, None] * member[:, None, :]).astype(F32).reshape(count, NCLASS)
    key_code = jnp.where(valid_mask == 1, code, -1.0).reshape(count, 1)
    info = jnp.pad(jnp.concatenate([key_code, of_class], 1), ((0, 0), (0, 7 - NCLASS)))
    coderow = jnp.pad(code.reshape(1, count), ((0, 0), (0, -count % LANES))).reshape(-1, 1, LANES)

    weights = (query_weight, key_weight, value_weight, output_weight.T, up_weight, down_weight.T)
    layer = on_grid if gridded() else off_grid
    layer_out, input_grad, grads, sums = layer(
        tokens, cotangent, info, coderow, rope_tables(heads), small, weights, up_bias[None], heads
    )
    query_grad, key_grad, value_grad, output_grad, up_grad, down_grad = grads
    attn_gain_grad, mlp_gain_grad, down_bias_grad, up_bias_grad = sums
    return (
        layer_out,
        input_grad,
        query_grad,
        key_grad,
        value_grad,
        output_grad.T,
        attn_gain_grad.reshape(share),
        mlp_gain_grad.reshape(share),
        up_grad,
        up_bias_grad.reshape(cols),
        down_grad.T,
        down_bias_grad.reshape(share),
    )


def small_sums(mine, other, *vectors):
    cols = vectors[-1].shape[1]
    count = mine.shape[0] - 2 * SMALL

    def body(ins, outs):
        outs[0][...] = jnp.zeros_like(outs[0])
        ends = plus(ins[0][count:, :], ins[1][count:, :])
        row = 0
        for total in [ends[0:1] + ends[1:2]] + [r[...] for r in ins[2:]]:
            for start in range(0, total.shape[1], cols):
                outs[0][row : row + 1, :] = total[:, start : start + cols]
                row += 1

    return combine("small_sums", body, [mine, other, *vectors], [shape((SMALL, cols), F32)])[0]


def put_own_parts(chip, sums, outs):
    share = outs[0].shape[1]
    for n in range(3):
        row = row_of(sums, 2 * n)
        part = jnp.zeros((1, share), F32)
        for c in range(row.shape[1] // share):
            part = jnp.where(chip == c, row[:, c * share : (c + 1) * share], part)
        outs[n][...] = part
    outs[3][...] = sums[6:7, :]


def own_shapes(share, cols):
    return [shape((1, share), F32)] * 3 + [shape((1, cols), F32)]


def own_parts(me, sums, share):
    body = lambda me, sums, *outs: put_own_parts(me[0], sums[...], outs)
    outs = own_shapes(share, sums.shape[1])
    return run("own_parts", body, [sums], outs, order=me.astype(jnp.int32).reshape(1))


def off_grid(tokens, cotangent, info, coderow, tables, small, weights, up_bias, heads):
    small = lax.psum(small, "dp")
    share = weights[0].shape[0]
    wq, wk, wv, wo, wu, wd = (lax.all_gather(w, "dp", axis=0, tiled=True) for w in weights)
    normed_one, queries, keys, values = project(tokens, tables, small, wq, wk, wv)
    probs, mixture = attend(info, coderow, queries, keys, values, heads)
    attn_part = project_back("attention_out", [mixture], [wo])
    attn_other = over_mp(attn_part)
    down_low, down_bias_sum = weigh_cotangent(cotangent, info, small)
    hidden, normed_two, activated, slope = mlp_up(tokens, attn_part, attn_other, small, up_bias, wu)
    pre_grad, normed_two_part, up_bias_sum = mlp_back(down_low, slope, wd, wu)
    normed_two_other = over_mp(normed_two_part)
    down_part = project_back("mlp_down", [activated], [wd])
    layer_out = finish_output(hidden, down_part, over_mp(down_part), small)
    hidden_grad, attn_low, mixture_grad, mlp_gain_sum = hidden_back(
        hidden, normed_two_part, normed_two_other, cotangent, info, small, wo
    )
    dq, dk, dv = attention_backward(queries, keys, values, probs, mixture_grad, tables, heads)
    normed_one_part = attention_in_back([dq, dk, dv], [wq, wk, wv], tokens)
    normed_one_other = over_mp(normed_one_part)
    input_grad = input_back(tokens, normed_one_part, normed_one_other, hidden_grad, small)
    locals_ = weight_grads("attention_grads", None, normed_one, [dq, dk, dv], share, "whole")
    for left, right in ((attn_low, mixture), (normed_two, pre_grad), (down_low, activated)):
        locals_ += weight_grads("weight_grads", None, left, [right], share, "whole")
    grads = [lax.psum_scatter(g.astype(F32), "dp", scatter_dimension=0, tiled=True) for g in locals_]
    sums = small_sums(normed_one_part, normed_one_other, mlp_gain_sum, down_bias_sum, up_bias_sum)
    sums = own_parts(lax.axis_index("dp"), lax.psum(sums, "dp"), share)
    return layer_out, input_grad, grads, sums


def from_hbm(name, groups):
    flat = [f for g in groups for f in g]
    outs = [shape((sum(f.shape[0] for f in g), g[0].shape[1]), g[0].dtype) for g in groups]

    def body(*refs):
        ins, refs = refs[: len(flat)], refs[len(flat) :]
        out, held, sem, out_sem = refs[: len(groups)], refs[len(groups) : -2], refs[-2], refs[-1]
        copies, at = [], 0
        for g, group in enumerate(groups):
            row = 0
            copies.append([])
            for field in group:
                to = held[g].at[pl.ds(row, field.shape[0])]
                copies[g].append(pltpu.make_async_copy(ins[at], to, sem.at[at]))
                copies[g][-1].start()
                row, at = row + field.shape[0], at + 1
        back = [pltpu.make_async_copy(held[g], out[g], out_sem.at[g]) for g in range(len(groups))]
        for g in range(len(groups)):
            for copy in copies[g]:
                copy.wait()
            back[g].start()
        for copy in back:
            copy.wait()

    moved = sum(math.prod(o.shape) * o.dtype.itemsize for o in outs)
    return pl.pallas_call(
        body,
        name=name,
        in_specs=[pl.BlockSpec(memory_space=pltpu.HBM)] * len(flat),
        out_specs=[pl.BlockSpec(memory_space=pltpu.HBM)] * len(outs),
        out_shape=outs,
        scratch_shapes=[pltpu.VMEM(o.shape, o.dtype) for o in outs]
        + [pltpu.SemaphoreType.DMA((len(flat),)), pltpu.SemaphoreType.DMA((len(groups),))],
        compiler_params=pltpu.CompilerParams(vmem_limit_bytes=58 * 1024 * 1024),
        cost_estimate=pl.CostEstimate(flops=0, bytes_accessed=2 * moved, transcendentals=0),
    )(*flat)


def on_grid(tokens, cotangent, info, coderow, tables, small, weights, up_bias, heads):
    order, me = chip_order(), lax.axis_index("dp").astype(jnp.int32).reshape(1)
    share, cols = weights[0].shape
    rows = 3 * share
    q, k, v, o, u, d = weights
    first, four = from_hbm("stack_first", [(q, k, v), (q, k, v, d)])
    cut, low, mid = upper(rows), rows - upper(rows), 2 * share
    block = shape((share, cols), BF)
    fourfold = shape((4, share, cols), BF)
    put = lambda name, pieces, into: place(name, order, pieces, 3, share, into)
    put_one = lambda name, pieces, into=None: place(name, order, pieces, 1, share, into)

    one, three = up_z(first, 1), up_z(first, 3)
    own_x, own_y = over_x(four), over_y(four)
    small_got = lax.ppermute(small, "dp", pairs(lambda z, y, x: (z ^ 1, y, x)))

    def cut_own(ins, outs):
        outs[0][...] = ins[0][:mid]
        outs[1][...] = ins[1][mid:]

    own_a, own_b = combine("cut_own", cut_own, [own_x, own_y], [shape((mid, cols), BF)] * 2)
    own_a, own_b = over_y(own_a), over_x(own_b)
    ready = together(
        four, own_x, own_y, one, three, own_a, own_b, small, small_got, info, coderow, order, me, up_bias
    )
    four, own_x, own_y, one, three, own_a, own_b, small, small_got, info, coderow, order, me, up_bias = ready
    small = small + small_got
    two = up_z(first, 2)
    both = stacked("stack_one_three", one, three)
    both_x, both_y = over_x(both), over_y(both)
    small_got = up_z(small, 2)

    def stack_down(ins, outs):
        four, own_x, own_y, own_b = ins
        outs[0][0] = four[rows:]
        outs[0][1] = own_x[rows:]
        outs[0][2] = own_y[rows:]
        outs[0][3] = own_b[rows - mid :]

    (down_0,) = combine("stack_down", stack_down, [four, own_x, own_y, own_b], [fourfold])
    mlp_0 = stacked("stack_mlp", o, u).reshape(2 * share, cols)
    attn = put(
        "place_0",
        [(four, None, 0, 0, 0), (own_x, None, 0, 1, 0), (own_y, None, 0, 2, 0), (own_a, None, 0, 3, 0)]
        + [(own_b, None, 0, 3, mid), (one, None, 1, 0, 0), (three, None, 3, 0, 0)],
        None,
    )
    both_x, both_y, two, small, small_got, down_0, mlp_0, o, *attn = together(
        both_x, both_y, two, small, small_got, down_0, mlp_0, o, *attn
    )
    small = small + small_got

    def next_step(ins, outs):
        two, both_x, both_y = ins
        outs[0][0] = two[...]
        outs[0][1] = both_y[1]
        outs[1][0] = two[...]
        outs[1][1] = both_x[0]

    by_x, by_y = combine("stack_two", next_step, [two, both_x, both_y], [shape(both.shape, BF)] * 2)
    mlp_1, out_3 = up_z(mlp_0, 1), up_z(o, 3)
    by_x, by_y = over_x(by_x), over_y(by_y)
    small_got = over_x(small)
    attn = put(
        "place_1",
        [(both_x, 0, 1, 1, 0), (both_y, 0, 1, 2, 0), (both_x, 1, 3, 1, 0), (both_y, 1, 3, 2, 0), (two, None, 2, 0, 0)],
        attn,
    )
    by_x, by_y, small, small_got, mlp_1, down_0, out_3, *attn = together(
        by_x, by_y, small, small_got, mlp_1, down_0, out_3, *attn
    )

    def halves(ins, outs):
        outs[0][...] = ins[0][0, :cut]
        outs[1][...] = ins[1][0, cut:]

    two_a, two_b = combine("cut_two", halves, [by_x, by_y], [shape((cut, cols), BF), shape((low, cols), BF)])
    small = small + small_got
    two_a, two_b = over_y(two_a), over_x(two_b)
    small_got = over_y(small)
    mlp_2, down_1 = up_z(mlp_1, 1), up_z(down_0, 1)
    attn = put(
        "place_2",
        [(by_y, 1, 1, 3, 0), (by_x, 1, 3, 3, 0), (by_x, 0, 2, 1, 0), (by_y, 0, 2, 2, 0)],
        attn,
    )
    two_a, two_b, small, small_got, mlp_2, *attn = together(two_a, two_b, small, small_got, mlp_2, *attn)
    small = small + small_got

    def stack_output(ins, outs):
        for k, ref in enumerate(ins):
            outs[0][k] = ref[:share]

    (wo_own,) = combine("stack_output", stack_output, [o, mlp_1, mlp_2, out_3], [fourfold])
    lines = lambda *arrays: [(a, k, k, s, 0) for s, a in enumerate(arrays) for k in range(4)]
    diagonal = lambda a, b: [((a, b)[k // 2], k % 2, k, 3, 0) for k in range(4)]
    wo_x, wo_y = over_x(wo_own), over_y(wo_own)
    mlp_3 = up_z(mlp_2, 1)
    wq, wk, wv = put("place_3", [(two_a, None, 2, 3, 0), (two_b, None, 2, 3, cut)], attn)
    normed_one, queries, keys, values = project(tokens, tables, small, wq, wk, wv)
    wo_x, wo_y, mlp_3, queries, wo_own, down_1 = together(wo_x, wo_y, mlp_3, queries, wo_own, down_1)

    def cut_output(ins, outs):
        wo_x, wo_y, up_0, mlp_1, mlp_2, mlp_3 = ins
        outs[0][...] = wo_x[:2]
        outs[1][...] = wo_y[2:]
        outs[2][0] = up_0[...]
        for k, ref in enumerate((mlp_1, mlp_2, mlp_3)):
            outs[2][k + 1] = ref[share:]

    twofold = shape((2, share, cols), BF)
    wo_a, wo_b, wu_own = combine(
        "cut_output", cut_output, [wo_x, wo_y, u, mlp_1, mlp_2, mlp_3], [twofold, twofold, fourfold]
    )
    wo_a, wo_b = over_y(wo_a), over_x(wo_b)
    wu_x, wu_y = over_x(wu_own), over_y(wu_own)
    down_2 = up_z(down_1, 1)
    probs, mixture = attend(info, coderow, queries, keys, values, heads)
    wo = put_one("place_output", lines(wo_own, wo_x, wo_y))
    down_low, down_bias_sum = weigh_cotangent(cotangent, info, small)
    (wo,) = put_one("place_output_end", diagonal(wo_a, wo_b), wo)
    attn_part = project_back("attention_out", [mixture], [wo])
    wu_x, wu_y, attn_part, down_low, down_2, wu_own = together(wu_x, wu_y, attn_part, down_low, down_2, wu_own)

    attn_other = over_mp(attn_part)
    wu_a, wu_b = cut_out("cut_up", (wu_x, 0, 2), (wu_y, 2, 4))
    wu_a, wu_b = over_y(wu_a), over_x(wu_b)
    down_3 = up_z(down_2, 1)
    wu = put_one("place_up", lines(wu_own, wu_x, wu_y))
    by_line = lambda k, a: [(a, s, k, s, 0) for s in range(4)]
    wd = put_one("place_down", by_line(0, down_0) + by_line(1, down_1) + by_line(2, down_2))
    attn_other, wu_a, wu_b, *wu = together(attn_other, wu_a, wu_b, *wu)
    (wu,) = put_one("place_up_end", diagonal(wu_a, wu_b), wu)
    hidden, normed_two, activated, slope = mlp_up(tokens, attn_part, attn_other, small, up_bias, wu)

    grads_of = lambda name, left, right, kind: weight_grads(name, order, left, right, share, kind)
    down_3, slope, activated = together(down_3, slope, activated)
    (wd,) = put_one("place_down_end", by_line(3, down_3), wd)
    pre_grad, normed_two_part, up_bias_sum = mlp_back(down_low, slope, wd, wu)
    normed_two_part, activated, down_low, pre_grad = together(normed_two_part, activated, down_low, pre_grad)
    normed_two_other = over_mp(normed_two_part)
    d_0, d_1, d_2, d_3 = grads_of("down_grads", down_low, [activated], "ring")
    d_got = up_z(d_1, 1)
    u_own, u_x, u_y, u_a, u_b = grads_of("up_grads", normed_two, [pre_grad], "square")
    u_a, u_b = over_x(u_a), over_y(u_b)
    down_part = project_back("mlp_down", [activated], [wd])
    hidden_grad, attn_low, mixture_grad, mlp_gain_sum = hidden_back(
        hidden, normed_two_part, normed_two_other, cotangent, info, small, wo
    )
    u_a, u_b, down_part, mixture_grad, attn_low = together(u_a, u_b, down_part, mixture_grad, attn_low)

    def ring_step(name, mine, got):
        def body(ins, outs):
            for s in range(4):
                outs[0][s] = plus(ins[0][s], ins[1][s]).astype(BF)

        return up_z(combine(name, body, [mine, got], [fourfold])[0], 1)

    u_x, u_y = relay("relay_up", u_x, u_y, u_a, u_b, 2)
    u_x, u_y = over_x(u_x), over_y(u_y)
    o_own, o_x, o_y, o_a, o_b = grads_of("output_grads", attn_low, [mixture], "square")
    d_got, o_a, o_b, mixture_grad = together(d_got, o_a, o_b, mixture_grad)
    d_got = ring_step("ring_two", d_2, d_got)
    o_a, o_b = over_x(o_a), over_y(o_b)
    dq, dk, dv = attention_backward(queries, keys, values, probs, mixture_grad, tables, heads)
    u_x, u_y, o_a, o_b, dq, dk, dv, down_part, d_got = together(u_x, u_y, o_a, o_b, dq, dk, dv, down_part, d_got)

    d_got = ring_step("ring_three", d_3, d_got)
    down_other = over_mp(down_part)
    o_x, o_y = relay("relay_output", o_x, o_y, o_a, o_b, 2)
    o_x, o_y = over_x(o_x), over_y(o_y)
    pieces = weight_grads("attention_grads", order, normed_one, [dq, dk, dv], share, "line")
    normed_one_part = attention_in_back([dq, dk, dv], [wq, wk, wv], tokens)
    o_x, o_y, normed_one_part, down_other, d_got, *pieces = together(
        o_x, o_y, normed_one_part, down_other, d_got, *pieces
    )

    g0, gx0, gy0, g1, gx1, gy1, g2, gx2, gy2, g3, gx3, gy3, even_x, even_y, odd_x, odd_y = pieces
    like = shape((rows, cols), BF)
    d_cut = upper(share)

    even_x, even_y = over_x(even_x), over_y(even_y)

    def square_sums(ins, outs):
        for n in range(2):
            at = slice(n * share, (n + 1) * share)
            for k in range(4):
                outs[k][at] = plus(*(r[k] for r in ins[3 * n : 3 * n + 3])).astype(outs[k].dtype)

    mlp_sums = combine(
        "sums_square",
        square_sums,
        [o_own, o_x, o_y, u_own, u_x, u_y],
        [shape((2 * share, cols), F32)] + [shape((2 * share, cols), BF)] * 3,
    )
    mlp_one = to_line(mlp_sums[1], 1)
    normed_one_other = over_mp(normed_one_part)
    even_x, even_y, normed_one_other, mlp_one, mlp_two, mlp_three = together(
        even_x, even_y, normed_one_other, mlp_one, *mlp_sums[2:]
    )

    sums = small_sums(normed_one_part, normed_one_other, mlp_gain_sum, down_bias_sum, up_bias_sum)
    x_rows, y_rows = rows + 2 * cut, rows + 2 * low

    def first_step(ins, outs):
        gx2, gy2, even_x, even_y, odd_x, odd_y, d_0, d_got, sums = ins
        to_x, to_y = outs[:2]
        put_relay(gx2, gy2, even_x.at[:cut], even_y.at[:low], to_x.at[:rows], to_y.at[:rows], cut)
        to_x[rows:x_rows] = odd_x[...]
        to_y[rows:y_rows] = odd_y[...]
        diagonal = plus(d_0[3], d_got[3]).astype(BF)
        to_x[x_rows : x_rows + d_cut] = diagonal[:d_cut]
        to_y[y_rows:] = diagonal[d_cut:]
        for s in range(3):
            outs[2 + s][...] = plus(d_0[s], d_got[s]).astype(BF)
        to_x[x_rows + d_cut :] = two_terms(sums[...])

    by_x, by_y, d_own, d_x, d_y = combine(
        "relay_two",
        first_step,
        [gx2, gy2, even_x, even_y, odd_x, odd_y, d_0, d_got, sums],
        [shape((x_rows + d_cut + 2 * SMALL, cols), BF), shape((y_rows + share - d_cut, cols), BF)] + [block] * 3,
    )
    by_x, by_y = over_x(by_x), over_y(by_y)
    mlp_two, mlp_three = to_line(mlp_two, 2), to_line(mlp_three, 3)
    input_grad = input_back(tokens, normed_one_part, normed_one_other, hidden_grad, small)
    by_x, by_y, mlp_two, mlp_three, input_grad = together(by_x, by_y, mlp_two, mlp_three, input_grad)

    wider = shape((rows + 2 * SMALL, cols), BF)

    def second_step(ins, outs):
        g2, by_x, by_y, gx1, gy1, gx3, gy3, d_x, d_y, sums = ins
        two, to_x, to_y, d_to_x, d_to_y, new_sums = outs
        two[:rows] = plus(g2[...], by_x[:rows], by_y[:rows]).astype(BF)
        for n, (gx, gy) in enumerate(((gx1, gy1), (gx3, gy3))):
            via_x = by_x.at[rows + n * cut : rows + (n + 1) * cut]
            via_y = by_y.at[rows + n * low : rows + (n + 1) * low]
            at = slice(n * rows, (n + 1) * rows)
            put_relay(gx, gy, via_x, via_y, to_x.at[at], to_y.at[at], cut)
        put_relay(d_x, d_y, by_x.at[x_rows : x_rows + d_cut], by_y.at[y_rows:], d_to_x, d_to_y, d_cut)
        total = sums[...] + one_term(by_x[x_rows + d_cut :])
        new_sums[...] = total
        two[rows:] = two_terms(total)
        to_y[2 * rows :] = two_terms(total)

    two_sum, by_x, by_y, d_x, d_y, sums = combine(
        "sums_two",
        second_step,
        [g2, by_x, by_y, gx1, gy1, gx3, gy3, d_x, d_y, sums],
        [wider, shape((2 * rows, cols), BF), shape((2 * rows + 2 * SMALL, cols), BF), block, block]
        + [shape((SMALL, cols), F32)],
    )
    two_got = to_line(two_sum, 2)
    by_x, by_y = over_x(by_x), over_y(by_y)
    layer_out = finish_output(hidden, down_part, down_other, small)
    by_x, by_y, layer_out, two_got = together(by_x, by_y, layer_out, two_got)

    def third_step(ins, outs):
        g1, g3, by_x, by_y, gx0, gy0, even_x, even_y, d_x, d_y, two_got, sums = ins
        one, three, to_x, to_y, new_sums = outs
        for n, (own, to) in enumerate(((g1, one), (g3, three))):
            at = slice(n * rows, (n + 1) * rows)
            to[:rows] = plus(own[...], by_x[at], by_y[at]).astype(BF)
        put_relay(gx0, gy0, even_x.at[cut:], even_y.at[low:], to_x.at[:rows], to_y.at[:rows], cut)
        to_x[rows:] = d_x[...]
        to_y[rows : rows + share] = d_y[...]
        total = sums[...] + one_term(by_y[2 * rows :])
        one[rows:] = two_terms(total)
        three[rows:] = two_terms(total)
        to_y[rows + share :] = two_got[rows:]
        new_sums[...] = total + one_term(two_got[rows:])

    one_sum, three_sum, gx0, gy0, sums = combine(
        "sums_one_three",
        third_step,
        [g1, g3, by_x, by_y, gx0, gy0, even_x, even_y, d_x, d_y, two_got, sums],
        [wider, wider, shape((rows + share, cols), BF), shape((rows + share + 2 * SMALL, cols), BF)]
        + [shape((SMALL, cols), F32)],
    )
    one_got, three_got = to_line(one_sum, 1), to_line(three_sum, 3)
    gx0, gy0 = over_x(gx0), over_y(gy0)

    def sum_parts(ins, outs):
        for n, out in enumerate(outs):
            out[...] = plus(*(r[n * share : (n + 1) * share] for r in ins))

    result = shape((share, cols), F32)
    output_grad, up_grad = combine("sums_mlp", sum_parts, [mlp_sums[0], mlp_one, mlp_two, mlp_three], [result] * 2)

    parts = [g0, gx0, gy0, one_got, two_got, three_got]

    def last_step(me, *refs):
        ins, d_own, sums, outs = refs[:6], refs[6], refs[7], refs[8:]
        sum_parts(ins, outs[:3])
        outs[3][...] = plus(d_own[...], ins[1][rows:], ins[2][rows : rows + share])
        ends = one_term(ins[2][rows + share :]) + one_term(ins[3][rows:]) + one_term(ins[5][rows:])
        put_own_parts(me[0], sums[...] + ends, outs[4:])

    outs = [result] * 4 + own_shapes(share, cols)
    *grads, down_grad, a, b, c, e = run("sums_attention", last_step, [*parts, d_own, sums], outs, order=me)
    return layer_out, input_grad, [*grads, output_grad, up_grad, down_grad], (a, b, c, e)


def solution(mesh):
    rows = P("dp", None)
    wide = P("dp", "mp")
    tall = P("mp", "dp")
    return jax.shard_map(
        local,
        mesh=mesh,
        in_specs=(rows,) * 5
        + (wide, wide, wide, tall, P("dp"), P("dp"), wide, P("mp"), tall, P("dp")),
        out_specs=(rows, rows, wide, wide, wide, tall, P("dp"), P("dp"), wide, P("mp"), tall, P("dp")),
        check_vma=False,
    )
```

```python
import math

import jax
import jax.numpy as jnp
import numpy as np
from jax import lax
from jax.experimental import pallas as pl
from jax.experimental.pallas import tpu as pltpu
from jax.sharding import PartitionSpec as P

HD = 80
NCLASS = 3
PATCHES = 16
TILE = 352
LANES = 128
BF = jnp.bfloat16
F32 = jnp.float32
ROOT = math.sqrt(HD)
ROOM = 6 * 1024 * 1024
SMALL = 8


def pairs(move):
    out = []
    for z in range(4):
        for y in range(2):
            for x in range(2):
                a, b, c = move(z, y, x)
                out.append(((z * 2 + y) * 2 + x, (a * 2 + b) * 2 + c))
    return out


def over_x(field):
    return lax.ppermute(field, "dp", pairs(lambda z, y, x: (z, y, 1 - x)))


def over_y(field):
    return lax.ppermute(field, "dp", pairs(lambda z, y, x: (z, 1 - y, x)))


def up_z(field, k):
    return lax.ppermute(field, "dp", pairs(lambda z, y, x: ((z + k) % 4, y, x)))


def over_mp(field):
    return lax.ppermute(field, "mp", [(0, 1), (1, 0)])


def gridded():
    return lax.axis_size("dp") == 16


def chip_order():
    me = lax.axis_index("dp")
    z, y, x = me // 4, (me // 2) % 2, me % 2
    k = jnp.arange(16, dtype=jnp.int32)
    line, square = k // 4, k % 4
    return ((z - line + 4) % 4) * 4 + (y ^ (square // 2)) * 2 + (x ^ (square % 2))


def together(*values):
    return lax.optimization_barrier(values)


def halves(rows):
    cut = (rows // 2 + 15) // 16 * 16
    return slice(0, cut), slice(cut, rows)


def to_line(field, k):
    return up_z(field, 4 - k)


COST = 1.0

NN = (((1,), (0,)), ((), ()))
NT = (((1,), (1,)), ((), ()))
TN = (((0,), (0,)), ((), ()))
shape = jax.ShapeDtypeStruct


def dot(a, b, dims=NN):
    return lax.dot_general(a, b, dims, preferred_element_type=F32)


def run(name, body, inputs, outs, scratch=(), flops=0, order=None, aliases=None):
    specs = [pl.BlockSpec(memory_space=pltpu.VMEM)] * len(inputs)
    if order is not None:
        inputs, specs = [order, *inputs], [pl.BlockSpec(memory_space=pltpu.SMEM), *specs]
    moved = sum(math.prod(a.shape) * a.dtype.itemsize for a in [*inputs, *outs])
    return pl.pallas_call(
        body,
        name=name,
        in_specs=specs,
        out_specs=[pl.BlockSpec(memory_space=pltpu.VMEM)] * len(outs),
        out_shape=outs,
        scratch_shapes=list(scratch),
        input_output_aliases=aliases or {},
        compiler_params=pltpu.CompilerParams(
            vmem_limit_bytes=ROOM + moved + sum(math.prod(f.shape) * f.dtype.itemsize for f in scratch)
        ),
        cost_estimate=pl.CostEstimate(flops=int(COST * flops), bytes_accessed=int(COST * moved), transcendentals=0),
    )(*inputs)


def tiles(count, size=TILE):
    return [slice(start, start + size) for start in range(0, count, size)]


def pair_columns(p):
    first = 2 * p * HD // LANES * LANES
    return slice(first, first + 2 * LANES)


def apart(p, field):
    lane = lax.broadcasted_iota(jnp.int32, (1, 2 * LANES), 1) + pair_columns(p).start
    zero = jnp.zeros((), field.dtype)
    heads = [jnp.where((lane >= h * HD) & (lane < h * HD + HD), field, zero) for h in (2 * p, 2 * p + 1)]
    return jnp.concatenate(heads, axis=0)


def add_pair(sums, p, part):
    first = pair_columns(p).start // LANES
    for c in range(2):
        piece = part[:, c * LANES : (c + 1) * LANES]
        sums[first + c] = piece if sums[first + c] is None else sums[first + c] + piece


def sideways(field, size):
    return jnp.concatenate([field[:, :size].T, field[:, size:].T], axis=1)


def rope(v, cos, left_sin, right_sin):
    rows, cols = v.shape
    left = pltpu.roll(v, cols - HD // 2, 1)
    right = pltpu.roll(v, HD // 2, 1)
    three = lambda f: f.reshape(rows // PATCHES, PATCHES, cols)
    out = three(v) * cos + three(left) * left_sin + three(right) * right_sin
    return out.reshape(rows, cols)


def rope_tables(heads):
    half = HD // 2
    i = np.arange(half, dtype=np.float32)
    rates = np.exp(np.float32(-math.log(10000.0)) * (np.float32(2.0) * i / np.float32(HD))).astype(np.float32)
    angle = np.arange(PATCHES, dtype=np.float32)[:, None] * rates[None, :]
    cos, sin = np.cos(angle).astype(np.float32), np.sin(angle).astype(np.float32)
    zero = np.zeros_like(sin)
    full = lambda a, b: np.tile(np.concatenate([a, b], 1), (1, heads))
    return full(cos, cos), full(-sin, zero), full(zero, sin)


def row_of(small, at):
    return jnp.concatenate([small[at : at + 1, :], small[at + 1 : at + 2, :]], axis=1)


def token_weight(info, rows, small):
    counts = [small[6:7, c : c + 1] for c in range(NCLASS)]
    total = counts[0] + counts[1] + counts[2]
    return sum(info[rows, 1 + c : 2 + c] * (total / (NCLASS * counts[c])) for c in range(NCLASS))


def scale_of(field):
    return lax.rsqrt(jnp.mean(field * field, axis=-1, keepdims=True) + 1e-06)


def upper(rows):
    return rows // 2 // 16 * 16 + 16


def query_blocks(count, do):
    full = count // LANES

    def body(b, carry):
        do(b, pl.ds(pl.multiple_of(b * LANES, LANES), LANES), LANES)
        return carry

    lax.fori_loop(0, full, body, 0)
    if count % LANES:
        do(full, slice(full * LANES, count), count % LANES)


def combine(name, body, inputs, outs):
    return run(name, lambda *refs: body(refs[: len(inputs)], refs[len(inputs) :]), inputs, outs)


def stacked(name, *fields):
    def body(ins, outs):
        for n, ref in enumerate(ins):
            outs[0][n] = ref[...]

    return combine(name, body, fields, [shape((len(fields), *fields[0].shape), fields[0].dtype)])[0]


def cut_out(name, *wanted):
    def body(ins, outs):
        for ref, out, (_, first, end) in zip(ins, outs, wanted):
            out[...] = ref[first:end]

    outs = [shape((end - first, *f.shape[1:]), f.dtype) for f, first, end in wanted]
    return combine(name, body, [f for f, _, _ in wanted], outs)


def two_terms(field):
    high = field.astype(BF).astype(F32)
    return jnp.concatenate([high, field - high], axis=0).astype(BF)


def one_term(pair):
    pair = pair.astype(F32)
    return pair[:SMALL] + pair[SMALL:]


def plus(*fields):
    return sum(f.astype(F32) for f in fields)


def put_relay(gx, gy, via_x, via_y, to_x, to_y, top):
    to_x[:top] = gx[:top]
    to_x[top:] = plus(gx[top:], via_y[...]).astype(BF)
    to_y[:top] = plus(gy[:top], via_x[...]).astype(BF)
    to_y[top:] = gy[top:]


def place(name, order, gathered, names, share, into=None):
    arrays = []
    for array, *_ in gathered:
        if not any(array is a for a in arrays):
            arrays.append(array)
    cols = arrays[0].shape[-1]
    into = list(into or ())

    def body(order, *refs):
        out = refs[len(arrays) + len(into) :]
        for array, index, line, square, start in gathered:
            ref = refs[[a is array for a in arrays].index(True)]
            chip = order[line * 4 + square] * share
            for n in range(names):
                low, high = max(start, n * share), min(start + array.shape[-2], (n + 1) * share)
                if low < high:
                    to = pl.ds(pl.multiple_of(chip + (low - n * share), 16), high - low)
                    rows = slice(low - start, high - start)
                    out[n][to, :] = ref[rows, :] if index is None else ref[index, rows, :]

    aliases = {1 + len(arrays) + n: n for n in range(len(into))}
    return run(
        name, body, [*arrays, *into], [shape((16 * share, cols), BF)] * names, order=order, aliases=aliases
    )


def project(tokens, tables, small, wq, wk, wv):
    count, width = tokens.shape
    cols = wq.shape[1]

    def body(tokens, cos, left_sin, right_sin, small, wq, wk, wv, normed, q_out, k_out, v_out):
        turn = cos[...], left_sin[...], right_sin[...]
        for rows in tiles(count):
            x = tokens[rows, :].astype(F32)
            low = (x * scale_of(x) * row_of(small, 0)).astype(BF)
            normed[rows, :] = low
            q_out[rows, :] = rope(dot(low, wq[...]), *turn).astype(BF)
            k_out[rows, :] = rope(dot(low, wk[...]), *turn).astype(BF)
            v_out[rows, :] = dot(low, wv[...]).astype(BF)

    return run(
        "project",
        body,
        [tokens, *tables, small, wq, wk, wv],
        [shape((count, width), BF)] + [shape((count, cols), BF)] * 3,
        flops=6 * count * width * cols,
    )


def attend(info, coderow, queries, keys, values, heads):
    count, cols = queries.shape

    def body(info, coderow, q, k, v, probs, mixture):
        def one_block(b, rows, size):
            key_at = lax.broadcasted_iota(jnp.int32, (size, 2 * size), 0)
            query_at = lax.broadcasted_iota(jnp.int32, (size, 2 * size), 1)
            query_at = jnp.where(query_at < size, query_at, query_at - size)
            code = coderow[b][:, :size]
            same = info[rows, 0:1] == jnp.concatenate([code, code], axis=1)
            allowed = (same & (key_at < query_at)) | (key_at == query_at)
            sums = [None] * (cols // LANES)
            for p in range(heads // 2):
                here = pair_columns(p)
                scores = dot(k[rows, here], apart(p, q[rows, here]), NT) * (1.0 / ROOT)
                scores = jnp.where(allowed, scores, -1e30)
                exponent = jnp.exp(scores - jnp.max(scores, axis=0, keepdims=True))
                soft = exponent * (1.0 / jnp.sum(exponent, axis=0, keepdims=True))
                probs[p, rows, 0 : 2 * size] = soft
                add_pair(sums, p, dot(sideways(soft.astype(BF), size), apart(p, v[rows, here])))
            mixture[rows, :] = jnp.concatenate(sums, axis=1).astype(BF)

        query_blocks(count, one_block)

    return run(
        "attend",
        body,
        [info, coderow, queries, keys, values],
        [shape((heads // 2, count, 2 * LANES), F32), shape((count, cols), BF)],
        flops=40 * count * LANES * cols,
    )


def attention_backward(q, k, v, probs, mixture_grad, tables, heads):
    count, cols = q.shape

    def body(q, k, v, probs, mg, cos, left_sin, right_sin, dq_out, dk_out, dv_out, dq, dk):
        def back(b, rows, size):
            sums = [[None] * (cols // LANES) for _ in range(3)]
            for p in range(heads // 2):
                here = pair_columns(p)
                soft = probs[p, rows, 0 : 2 * size]
                grad = apart(p, mg[rows, here])
                soft_grad = dot(v[rows, here], grad, NT)
                inner = jnp.sum(soft * soft_grad, axis=0, keepdims=True)
                score_grad = (soft * (soft_grad - inner)).astype(BF)
                add_pair(sums[2], p, dot(soft.astype(BF), grad))
                add_pair(sums[0], p, dot(sideways(score_grad, size), apart(p, k[rows, here])))
                add_pair(sums[1], p, dot(score_grad, apart(p, q[rows, here])))
            dv_out[rows, :] = jnp.concatenate(sums[2], axis=1).astype(BF)
            dq[rows, :] = jnp.concatenate(sums[0], axis=1)
            dk[rows, :] = jnp.concatenate(sums[1], axis=1)

        query_blocks(count, back)
        turn = cos[...], -left_sin[...], -right_sin[...]
        for grad, out in ((dq, dq_out), (dk, dk_out)):
            for rows in tiles(count):
                out[rows, :] = rope(grad[rows, :] * (1.0 / ROOT), *turn).astype(BF)

    return run(
        "attention_backward",
        body,
        [q, k, v, probs, mixture_grad, *tables],
        [shape((count, cols), BF)] * 3,
        [pltpu.VMEM((count, cols), F32)] * 2,
        flops=12 * count * LANES * cols,
    )


def project_back(name, fields, weights):
    count, cols = fields[0].shape
    width, n = weights[0].shape[0], len(fields)

    def body(*refs):
        out = refs[-1]
        for rows in tiles(count):
            total = dot(refs[0][rows, :], refs[n][...], NT)
            for f in range(1, n):
                total = total + dot(refs[f][rows, :], refs[n + f][...], NT)
            out[rows, :] = total.astype(BF)

    return run(
        name, body, [*fields, *weights], [shape((count, width), BF)], flops=2 * n * count * width * cols
    )[0]


def attention_in_back(fields, weights, tokens):
    count, cols = fields[0].shape
    width, n = weights[0].shape[0], len(fields)

    def body(*refs):
        tokens, out = refs[2 * n :]
        parts = []
        for rows in tiles(count):
            total = dot(refs[0][rows, :], refs[n][...], NT)
            for f in range(1, n):
                total = total + dot(refs[f][rows, :], refs[n + f][...], NT)
            out[rows, :] = total.astype(BF)
            field = tokens[rows, :].astype(F32)
            parts.append(jnp.sum(total * field * scale_of(field), axis=0, keepdims=True))
        gain = sum(parts)
        high = gain.astype(BF).astype(F32)
        row = lax.broadcasted_iota(jnp.int32, (2 * SMALL, width), 0)
        out[count:, :] = jnp.where(row == 0, high, jnp.where(row == 1, gain - high, 0.0)).astype(BF)

    return run(
        "attention_in_back",
        body,
        [*fields, *weights, tokens],
        [shape((count + 2 * SMALL, width), BF)],
        flops=2 * n * count * width * cols,
    )[0]


def weigh_cotangent(cotangent, info, small):
    count, width = cotangent.shape

    def body(cot, info, small, low, total):
        parts = []
        for rows in tiles(count):
            low[rows, :] = (cot[rows, :].astype(F32) * token_weight(info, rows, small)).astype(BF)
            parts.append(jnp.sum(low[rows, :].astype(F32), axis=0, keepdims=True))
        total[...] = sum(parts)

    return run(
        "weigh_cotangent",
        body,
        [cotangent, info, small],
        [shape((count, width), BF), shape((1, width), F32)],
    )


def mlp_up(tokens, mine, other, small, up_bias, weight):
    count, width = tokens.shape
    cols = up_bias.shape[1]

    def body(tokens, mine, other, small, bias, w, hidden, normed, act, slope):
        for rows in tiles(count):
            field = tokens[rows, :].astype(F32) + (mine[rows, :].astype(F32) + other[rows, :].astype(F32))
            hidden[rows, :] = field
            low = (field * scale_of(field) * row_of(small, 2)).astype(BF)
            normed[rows, :] = low
            pre = dot(low, w[...]) + bias[...].astype(F32)
            sig = 1.0 / (1.0 + jnp.exp(-pre))
            act[rows, :] = (pre * sig).astype(BF)
            slope[rows, :] = sig * (1.0 + pre * (1.0 - sig))

    return run(
        "mlp_up",
        body,
        [tokens, mine, other, small, up_bias, weight],
        [shape((count, width), F32), shape((count, width), BF), shape((count, cols), BF), shape((count, cols), F32)],
        flops=2 * count * width * cols,
    )


def mlp_back(low, slope, down, up):
    count, width = low.shape
    cols = slope.shape[1]

    def body(low, slope, down, up, pre_grad, part, total):
        sums = []
        for rows in tiles(count):
            grad = (dot(low[rows, :], down[...]) * slope[rows, :]).astype(BF)
            pre_grad[rows, :] = grad
            sums.append(jnp.sum(grad.astype(F32), axis=0, keepdims=True))
            part[rows, :] = dot(grad, up[...], NT).astype(BF)
        total[...] = sum(sums)

    return run(
        "mlp_back",
        body,
        [low, slope, down, up],
        [shape((count, cols), BF), shape((count, width), BF), shape((1, cols), F32)],
        flops=4 * count * width * cols,
    )


def finish_output(hidden, mine, other, small):
    def body(hidden, mine, other, small, out):
        for rows in tiles(hidden.shape[0]):
            down = mine[rows, :].astype(F32) + other[rows, :].astype(F32)
            out[rows, :] = (hidden[rows, :] + (down + row_of(small, 4))).astype(BF)

    return run("finish_output", body, [hidden, mine, other, small], [shape(hidden.shape, BF)])[0]


def norm_back(field, scale, gain, grad):
    scaled = grad * gain
    inner = jnp.mean(scaled * field, axis=-1, keepdims=True)
    return scale * scaled - field * (scale * scale * scale * inner)


def hidden_back(hidden, mine, other, cotangent, info, small, weight):
    count, width = hidden.shape
    cols = weight.shape[1]

    def body(hidden, mine, other, cot, info, small, w, grad_out, low, mg, total):
        parts = []
        for rows in tiles(count):
            field = hidden[rows, :]
            grad = mine[rows, :].astype(F32) + other[rows, :].astype(F32)
            scale = scale_of(field)
            parts.append(jnp.sum(grad * field * scale, axis=0, keepdims=True))
            through = norm_back(field, scale, row_of(small, 2), grad)
            result = cot[rows, :].astype(F32) * token_weight(info, rows, small) + through
            grad_out[rows, :] = result
            low[rows, :] = result.astype(BF)
            mg[rows, :] = dot(result.astype(BF), w[...]).astype(BF)
        total[...] = sum(parts)

    return run(
        "hidden_back",
        body,
        [hidden, mine, other, cotangent, info, small, weight],
        [shape((count, width), F32), shape((count, width), BF), shape((count, cols), BF), shape((1, width), F32)],
        flops=2 * count * width * cols,
    )


def input_back(tokens, mine, other, hidden_grad, small):
    count, width = tokens.shape

    def body(tokens, mine, other, hidden_grad, small, out):
        for rows in tiles(count):
            field = tokens[rows, :].astype(F32)
            grad = mine[rows, :].astype(F32) + other[rows, :].astype(F32)
            out[rows, :] = hidden_grad[rows, :] + norm_back(field, scale_of(field), row_of(small, 0), grad)

    return run(
        "input_back", body, [tokens, mine, other, hidden_grad, small], [shape((count, width), F32)]
    )[0]


def weight_grads(name, order, left, rights, share, kind):
    count, width = left.shape
    cols = rights[0].shape[1]
    n = len(rights)
    rows = n * share
    if kind == "whole":
        outs = [shape((width, cols), BF)] * n
    elif kind == "ring":
        outs = [shape((4, rows, cols), BF)] * 4
    elif kind == "square":
        outs = [shape((4, rows, cols), BF)] * 3 + [shape((2, rows, cols), BF)] * 2
    else:
        cut = upper(rows)
        outs = [shape((rows, cols), BF)] * 12
        outs += [shape((2 * cut, cols), BF), shape((2 * (rows - cut), cols), BF)] * 2

    def body(*refs):
        order, refs = (None, refs) if kind == "whole" else (refs[0], refs[1:])
        left, right, out = refs[0], refs[1 : n + 1], refs[n + 1 : n + 1 + len(outs)]
        whole = out if kind == "whole" else [refs[-1].at[r] for r in range(n)]
        for at in tiles(width, width // 2):
            for r in range(n):
                whole[r][at, :] = dot(left[:, at], right[r][...], TN).astype(BF)
        if kind == "whole":
            return
        for line in range(4):
            for square in range(4):
                chip = order[line * 4 + square]
                for r in range(n):
                    block = whole[r][pl.ds(pl.multiple_of(chip * share, 16), share), :]
                    to = slice(r * share, (r + 1) * share)
                    if kind == "ring":
                        out[line][square, to, :] = block
                    elif kind == "line" and square < 3:
                        out[line * 3 + square][to, :] = block
                    elif kind == "line":
                        top, rest = out[12:14] if line % 2 == 0 else out[14:16]
                        second = line in (0, 3)
                        start, end = r * share, (r + 1) * share
                        mid = min(max(cut, start), end)
                        if start < mid:
                            at = cut * second
                            top[at + start : at + mid, :] = block[: mid - start]
                        if mid < end:
                            at = (rows - cut) * second - cut
                            rest[at + mid : at + end, :] = block[mid - start :]
                    elif square < 3:
                        out[square][line, to, :] = block
                    else:
                        out[3 + line // 2][line % 2, to, :] = block

    return run(
        name,
        body,
        [left, *rights],
        outs,
        [] if kind == "whole" else [pltpu.VMEM((n, width, cols), BF)],
        flops=2 * n * count * width * cols,
        order=order,
    )


def local(
    tokens,
    cotangent,
    segment_ids,
    valid_mask,
    frequency,
    query_weight,
    key_weight,
    value_weight,
    output_weight,
    attn_gain,
    mlp_gain,
    up_weight,
    up_bias,
    down_weight,
    down_bias,
):
    dp = lax.axis_size("dp")
    me = lax.axis_index("dp")
    block_rows, patches = segment_ids.shape
    count, width = tokens.shape
    share, cols = query_weight.shape
    heads = cols // HD
    member = (frequency == jnp.arange(NCLASS, dtype=jnp.int32)[None, :]).astype(jnp.int32)
    row_valid = jnp.sum(valid_mask, axis=1)
    local_counts = jnp.sum(member * row_valid[:, None], axis=0)
    here = (jnp.arange(dp, dtype=jnp.int32) == me)[:, None]
    vectors = jnp.stack([attn_gain, mlp_gain, down_bias]).astype(F32)
    vectors = jnp.where(here[None], vectors[:, None, :], 0.0).reshape(6, cols)
    count_row = jnp.pad(local_counts.astype(F32)[None], ((0, 1), (0, cols - NCLASS)))
    small = jnp.concatenate([vectors, count_row])

    code = (jnp.arange(block_rows, dtype=jnp.int32)[:, None] * PATCHES + segment_ids).astype(F32)
    of_class = (valid_mask[:, :, None] * member[:, None, :]).astype(F32).reshape(count, NCLASS)
    key_code = jnp.where(valid_mask == 1, code, -1.0).reshape(count, 1)
    info = jnp.pad(jnp.concatenate([key_code, of_class], 1), ((0, 0), (0, 7 - NCLASS)))
    coderow = jnp.pad(code.reshape(1, count), ((0, 0), (0, -count % LANES))).reshape(-1, 1, LANES)

    weights = (query_weight, key_weight, value_weight, output_weight.T, up_weight, down_weight.T)
    layer = on_grid if gridded() else off_grid
    layer_out, input_grad, grads, sums = layer(
        tokens, cotangent, info, coderow, rope_tables(heads), small, weights, up_bias[None], heads
    )
    query_grad, key_grad, value_grad, output_grad, up_grad, down_grad = grads
    attn_gain_grad, mlp_gain_grad, down_bias_grad, up_bias_grad = sums
    return (
        layer_out,
        input_grad,
        query_grad,
        key_grad,
        value_grad,
        output_grad.T,
        attn_gain_grad.reshape(share),
        mlp_gain_grad.reshape(share),
        up_grad,
        up_bias_grad.reshape(cols),
        down_grad.T,
        down_bias_grad.reshape(share),
    )


def small_sums(mine, other, *vectors):
    cols = vectors[-1].shape[1]
    count = mine.shape[0] - 2 * SMALL

    def body(ins, outs):
        outs[0][...] = jnp.zeros_like(outs[0])
        ends = plus(ins[0][count:, :], ins[1][count:, :])
        row = 0
        for total in [ends[0:1] + ends[1:2]] + [r[...] for r in ins[2:]]:
            for start in range(0, total.shape[1], cols):
                outs[0][row : row + 1, :] = total[:, start : start + cols]
                row += 1

    return combine("small_sums", body, [mine, other, *vectors], [shape((SMALL, cols), F32)])[0]


def put_own_parts(chip, sums, outs):
    share = outs[0].shape[1]
    for n in range(3):
        row = row_of(sums, 2 * n)
        part = jnp.zeros((1, share), F32)
        for c in range(row.shape[1] // share):
            part = jnp.where(chip == c, row[:, c * share : (c + 1) * share], part)
        outs[n][...] = part
    outs[3][...] = sums[6:7, :]


def own_shapes(share, cols):
    return [shape((1, share), F32)] * 3 + [shape((1, cols), F32)]


def own_parts(me, sums, share):
    body = lambda me, sums, *outs: put_own_parts(me[0], sums[...], outs)
    outs = own_shapes(share, sums.shape[1])
    return run("own_parts", body, [sums], outs, order=me.astype(jnp.int32).reshape(1))


def off_grid(tokens, cotangent, info, coderow, tables, small, weights, up_bias, heads):
    small = lax.psum(small, "dp")
    share = weights[0].shape[0]
    wq, wk, wv, wo, wu, wd = (lax.all_gather(w, "dp", axis=0, tiled=True) for w in weights)
    normed_one, queries, keys, values = project(tokens, tables, small, wq, wk, wv)
    probs, mixture = attend(info, coderow, queries, keys, values, heads)
    attn_part = project_back("attention_out", [mixture], [wo])
    attn_other = over_mp(attn_part)
    down_low, down_bias_sum = weigh_cotangent(cotangent, info, small)
    hidden, normed_two, activated, slope = mlp_up(tokens, attn_part, attn_other, small, up_bias, wu)
    pre_grad, normed_two_part, up_bias_sum = mlp_back(down_low, slope, wd, wu)
    normed_two_other = over_mp(normed_two_part)
    down_part = project_back("mlp_down", [activated], [wd])
    layer_out = finish_output(hidden, down_part, over_mp(down_part), small)
    hidden_grad, attn_low, mixture_grad, mlp_gain_sum = hidden_back(
        hidden, normed_two_part, normed_two_other, cotangent, info, small, wo
    )
    dq, dk, dv = attention_backward(queries, keys, values, probs, mixture_grad, tables, heads)
    normed_one_part = attention_in_back([dq, dk, dv], [wq, wk, wv], tokens)
    normed_one_other = over_mp(normed_one_part)
    input_grad = input_back(tokens, normed_one_part, normed_one_other, hidden_grad, small)
    locals_ = weight_grads("attention_grads", None, normed_one, [dq, dk, dv], share, "whole")
    for left, right in ((attn_low, mixture), (normed_two, pre_grad), (down_low, activated)):
        locals_ += weight_grads("weight_grads", None, left, [right], share, "whole")
    grads = [lax.psum_scatter(g.astype(F32), "dp", scatter_dimension=0, tiled=True) for g in locals_]
    sums = small_sums(normed_one_part, normed_one_other, mlp_gain_sum, down_bias_sum, up_bias_sum)
    sums = own_parts(lax.axis_index("dp"), lax.psum(sums, "dp"), share)
    return layer_out, input_grad, grads, sums


def from_hbm(name, groups):
    flat = [f for g in groups for f in g]
    outs = [shape((sum(f.shape[0] for f in g), g[0].shape[1]), g[0].dtype) for g in groups]

    def body(*refs):
        ins, refs = refs[: len(flat)], refs[len(flat) :]
        out, held, sem, out_sem = refs[: len(groups)], refs[len(groups) : -2], refs[-2], refs[-1]
        copies, at = [], 0
        for g, group in enumerate(groups):
            row = 0
            copies.append([])
            for field in group:
                to = held[g].at[pl.ds(row, field.shape[0])]
                copies[g].append(pltpu.make_async_copy(ins[at], to, sem.at[at]))
                copies[g][-1].start()
                row, at = row + field.shape[0], at + 1
        back = [pltpu.make_async_copy(held[g], out[g], out_sem.at[g]) for g in range(len(groups))]
        for g in range(len(groups)):
            for copy in copies[g]:
                copy.wait()
            back[g].start()
        for copy in back:
            copy.wait()

    moved = sum(math.prod(o.shape) * o.dtype.itemsize for o in outs)
    return pl.pallas_call(
        body,
        name=name,
        in_specs=[pl.BlockSpec(memory_space=pltpu.HBM)] * len(flat),
        out_specs=[pl.BlockSpec(memory_space=pltpu.HBM)] * len(outs),
        out_shape=outs,
        scratch_shapes=[pltpu.VMEM(o.shape, o.dtype) for o in outs]
        + [pltpu.SemaphoreType.DMA((len(flat),)), pltpu.SemaphoreType.DMA((len(groups),))],
        compiler_params=pltpu.CompilerParams(vmem_limit_bytes=58 * 1024 * 1024),
        cost_estimate=pl.CostEstimate(flops=0, bytes_accessed=2 * moved, transcendentals=0),
    )(*flat)


def on_grid(tokens, cotangent, info, coderow, tables, small, weights, up_bias, heads):
    order, me = chip_order(), lax.axis_index("dp").astype(jnp.int32).reshape(1)
    share, cols = weights[0].shape
    rows = 3 * share
    q, k, v, o, u, d = weights
    first, four = from_hbm("stack_first", [(q, k, v), (q, k, v, d)])
    cut, low, mid = upper(rows), rows - upper(rows), 2 * share
    block = shape((share, cols), BF)
    fourfold = shape((4, share, cols), BF)
    put = lambda name, pieces, into: place(name, order, pieces, 3, share, into)
    put_one = lambda name, pieces, into=None: place(name, order, pieces, 1, share, into)

    one, three = up_z(first, 1), up_z(first, 3)
    own_x, own_y = over_x(four), over_y(four)
    small_got = lax.ppermute(small, "dp", pairs(lambda z, y, x: (z ^ 1, y, x)))

    def cut_own(ins, outs):
        outs[0][...] = ins[0][:mid]
        outs[1][...] = ins[1][mid:]

    own_a, own_b = combine("cut_own", cut_own, [own_x, own_y], [shape((mid, cols), BF)] * 2)
    own_a, own_b = over_y(own_a), over_x(own_b)
    ready = together(
        four, own_x, own_y, one, three, own_a, own_b, small, small_got, info, coderow, order, me, up_bias
    )
    four, own_x, own_y, one, three, own_a, own_b, small, small_got, info, coderow, order, me, up_bias = ready
    small = small + small_got
    two = up_z(first, 2)
    both = stacked("stack_one_three", one, three)
    both_x, both_y = over_x(both), over_y(both)
    small_got = up_z(small, 2)

    def stack_down(ins, outs):
        four, own_x, own_y, own_b = ins
        outs[0][0] = four[rows:]
        outs[0][1] = own_x[rows:]
        outs[0][2] = own_y[rows:]
        outs[0][3] = own_b[rows - mid :]

    (down_0,) = combine("stack_down", stack_down, [four, own_x, own_y, own_b], [fourfold])
    mlp_0 = stacked("stack_mlp", o, u).reshape(2 * share, cols)
    attn = put(
        "place_0",
        [(four, None, 0, 0, 0), (own_x, None, 0, 1, 0), (own_y, None, 0, 2, 0), (own_a, None, 0, 3, 0)]
        + [(own_b, None, 0, 3, mid), (one, None, 1, 0, 0), (three, None, 3, 0, 0)],
        None,
    )
    both_x, both_y, two, small, small_got, down_0, mlp_0, *attn = together(
        both_x, both_y, two, small, small_got, down_0, mlp_0, *attn
    )
    small = small + small_got

    def next_step(ins, outs):
        two, both_x, both_y = ins
        outs[0][0] = two[...]
        outs[0][1] = both_y[1]
        outs[1][0] = two[...]
        outs[1][1] = both_x[0]

    by_x, by_y = combine("stack_two", next_step, [two, both_x, both_y], [shape(both.shape, BF)] * 2)
    mlp_1, mlp_3 = up_z(mlp_0, 1), up_z(mlp_0, 3)
    by_x, by_y = over_x(by_x), over_y(by_y)
    small_got = over_x(small)
    attn = put(
        "place_1",
        [(both_x, 0, 1, 1, 0), (both_y, 0, 1, 2, 0), (both_x, 1, 3, 1, 0), (both_y, 1, 3, 2, 0), (two, None, 2, 0, 0)],
        attn,
    )
    by_x, by_y, small, small_got, mlp_1, mlp_3, *attn = together(
        by_x, by_y, small, small_got, mlp_1, mlp_3, *attn
    )

    def halves(ins, outs):
        outs[0][...] = ins[0][0, :cut]
        outs[1][...] = ins[1][0, cut:]

    two_a, two_b = combine("cut_two", halves, [by_x, by_y], [shape((cut, cols), BF), shape((low, cols), BF)])
    small = small + small_got
    two_a, two_b = over_y(two_a), over_x(two_b)
    small_got = over_y(small)
    mlp_2 = up_z(mlp_1, 1)
    attn = put(
        "place_2",
        [(by_y, 1, 1, 3, 0), (by_x, 1, 3, 3, 0), (by_x, 0, 2, 1, 0), (by_y, 0, 2, 2, 0)],
        attn,
    )
    two_a, two_b, small, small_got, mlp_2, down_0, *attn = together(
        two_a, two_b, small, small_got, mlp_2, down_0, *attn
    )
    small = small + small_got

    def stack_output(ins, outs):
        for k, ref in enumerate(ins):
            outs[0][k] = ref[:share]

    (wo_own,) = combine("stack_output", stack_output, [o, mlp_1, mlp_2, mlp_3], [fourfold])
    lines = lambda *arrays: [(a, k, k, s, 0) for s, a in enumerate(arrays) for k in range(4)]
    diagonal = lambda a, b: [((a, b)[k // 2], k % 2, k, 3, 0) for k in range(4)]
    wo_x, wo_y = over_x(wo_own), over_y(wo_own)
    down_1 = up_z(down_0, 1)
    wq, wk, wv = put("place_3", [(two_a, None, 2, 3, 0), (two_b, None, 2, 3, cut)], attn)
    normed_one, queries, keys, values = project(tokens, tables, small, wq, wk, wv)
    wo_x, wo_y, queries, wo_own = together(wo_x, wo_y, queries, wo_own)

    def add_up(ins, outs):
        wo_x, wo_y, up_0, mlp_1, mlp_2, mlp_3 = ins
        for out in outs:
            out[0] = up_0[...]
            for k, ref in enumerate((mlp_1, mlp_2, mlp_3)):
                out[k + 1] = ref[share:]
        outs[0][4:] = wo_y[2:]
        outs[1][4:] = wo_x[:2]

    sixfold = shape((6, share, cols), BF)
    wu_own, up_y = combine("add_up", add_up, [wo_x, wo_y, u, mlp_1, mlp_2, mlp_3], [sixfold] * 2)
    up_x, up_y = over_x(wu_own), over_y(up_y)
    down_1, queries = together(down_1, queries)
    down_2, down_3 = up_z(down_1, 1), up_z(down_0, 3)
    probs, mixture = attend(info, coderow, queries, keys, values, heads)
    wo = put_one("place_output", lines(wo_own, wo_x, wo_y))
    down_low, down_bias_sum = weigh_cotangent(cotangent, info, small)
    up_x, up_y, mixture, down_low, down_2, wu_own, *wo = together(up_x, up_y, mixture, down_low, down_2, wu_own, *wo)

    wu_a, wu_b = cut_out("cut_up", (up_x, 0, 2), (up_y, 2, 4))
    wu_a, wu_b = over_y(wu_a), over_x(wu_b)
    (wo,) = put_one("place_output_end", [((up_y, up_x)[k // 2], 4 + k % 2, k, 3, 0) for k in range(4)], wo)
    attn_part = project_back("attention_out", [mixture], [wo])
    attn_other = over_mp(attn_part)
    wu = put_one("place_up", lines(wu_own, up_x, up_y))
    by_line = lambda k, a: [(a, s, k, s, 0) for s in range(4)]
    wd = put_one("place_down", by_line(0, down_0) + by_line(1, down_1) + by_line(2, down_2))
    attn_other, wu_a, wu_b, *wu = together(attn_other, wu_a, wu_b, *wu)
    (wu,) = put_one("place_up_end", diagonal(wu_a, wu_b), wu)
    hidden, normed_two, activated, slope = mlp_up(tokens, attn_part, attn_other, small, up_bias, wu)

    grads_of = lambda name, left, right, kind: weight_grads(name, order, left, right, share, kind)
    d_0, d_1, d_2, d_3 = grads_of("down_grads", down_low, [activated], "ring")
    down_3, slope, d_1 = together(down_3, slope, d_1)
    (wd,) = put_one("place_down_end", by_line(3, down_3), wd)
    pre_grad, normed_two_part, up_bias_sum = mlp_back(down_low, slope, wd, wu)
    normed_two_part, pre_grad = together(normed_two_part, pre_grad)
    normed_two_other = over_mp(normed_two_part)
    d_got = up_z(d_1, 1)
    u_own, u_x, u_y, u_a, u_b = grads_of("up_grads", normed_two, [pre_grad], "square")
    u_a, u_b = over_x(u_a), over_y(u_b)
    down_part = project_back("mlp_down", [activated], [wd])
    hidden_grad, attn_low, mixture_grad, mlp_gain_sum = hidden_back(
        hidden, normed_two_part, normed_two_other, cotangent, info, small, wo
    )
    o_own, o_x, o_y, o_a, o_b = grads_of("output_grads", attn_low, [mixture], "square")
    u_a, u_b, down_part, mixture_grad, o_a, o_b, d_got = together(u_a, u_b, down_part, mixture_grad, o_a, o_b, d_got)

    def ring_step(name, mine, got):
        def body(ins, outs):
            for s in range(4):
                outs[0][s] = plus(ins[0][s], ins[1][s]).astype(BF)

        return up_z(combine(name, body, [mine, got], [fourfold])[0], 1)

    def relay_up(ins, outs):
        put_relay(*ins[:4], outs[0].at[:4], outs[1].at[:4], 2)
        outs[0][4:] = ins[4][...]
        outs[1][4:] = ins[5][...]

    up_x, up_y = combine("relay_up", relay_up, [u_x, u_y, u_a, u_b, o_a, o_b], [sixfold] * 2)
    up_x, up_y = over_x(up_x), over_y(up_y)
    d_got = ring_step("ring_two", d_2, d_got)
    dq, dk, dv = attention_backward(queries, keys, values, probs, mixture_grad, tables, heads)
    d_got, dq = together(d_got, dq)
    d_got = ring_step("ring_three", d_3, d_got)
    up_x, up_y, dq, dk, dv, down_part = together(up_x, up_y, dq, dk, dv, down_part)

    down_other = over_mp(down_part)

    def relay_output(ins, outs):
        o_x, o_y, up_x, up_y = ins
        put_relay(o_x, o_y, up_x.at[4:], up_y.at[4:], *outs, 2)

    o_x, o_y = combine("relay_output", relay_output, [o_x, o_y, up_x, up_y], [fourfold] * 2)
    o_x, o_y = over_x(o_x), over_y(o_y)
    pieces = weight_grads("attention_grads", order, normed_one, [dq, dk, dv], share, "line")
    normed_one_part = attention_in_back([dq, dk, dv], [wq, wk, wv], tokens)
    o_x, o_y, normed_one_part, down_other, d_got, *pieces = together(
        o_x, o_y, normed_one_part, down_other, d_got, *pieces
    )

    g0, gx0, gy0, g1, gx1, gy1, g2, gx2, gy2, g3, gx3, gy3, even_x, even_y, odd_x, odd_y = pieces
    like = shape((rows, cols), BF)
    d_cut = upper(share)

    even_x, even_y = over_x(even_x), over_y(even_y)

    def square_sums(ins, outs):
        for n in range(2):
            at = slice(n * share, (n + 1) * share)
            for k in range(4):
                outs[k][at] = plus(*(r[k] for r in ins[3 * n : 3 * n + 3])).astype(outs[k].dtype)

    mlp_sums = combine(
        "sums_square",
        square_sums,
        [o_own, o_x, o_y, u_own, up_x, up_y],
        [shape((2 * share, cols), F32)] + [shape((2 * share, cols), BF)] * 3,
    )
    mlp_one = to_line(mlp_sums[1], 1)
    normed_one_other = over_mp(normed_one_part)
    even_x, even_y, normed_one_other, mlp_one, mlp_two, mlp_three = together(
        even_x, even_y, normed_one_other, mlp_one, *mlp_sums[2:]
    )

    sums = small_sums(normed_one_part, normed_one_other, mlp_gain_sum, down_bias_sum, up_bias_sum)
    x_rows, y_rows = rows + 2 * cut, rows + 2 * low

    def first_step(ins, outs):
        gx2, gy2, even_x, even_y, odd_x, odd_y, d_0, d_got, sums = ins
        to_x, to_y = outs[:2]
        put_relay(gx2, gy2, even_x.at[:cut], even_y.at[:low], to_x.at[:rows], to_y.at[:rows], cut)
        to_x[rows:x_rows] = odd_x[...]
        to_y[rows:y_rows] = odd_y[...]
        diagonal = plus(d_0[3], d_got[3]).astype(BF)
        to_x[x_rows : x_rows + d_cut] = diagonal[:d_cut]
        to_y[y_rows:] = diagonal[d_cut:]
        for s in range(3):
            outs[2 + s][...] = plus(d_0[s], d_got[s]).astype(BF)
        to_x[x_rows + d_cut :] = two_terms(sums[...])

    by_x, by_y, d_own, d_x, d_y = combine(
        "relay_two",
        first_step,
        [gx2, gy2, even_x, even_y, odd_x, odd_y, d_0, d_got, sums],
        [shape((x_rows + d_cut + 2 * SMALL, cols), BF), shape((y_rows + share - d_cut, cols), BF)] + [block] * 3,
    )
    by_x, by_y = over_x(by_x), over_y(by_y)
    mlp_two, mlp_three = to_line(mlp_two, 2), to_line(mlp_three, 3)
    input_grad = input_back(tokens, normed_one_part, normed_one_other, hidden_grad, small)
    by_x, by_y, mlp_two, mlp_three, input_grad = together(by_x, by_y, mlp_two, mlp_three, input_grad)

    wider = shape((rows + 2 * SMALL, cols), BF)

    def second_step(ins, outs):
        g2, by_x, by_y, gx1, gy1, gx3, gy3, d_x, d_y, sums = ins
        two, to_x, to_y, d_to_x, d_to_y, new_sums = outs
        two[:rows] = plus(g2[...], by_x[:rows], by_y[:rows]).astype(BF)
        for n, (gx, gy) in enumerate(((gx1, gy1), (gx3, gy3))):
            via_x = by_x.at[rows + n * cut : rows + (n + 1) * cut]
            via_y = by_y.at[rows + n * low : rows + (n + 1) * low]
            at = slice(n * rows, (n + 1) * rows)
            put_relay(gx, gy, via_x, via_y, to_x.at[at], to_y.at[at], cut)
        put_relay(d_x, d_y, by_x.at[x_rows : x_rows + d_cut], by_y.at[y_rows:], d_to_x, d_to_y, d_cut)
        total = sums[...] + one_term(by_x[x_rows + d_cut :])
        new_sums[...] = total
        two[rows:] = two_terms(total)
        to_y[2 * rows :] = two_terms(total)

    two_sum, by_x, by_y, d_x, d_y, sums = combine(
        "sums_two",
        second_step,
        [g2, by_x, by_y, gx1, gy1, gx3, gy3, d_x, d_y, sums],
        [wider, shape((2 * rows, cols), BF), shape((2 * rows + 2 * SMALL, cols), BF), block, block]
        + [shape((SMALL, cols), F32)],
    )
    two_got = to_line(two_sum, 2)
    by_x, by_y = over_x(by_x), over_y(by_y)
    layer_out = finish_output(hidden, down_part, down_other, small)
    by_x, by_y, layer_out, two_got = together(by_x, by_y, layer_out, two_got)

    def third_step(ins, outs):
        g1, g3, by_x, by_y, gx0, gy0, even_x, even_y, d_x, d_y, two_got, sums = ins
        one, three, to_x, to_y, new_sums = outs
        for n, (own, to) in enumerate(((g1, one), (g3, three))):
            at = slice(n * rows, (n + 1) * rows)
            to[:rows] = plus(own[...], by_x[at], by_y[at]).astype(BF)
        put_relay(gx0, gy0, even_x.at[cut:], even_y.at[low:], to_x.at[:rows], to_y.at[:rows], cut)
        to_x[rows:] = d_x[...]
        to_y[rows : rows + share] = d_y[...]
        total = sums[...] + one_term(by_y[2 * rows :])
        one[rows:] = two_terms(total)
        three[rows:] = two_terms(total)
        to_y[rows + share :] = two_got[rows:]
        new_sums[...] = total + one_term(two_got[rows:])

    one_sum, three_sum, gx0, gy0, sums = combine(
        "sums_one_three",
        third_step,
        [g1, g3, by_x, by_y, gx0, gy0, even_x, even_y, d_x, d_y, two_got, sums],
        [wider, wider, shape((rows + share, cols), BF), shape((rows + share + 2 * SMALL, cols), BF)]
        + [shape((SMALL, cols), F32)],
    )
    one_got, three_got = to_line(one_sum, 1), to_line(three_sum, 3)
    gx0, gy0 = over_x(gx0), over_y(gy0)

    def sum_parts(ins, outs):
        for n, out in enumerate(outs):
            out[...] = plus(*(r[n * share : (n + 1) * share] for r in ins))

    result = shape((share, cols), F32)
    output_grad, up_grad = combine("sums_mlp", sum_parts, [mlp_sums[0], mlp_one, mlp_two, mlp_three], [result] * 2)

    parts = [g0, gx0, gy0, one_got, two_got, three_got]

    def last_step(me, *refs):
        ins, d_own, sums, outs = refs[:6], refs[6], refs[7], refs[8:]
        sum_parts(ins, outs[:3])
        outs[3][...] = plus(d_own[...], ins[1][rows:], ins[2][rows : rows + share])
        ends = one_term(ins[2][rows + share :]) + one_term(ins[3][rows:]) + one_term(ins[5][rows:])
        put_own_parts(me[0], sums[...] + ends, outs[4:])

    outs = [result] * 4 + own_shapes(share, cols)
    *grads, down_grad, a, b, c, e = run("sums_attention", last_step, [*parts, d_own, sums], outs, order=me)
    return layer_out, input_grad, [*grads, output_grad, up_grad, down_grad], (a, b, c, e)


def solution(mesh):
    rows = P("dp", None)
    wide = P("dp", "mp")
    tall = P("mp", "dp")
    return jax.shard_map(
        local,
        mesh=mesh,
        in_specs=(rows,) * 5
        + (wide, wide, wide, tall, P("dp"), P("dp"), wide, P("mp"), tall, P("dp")),
        out_specs=(rows, rows, wide, wide, wide, tall, P("dp"), P("dp"), wide, P("mp"), tall, P("dp")),
        check_vma=False,
    )
```

```python
import math

import jax
import jax.numpy as jnp
import numpy as np
from jax import lax
from jax.experimental import pallas as pl
from jax.experimental.pallas import tpu as pltpu
from jax.sharding import PartitionSpec as P

HD = 80
NCLASS = 3
PATCHES = 16
TILE = 352
LANES = 128
BF = jnp.bfloat16
F32 = jnp.float32
ROOT = math.sqrt(HD)
ROOM = 6 * 1024 * 1024
SMALL = 8


def pairs(move):
    out = []
    for z in range(4):
        for y in range(2):
            for x in range(2):
                a, b, c = move(z, y, x)
                out.append(((z * 2 + y) * 2 + x, (a * 2 + b) * 2 + c))
    return out


def over_x(field):
    return lax.ppermute(field, "dp", pairs(lambda z, y, x: (z, y, 1 - x)))


def over_y(field):
    return lax.ppermute(field, "dp", pairs(lambda z, y, x: (z, 1 - y, x)))


def up_z(field, k):
    return lax.ppermute(field, "dp", pairs(lambda z, y, x: ((z + k) % 4, y, x)))


def over_mp(field):
    return lax.ppermute(field, "mp", [(0, 1), (1, 0)])


def gridded():
    return lax.axis_size("dp") == 16


def chip_order():
    me = lax.axis_index("dp")
    z, y, x = me // 4, (me // 2) % 2, me % 2
    k = jnp.arange(16, dtype=jnp.int32)
    line, square = k // 4, k % 4
    return ((z - line + 4) % 4) * 4 + (y ^ (square // 2)) * 2 + (x ^ (square % 2))


def together(*values):
    return lax.optimization_barrier(values)


def halves(rows):
    cut = (rows // 2 + 15) // 16 * 16
    return slice(0, cut), slice(cut, rows)


def to_line(field, k):
    return up_z(field, 4 - k)


COST = 1.0

NN = (((1,), (0,)), ((), ()))
NT = (((1,), (1,)), ((), ()))
TN = (((0,), (0,)), ((), ()))
shape = jax.ShapeDtypeStruct


def dot(a, b, dims=NN):
    return lax.dot_general(a, b, dims, preferred_element_type=F32)


def run(name, body, inputs, outs, scratch=(), flops=0, order=None, aliases=None):
    specs = [pl.BlockSpec(memory_space=pltpu.VMEM)] * len(inputs)
    if order is not None:
        inputs, specs = [order, *inputs], [pl.BlockSpec(memory_space=pltpu.SMEM), *specs]
    moved = sum(math.prod(a.shape) * a.dtype.itemsize for a in [*inputs, *outs])
    return pl.pallas_call(
        body,
        name=name,
        in_specs=specs,
        out_specs=[pl.BlockSpec(memory_space=pltpu.VMEM)] * len(outs),
        out_shape=outs,
        scratch_shapes=list(scratch),
        input_output_aliases=aliases or {},
        compiler_params=pltpu.CompilerParams(
            vmem_limit_bytes=ROOM + moved + sum(math.prod(f.shape) * f.dtype.itemsize for f in scratch)
        ),
        cost_estimate=pl.CostEstimate(flops=int(COST * flops), bytes_accessed=int(COST * moved), transcendentals=0),
    )(*inputs)


def tiles(count, size=TILE):
    return [slice(start, start + size) for start in range(0, count, size)]


def pair_columns(p):
    first = 2 * p * HD // LANES * LANES
    return slice(first, first + 2 * LANES)


def apart(p, field):
    lane = lax.broadcasted_iota(jnp.int32, (1, 2 * LANES), 1) + pair_columns(p).start
    zero = jnp.zeros((), field.dtype)
    heads = [jnp.where((lane >= h * HD) & (lane < h * HD + HD), field, zero) for h in (2 * p, 2 * p + 1)]
    return jnp.concatenate(heads, axis=0)


def add_pair(sums, p, part):
    first = pair_columns(p).start // LANES
    for c in range(2):
        piece = part[:, c * LANES : (c + 1) * LANES]
        sums[first + c] = piece if sums[first + c] is None else sums[first + c] + piece


def sideways(field, size):
    return jnp.concatenate([field[:, :size].T, field[:, size:].T], axis=1)


def rope(v, cos, left_sin, right_sin):
    rows, cols = v.shape
    left = pltpu.roll(v, cols - HD // 2, 1)
    right = pltpu.roll(v, HD // 2, 1)
    three = lambda f: f.reshape(rows // PATCHES, PATCHES, cols)
    out = three(v) * cos + three(left) * left_sin + three(right) * right_sin
    return out.reshape(rows, cols)


def rope_tables(heads):
    half = HD // 2
    i = np.arange(half, dtype=np.float32)
    rates = np.exp(np.float32(-math.log(10000.0)) * (np.float32(2.0) * i / np.float32(HD))).astype(np.float32)
    angle = np.arange(PATCHES, dtype=np.float32)[:, None] * rates[None, :]
    cos, sin = np.cos(angle).astype(np.float32), np.sin(angle).astype(np.float32)
    zero = np.zeros_like(sin)
    full = lambda a, b: np.tile(np.concatenate([a, b], 1), (1, heads))
    return full(cos, cos), full(-sin, zero), full(zero, sin)


def row_of(small, at):
    return jnp.concatenate([small[at : at + 1, :], small[at + 1 : at + 2, :]], axis=1)


def token_weight(info, rows, small):
    counts = [small[6:7, c : c + 1] for c in range(NCLASS)]
    total = counts[0] + counts[1] + counts[2]
    return sum(info[rows, 1 + c : 2 + c] * (total / (NCLASS * counts[c])) for c in range(NCLASS))


def scale_of(field):
    return lax.rsqrt(jnp.mean(field * field, axis=-1, keepdims=True) + 1e-06)


def upper(rows):
    return rows // 2 // 16 * 16 + 16


def query_blocks(count, do):
    full = count // LANES

    def body(b, carry):
        do(b, pl.ds(pl.multiple_of(b * LANES, LANES), LANES), LANES)
        return carry

    lax.fori_loop(0, full, body, 0)
    if count % LANES:
        do(full, slice(full * LANES, count), count % LANES)


def combine(name, body, inputs, outs):
    return run(name, lambda *refs: body(refs[: len(inputs)], refs[len(inputs) :]), inputs, outs)


def stacked(name, *fields):
    def body(ins, outs):
        for n, ref in enumerate(ins):
            outs[0][n] = ref[...]

    return combine(name, body, fields, [shape((len(fields), *fields[0].shape), fields[0].dtype)])[0]


def cut_out(name, *wanted):
    def body(ins, outs):
        for ref, out, (_, first, end) in zip(ins, outs, wanted):
            out[...] = ref[first:end]

    outs = [shape((end - first, *f.shape[1:]), f.dtype) for f, first, end in wanted]
    return combine(name, body, [f for f, _, _ in wanted], outs)


def two_terms(field):
    high = field.astype(BF).astype(F32)
    return jnp.concatenate([high, field - high], axis=0).astype(BF)


def one_term(pair):
    pair = pair.astype(F32)
    return pair[:SMALL] + pair[SMALL:]


def plus(*fields):
    return sum(f.astype(F32) for f in fields)


def put_relay(gx, gy, via_x, via_y, to_x, to_y, top):
    to_x[:top] = gx[:top]
    to_x[top:] = plus(gx[top:], via_y[...]).astype(BF)
    to_y[:top] = plus(gy[:top], via_x[...]).astype(BF)
    to_y[top:] = gy[top:]


def place(name, order, gathered, names, share, into=None):
    arrays = []
    for array, *_ in gathered:
        if not any(array is a for a in arrays):
            arrays.append(array)
    cols = arrays[0].shape[-1]
    into = list(into or ())

    def body(order, *refs):
        out = refs[len(arrays) + len(into) :]
        for array, index, line, square, start in gathered:
            ref = refs[[a is array for a in arrays].index(True)]
            chip = order[line * 4 + square] * share
            for n in range(names):
                low, high = max(start, n * share), min(start + array.shape[-2], (n + 1) * share)
                if low < high:
                    to = pl.ds(pl.multiple_of(chip + (low - n * share), 16), high - low)
                    rows = slice(low - start, high - start)
                    out[n][to, :] = ref[rows, :] if index is None else ref[index, rows, :]

    aliases = {1 + len(arrays) + n: n for n in range(len(into))}
    return run(
        name, body, [*arrays, *into], [shape((16 * share, cols), BF)] * names, order=order, aliases=aliases
    )


def project(tokens, tables, small, wq, wk, wv):
    count, width = tokens.shape
    cols = wq.shape[1]

    def body(tokens, cos, left_sin, right_sin, small, wq, wk, wv, normed, q_out, k_out, v_out):
        turn = cos[...], left_sin[...], right_sin[...]
        for rows in tiles(count):
            x = tokens[rows, :].astype(F32)
            low = (x * scale_of(x) * row_of(small, 0)).astype(BF)
            normed[rows, :] = low
            q_out[rows, :] = rope(dot(low, wq[...]), *turn).astype(BF)
            k_out[rows, :] = rope(dot(low, wk[...]), *turn).astype(BF)
            v_out[rows, :] = dot(low, wv[...]).astype(BF)

    return run(
        "project",
        body,
        [tokens, *tables, small, wq, wk, wv],
        [shape((count, width), BF)] + [shape((count, cols), BF)] * 3,
        flops=6 * count * width * cols,
    )


def attend(info, coderow, queries, keys, values, heads):
    count, cols = queries.shape

    def body(info, coderow, q, k, v, probs, mixture):
        def one_block(b, rows, size):
            key_at = lax.broadcasted_iota(jnp.int32, (size, 2 * size), 0)
            query_at = lax.broadcasted_iota(jnp.int32, (size, 2 * size), 1)
            query_at = jnp.where(query_at < size, query_at, query_at - size)
            code = coderow[b][:, :size]
            same = info[rows, 0:1] == jnp.concatenate([code, code], axis=1)
            allowed = (same & (key_at < query_at)) | (key_at == query_at)
            sums = [None] * (cols // LANES)
            for p in range(heads // 2):
                here = pair_columns(p)
                scores = dot(k[rows, here], apart(p, q[rows, here]), NT) * (1.0 / ROOT)
                scores = jnp.where(allowed, scores, -1e30)
                exponent = jnp.exp(scores - jnp.max(scores, axis=0, keepdims=True))
                soft = exponent * (1.0 / jnp.sum(exponent, axis=0, keepdims=True))
                probs[p, rows, 0 : 2 * size] = soft
                add_pair(sums, p, dot(sideways(soft.astype(BF), size), apart(p, v[rows, here])))
            mixture[rows, :] = jnp.concatenate(sums, axis=1).astype(BF)

        query_blocks(count, one_block)

    return run(
        "attend",
        body,
        [info, coderow, queries, keys, values],
        [shape((heads // 2, count, 2 * LANES), F32), shape((count, cols), BF)],
        flops=40 * count * LANES * cols,
    )


def attention_backward(q, k, v, probs, mixture_grad, tables, heads):
    count, cols = q.shape

    def body(q, k, v, probs, mg, cos, left_sin, right_sin, dq_out, dk_out, dv_out, dq, dk):
        def back(b, rows, size):
            sums = [[None] * (cols // LANES) for _ in range(3)]
            for p in range(heads // 2):
                here = pair_columns(p)
                soft = probs[p, rows, 0 : 2 * size]
                grad = apart(p, mg[rows, here])
                soft_grad = dot(v[rows, here], grad, NT)
                inner = jnp.sum(soft * soft_grad, axis=0, keepdims=True)
                score_grad = (soft * (soft_grad - inner)).astype(BF)
                add_pair(sums[2], p, dot(soft.astype(BF), grad))
                add_pair(sums[0], p, dot(sideways(score_grad, size), apart(p, k[rows, here])))
                add_pair(sums[1], p, dot(score_grad, apart(p, q[rows, here])))
            dv_out[rows, :] = jnp.concatenate(sums[2], axis=1).astype(BF)
            dq[rows, :] = jnp.concatenate(sums[0], axis=1)
            dk[rows, :] = jnp.concatenate(sums[1], axis=1)

        query_blocks(count, back)
        turn = cos[...], -left_sin[...], -right_sin[...]
        for grad, out in ((dq, dq_out), (dk, dk_out)):
            for rows in tiles(count):
                out[rows, :] = rope(grad[rows, :] * (1.0 / ROOT), *turn).astype(BF)

    return run(
        "attention_backward",
        body,
        [q, k, v, probs, mixture_grad, *tables],
        [shape((count, cols), BF)] * 3,
        [pltpu.VMEM((count, cols), F32)] * 2,
        flops=12 * count * LANES * cols,
    )


def project_back(name, fields, weights):
    count, cols = fields[0].shape
    width, n = weights[0].shape[0], len(fields)

    def body(*refs):
        out = refs[-1]
        for rows in tiles(count):
            total = dot(refs[0][rows, :], refs[n][...], NT)
            for f in range(1, n):
                total = total + dot(refs[f][rows, :], refs[n + f][...], NT)
            out[rows, :] = total.astype(BF)

    return run(
        name, body, [*fields, *weights], [shape((count, width), BF)], flops=2 * n * count * width * cols
    )[0]


def attention_in_back(fields, weights, tokens):
    count, cols = fields[0].shape
    width, n = weights[0].shape[0], len(fields)

    def body(*refs):
        tokens, out = refs[2 * n :]
        parts = []
        for rows in tiles(count):
            total = dot(refs[0][rows, :], refs[n][...], NT)
            for f in range(1, n):
                total = total + dot(refs[f][rows, :], refs[n + f][...], NT)
            out[rows, :] = total.astype(BF)
            field = tokens[rows, :].astype(F32)
            parts.append(jnp.sum(total * field * scale_of(field), axis=0, keepdims=True))
        gain = sum(parts)
        high = gain.astype(BF).astype(F32)
        row = lax.broadcasted_iota(jnp.int32, (2 * SMALL, width), 0)
        out[count:, :] = jnp.where(row == 0, high, jnp.where(row == 1, gain - high, 0.0)).astype(BF)

    return run(
        "attention_in_back",
        body,
        [*fields, *weights, tokens],
        [shape((count + 2 * SMALL, width), BF)],
        flops=2 * n * count * width * cols,
    )[0]


def weigh_cotangent(cotangent, info, small):
    count, width = cotangent.shape

    def body(cot, info, small, low, total):
        parts = []
        for rows in tiles(count):
            low[rows, :] = (cot[rows, :].astype(F32) * token_weight(info, rows, small)).astype(BF)
            parts.append(jnp.sum(low[rows, :].astype(F32), axis=0, keepdims=True))
        total[...] = sum(parts)

    return run(
        "weigh_cotangent",
        body,
        [cotangent, info, small],
        [shape((count, width), BF), shape((1, width), F32)],
    )


def mlp_up(tokens, mine, other, small, up_bias, weight):
    count, width = tokens.shape
    cols = up_bias.shape[1]

    def body(tokens, mine, other, small, bias, w, hidden, normed, act, slope):
        for rows in tiles(count):
            field = tokens[rows, :].astype(F32) + (mine[rows, :].astype(F32) + other[rows, :].astype(F32))
            hidden[rows, :] = field
            low = (field * scale_of(field) * row_of(small, 2)).astype(BF)
            normed[rows, :] = low
            pre = dot(low, w[...]) + bias[...].astype(F32)
            sig = 1.0 / (1.0 + jnp.exp(-pre))
            act[rows, :] = (pre * sig).astype(BF)
            slope[rows, :] = sig * (1.0 + pre * (1.0 - sig))

    return run(
        "mlp_up",
        body,
        [tokens, mine, other, small, up_bias, weight],
        [shape((count, width), F32), shape((count, width), BF), shape((count, cols), BF), shape((count, cols), F32)],
        flops=2 * count * width * cols,
    )


def mlp_back(low, slope, down, up):
    count, width = low.shape
    cols = slope.shape[1]

    def body(low, slope, down, up, pre_grad, part, total):
        sums = []
        for rows in tiles(count):
            grad = (dot(low[rows, :], down[...]) * slope[rows, :]).astype(BF)
            pre_grad[rows, :] = grad
            sums.append(jnp.sum(grad.astype(F32), axis=0, keepdims=True))
            part[rows, :] = dot(grad, up[...], NT).astype(BF)
        total[...] = sum(sums)

    return run(
        "mlp_back",
        body,
        [low, slope, down, up],
        [shape((count, cols), BF), shape((count, width), BF), shape((1, cols), F32)],
        flops=4 * count * width * cols,
    )


def finish_output(hidden, mine, other, small):
    def body(hidden, mine, other, small, out):
        for rows in tiles(hidden.shape[0]):
            down = mine[rows, :].astype(F32) + other[rows, :].astype(F32)
            out[rows, :] = (hidden[rows, :] + (down + row_of(small, 4))).astype(BF)

    return run("finish_output", body, [hidden, mine, other, small], [shape(hidden.shape, BF)])[0]


def norm_back(field, scale, gain, grad):
    scaled = grad * gain
    inner = jnp.mean(scaled * field, axis=-1, keepdims=True)
    return scale * scaled - field * (scale * scale * scale * inner)


def hidden_back(hidden, mine, other, cotangent, info, small, weight):
    count, width = hidden.shape
    cols = weight.shape[1]

    def body(hidden, mine, other, cot, info, small, w, grad_out, low, mg, total):
        parts = []
        for rows in tiles(count):
            field = hidden[rows, :]
            grad = mine[rows, :].astype(F32) + other[rows, :].astype(F32)
            scale = scale_of(field)
            parts.append(jnp.sum(grad * field * scale, axis=0, keepdims=True))
            through = norm_back(field, scale, row_of(small, 2), grad)
            result = cot[rows, :].astype(F32) * token_weight(info, rows, small) + through
            grad_out[rows, :] = result
            low[rows, :] = result.astype(BF)
            mg[rows, :] = dot(result.astype(BF), w[...]).astype(BF)
        total[...] = sum(parts)

    return run(
        "hidden_back",
        body,
        [hidden, mine, other, cotangent, info, small, weight],
        [shape((count, width), F32), shape((count, width), BF), shape((count, cols), BF), shape((1, width), F32)],
        flops=2 * count * width * cols,
    )


def input_back(tokens, mine, other, hidden_grad, small):
    count, width = tokens.shape

    def body(tokens, mine, other, hidden_grad, small, out):
        for rows in tiles(count):
            field = tokens[rows, :].astype(F32)
            grad = mine[rows, :].astype(F32) + other[rows, :].astype(F32)
            out[rows, :] = hidden_grad[rows, :] + norm_back(field, scale_of(field), row_of(small, 0), grad)

    return run(
        "input_back", body, [tokens, mine, other, hidden_grad, small], [shape((count, width), F32)]
    )[0]


def weight_grads(name, order, left, rights, share, kind):
    count, width = left.shape
    cols = rights[0].shape[1]
    n = len(rights)
    rows = n * share
    if kind == "whole":
        outs = [shape((width, cols), BF)] * n
    elif kind == "ring":
        outs = [shape((4, rows, cols), BF)] * 4
    elif kind == "square":
        outs = [shape((4, rows, cols), BF)] * 3 + [shape((2, rows, cols), BF)] * 2
    else:
        cut = upper(rows)
        outs = [shape((rows, cols), BF)] * 12
        outs += [shape((2 * top, cols), BF) for top in (cut, rows - cut, rows - cut, cut)]

    def body(*refs):
        order, refs = (None, refs) if kind == "whole" else (refs[0], refs[1:])
        left, right, out = refs[0], refs[1 : n + 1], refs[n + 1 : n + 1 + len(outs)]
        whole = out if kind == "whole" else [refs[-1].at[r] for r in range(n)]
        for at in tiles(width, width // 2):
            for r in range(n):
                whole[r][at, :] = dot(left[:, at], right[r][...], TN).astype(BF)
        if kind == "whole":
            return
        for line in range(4):
            for square in range(4):
                chip = order[line * 4 + square]
                for r in range(n):
                    block = whole[r][pl.ds(pl.multiple_of(chip * share, 16), share), :]
                    to = slice(r * share, (r + 1) * share)
                    if kind == "ring":
                        out[line][square, to, :] = block
                    elif kind == "line" and square < 3:
                        out[line * 3 + square][to, :] = block
                    elif kind == "line":
                        top, rest = out[12:14] if line % 2 == 0 else out[14:16]
                        second, head = line in (0, 3), top.shape[0] // 2
                        start, end = r * share, (r + 1) * share
                        mid = min(max(head, start), end)
                        if start < mid:
                            at = head * second
                            top[at + start : at + mid, :] = block[: mid - start]
                        if mid < end:
                            at = (rows - head) * second - head
                            rest[at + mid : at + end, :] = block[mid - start :]
                    elif square < 3:
                        out[square][line, to, :] = block
                    else:
                        out[3 + line // 2][line % 2, to, :] = block

    return run(
        name,
        body,
        [left, *rights],
        outs,
        [] if kind == "whole" else [pltpu.VMEM((n, width, cols), BF)],
        flops=2 * n * count * width * cols,
        order=order,
    )


def local(
    tokens,
    cotangent,
    segment_ids,
    valid_mask,
    frequency,
    query_weight,
    key_weight,
    value_weight,
    output_weight,
    attn_gain,
    mlp_gain,
    up_weight,
    up_bias,
    down_weight,
    down_bias,
):
    dp = lax.axis_size("dp")
    me = lax.axis_index("dp")
    block_rows, patches = segment_ids.shape
    count, width = tokens.shape
    share, cols = query_weight.shape
    heads = cols // HD
    member = (frequency == jnp.arange(NCLASS, dtype=jnp.int32)[None, :]).astype(jnp.int32)
    row_valid = jnp.sum(valid_mask, axis=1)
    local_counts = jnp.sum(member * row_valid[:, None], axis=0)
    here = (jnp.arange(dp, dtype=jnp.int32) == me)[:, None]
    vectors = jnp.stack([attn_gain, mlp_gain, down_bias]).astype(F32)
    vectors = jnp.where(here[None], vectors[:, None, :], 0.0).reshape(6, cols)
    count_row = jnp.pad(local_counts.astype(F32)[None], ((0, 1), (0, cols - NCLASS)))
    small = jnp.concatenate([vectors, count_row])

    code = (jnp.arange(block_rows, dtype=jnp.int32)[:, None] * PATCHES + segment_ids).astype(F32)
    of_class = (valid_mask[:, :, None] * member[:, None, :]).astype(F32).reshape(count, NCLASS)
    key_code = jnp.where(valid_mask == 1, code, -1.0).reshape(count, 1)
    info = jnp.pad(jnp.concatenate([key_code, of_class], 1), ((0, 0), (0, 7 - NCLASS)))
    coderow = jnp.pad(code.reshape(1, count), ((0, 0), (0, -count % LANES))).reshape(-1, 1, LANES)

    weights = (query_weight, key_weight, value_weight, output_weight.T, up_weight, down_weight.T)
    layer = on_grid if gridded() else off_grid
    layer_out, input_grad, grads, sums = layer(
        tokens, cotangent, info, coderow, rope_tables(heads), small, weights, up_bias[None], heads
    )
    query_grad, key_grad, value_grad, output_grad, up_grad, down_grad = grads
    attn_gain_grad, mlp_gain_grad, down_bias_grad, up_bias_grad = sums
    return (
        layer_out,
        input_grad,
        query_grad,
        key_grad,
        value_grad,
        output_grad.T,
        attn_gain_grad.reshape(share),
        mlp_gain_grad.reshape(share),
        up_grad,
        up_bias_grad,
        down_grad.T,
        down_bias_grad.reshape(share),
    )


def small_sums(mine, other, *vectors):
    cols = vectors[-1].shape[1]
    count = mine.shape[0] - 2 * SMALL

    def body(ins, outs):
        outs[0][...] = jnp.zeros_like(outs[0])
        ends = plus(ins[0][count:, :], ins[1][count:, :])
        row = 0
        for total in [ends[0:1] + ends[1:2]] + [r[...] for r in ins[2:]]:
            for start in range(0, total.shape[1], cols):
                outs[0][row : row + 1, :] = total[:, start : start + cols]
                row += 1

    return combine("small_sums", body, [mine, other, *vectors], [shape((SMALL, cols), F32)])[0]


def put_own_parts(chip, sums, outs):
    share = outs[0].shape[1]
    for n in range(3):
        row = row_of(sums, 2 * n)
        part = jnp.zeros((1, share), F32)
        for c in range(row.shape[1] // share):
            part = jnp.where(chip == c, row[:, c * share : (c + 1) * share], part)
        outs[n][...] = part
    outs[3][...] = sums[6]


def own_shapes(share, cols):
    return [shape((1, share), F32)] * 3 + [shape((cols,), F32)]


def own_parts(me, sums, share):
    body = lambda me, sums, *outs: put_own_parts(me[0], sums[...], outs)
    outs = own_shapes(share, sums.shape[1])
    return run("own_parts", body, [sums], outs, order=me.astype(jnp.int32).reshape(1))


def off_grid(tokens, cotangent, info, coderow, tables, small, weights, up_bias, heads):
    small = lax.psum(small, "dp")
    share = weights[0].shape[0]
    wq, wk, wv, wo, wu, wd = (lax.all_gather(w, "dp", axis=0, tiled=True) for w in weights)
    normed_one, queries, keys, values = project(tokens, tables, small, wq, wk, wv)
    probs, mixture = attend(info, coderow, queries, keys, values, heads)
    attn_part = project_back("attention_out", [mixture], [wo])
    attn_other = over_mp(attn_part)
    down_low, down_bias_sum = weigh_cotangent(cotangent, info, small)
    hidden, normed_two, activated, slope = mlp_up(tokens, attn_part, attn_other, small, up_bias, wu)
    pre_grad, normed_two_part, up_bias_sum = mlp_back(down_low, slope, wd, wu)
    normed_two_other = over_mp(normed_two_part)
    down_part = project_back("mlp_down", [activated], [wd])
    layer_out = finish_output(hidden, down_part, over_mp(down_part), small)
    hidden_grad, attn_low, mixture_grad, mlp_gain_sum = hidden_back(
        hidden, normed_two_part, normed_two_other, cotangent, info, small, wo
    )
    dq, dk, dv = attention_backward(queries, keys, values, probs, mixture_grad, tables, heads)
    normed_one_part = attention_in_back([dq, dk, dv], [wq, wk, wv], tokens)
    normed_one_other = over_mp(normed_one_part)
    input_grad = input_back(tokens, normed_one_part, normed_one_other, hidden_grad, small)
    locals_ = weight_grads("attention_grads", None, normed_one, [dq, dk, dv], share, "whole")
    for left, right in ((attn_low, mixture), (normed_two, pre_grad), (down_low, activated)):
        locals_ += weight_grads("weight_grads", None, left, [right], share, "whole")
    grads = [lax.psum_scatter(g.astype(F32), "dp", scatter_dimension=0, tiled=True) for g in locals_]
    sums = small_sums(normed_one_part, normed_one_other, mlp_gain_sum, down_bias_sum, up_bias_sum)
    sums = own_parts(lax.axis_index("dp"), lax.psum(sums, "dp"), share)
    return layer_out, input_grad, grads, sums


def from_hbm(name, groups):
    flat = [f for g in groups for f in g]
    outs = [shape((sum(f.shape[0] for f in g), g[0].shape[1]), g[0].dtype) for g in groups]

    def body(*refs):
        ins, refs = refs[: len(flat)], refs[len(flat) :]
        out, held, sem, out_sem = refs[: len(groups)], refs[len(groups) : -2], refs[-2], refs[-1]
        copies, at = [], 0
        for g, group in enumerate(groups):
            row = 0
            copies.append([])
            for field in group:
                to = held[g].at[pl.ds(row, field.shape[0])]
                copies[g].append(pltpu.make_async_copy(ins[at], to, sem.at[at]))
                copies[g][-1].start()
                row, at = row + field.shape[0], at + 1
        back = [pltpu.make_async_copy(held[g], out[g], out_sem.at[g]) for g in range(len(groups))]
        for g in range(len(groups)):
            for copy in copies[g]:
                copy.wait()
            back[g].start()
        for copy in back:
            copy.wait()

    moved = sum(math.prod(o.shape) * o.dtype.itemsize for o in outs)
    return pl.pallas_call(
        body,
        name=name,
        in_specs=[pl.BlockSpec(memory_space=pltpu.HBM)] * len(flat),
        out_specs=[pl.BlockSpec(memory_space=pltpu.HBM)] * len(outs),
        out_shape=outs,
        scratch_shapes=[pltpu.VMEM(o.shape, o.dtype) for o in outs]
        + [pltpu.SemaphoreType.DMA((len(flat),)), pltpu.SemaphoreType.DMA((len(groups),))],
        compiler_params=pltpu.CompilerParams(vmem_limit_bytes=58 * 1024 * 1024),
        cost_estimate=pl.CostEstimate(flops=0, bytes_accessed=2 * moved, transcendentals=0),
    )(*flat)


def on_grid(tokens, cotangent, info, coderow, tables, small, weights, up_bias, heads):
    order, me = chip_order(), lax.axis_index("dp").astype(jnp.int32).reshape(1)
    share, cols = weights[0].shape
    rows = 3 * share
    q, k, v, o, u, d = weights
    first, four = from_hbm("stack_first", [(q, k, v), (q, k, v, d)])
    cut, low, mid = upper(rows), rows - upper(rows), 2 * share
    block = shape((share, cols), BF)
    fourfold = shape((4, share, cols), BF)
    put = lambda name, pieces, into: place(name, order, pieces, 3, share, into)
    put_one = lambda name, pieces, into=None: place(name, order, pieces, 1, share, into)

    one, three = up_z(first, 1), up_z(first, 3)
    own_x, own_y = over_x(four), over_y(four)
    small_got = lax.ppermute(small, "dp", pairs(lambda z, y, x: (z ^ 1, y, x)))

    def cut_own(ins, outs):
        outs[0][...] = ins[0][:mid]
        outs[1][...] = ins[1][mid:]

    own_a, own_b = combine("cut_own", cut_own, [own_x, own_y], [shape((mid, cols), BF)] * 2)
    own_a, own_b = over_y(own_a), over_x(own_b)
    ready = together(
        four, own_x, own_y, one, three, own_a, own_b, small, small_got, info, coderow, order, me, up_bias
    )
    four, own_x, own_y, one, three, own_a, own_b, small, small_got, info, coderow, order, me, up_bias = ready
    small = small + small_got
    two = up_z(first, 2)
    both = stacked("stack_one_three", one, three)
    both_x, both_y = over_x(both), over_y(both)
    small_got = up_z(small, 2)

    def stack_down(ins, outs):
        four, own_x, own_y, own_b = ins
        outs[0][0] = four[rows:]
        outs[0][1] = own_x[rows:]
        outs[0][2] = own_y[rows:]
        outs[0][3] = own_b[rows - mid :]

    (down_0,) = combine("stack_down", stack_down, [four, own_x, own_y, own_b], [fourfold])
    mlp_0 = stacked("stack_mlp", o, u).reshape(2 * share, cols)
    attn = put(
        "place_0",
        [(four, None, 0, 0, 0), (own_x, None, 0, 1, 0), (own_y, None, 0, 2, 0), (own_a, None, 0, 3, 0)]
        + [(own_b, None, 0, 3, mid), (one, None, 1, 0, 0), (three, None, 3, 0, 0)],
        None,
    )
    both_x, both_y, two, small, small_got, down_0, mlp_0, *attn = together(
        both_x, both_y, two, small, small_got, down_0, mlp_0, *attn
    )
    small = small + small_got

    def next_step(ins, outs):
        two, both_x, both_y = ins
        outs[0][0] = two[...]
        outs[0][1] = both_y[1]
        outs[1][0] = two[...]
        outs[1][1] = both_x[0]

    by_x, by_y = combine("stack_two", next_step, [two, both_x, both_y], [shape(both.shape, BF)] * 2)
    mlp_1, mlp_3 = up_z(mlp_0, 1), up_z(mlp_0, 3)
    by_x, by_y = over_x(by_x), over_y(by_y)
    small_got = over_x(small)
    attn = put(
        "place_1",
        [(both_x, 0, 1, 1, 0), (both_y, 0, 1, 2, 0), (both_x, 1, 3, 1, 0), (both_y, 1, 3, 2, 0), (two, None, 2, 0, 0)],
        attn,
    )
    by_x, by_y, small, small_got, mlp_1, mlp_3, *attn = together(
        by_x, by_y, small, small_got, mlp_1, mlp_3, *attn
    )

    def halves(ins, outs):
        outs[0][...] = ins[0][0, :cut]
        outs[1][...] = ins[1][0, cut:]

    two_a, two_b = combine("cut_two", halves, [by_x, by_y], [shape((cut, cols), BF), shape((low, cols), BF)])
    small = small + small_got
    two_a, two_b = over_y(two_a), over_x(two_b)
    small_got = over_y(small)
    mlp_2 = up_z(mlp_1, 1)
    attn = put(
        "place_2",
        [(by_y, 1, 1, 3, 0), (by_x, 1, 3, 3, 0), (by_x, 0, 2, 1, 0), (by_y, 0, 2, 2, 0)],
        attn,
    )
    two_a, two_b, small, small_got, mlp_2, down_0, *attn = together(
        two_a, two_b, small, small_got, mlp_2, down_0, *attn
    )
    small = small + small_got

    def stack_output(ins, outs):
        for k, ref in enumerate(ins):
            outs[0][k] = ref[:share]

    (wo_own,) = combine("stack_output", stack_output, [o, mlp_1, mlp_2, mlp_3], [fourfold])
    lines = lambda *arrays: [(a, k, k, s, 0) for s, a in enumerate(arrays) for k in range(4)]
    diagonal = lambda a, b: [((a, b)[k // 2], k % 2, k, 3, 0) for k in range(4)]
    wo_x, wo_y = over_x(wo_own), over_y(wo_own)
    down_1 = up_z(down_0, 1)
    wq, wk, wv = put("place_3", [(two_a, None, 2, 3, 0), (two_b, None, 2, 3, cut)], attn)
    normed_one, queries, keys, values = project(tokens, tables, small, wq, wk, wv)
    wo_x, wo_y, queries, wo_own = together(wo_x, wo_y, queries, wo_own)

    def add_up(ins, outs):
        wo_x, wo_y, up_0, mlp_1, mlp_2, mlp_3 = ins
        for out in outs:
            out[0] = up_0[...]
            for k, ref in enumerate((mlp_1, mlp_2, mlp_3)):
                out[k + 1] = ref[share:]
        outs[0][4:] = wo_y[2:]
        outs[1][4:] = wo_x[:2]

    sixfold = shape((6, share, cols), BF)
    wu_own, up_y = combine("add_up", add_up, [wo_x, wo_y, u, mlp_1, mlp_2, mlp_3], [sixfold] * 2)
    up_x, up_y = over_x(wu_own), over_y(up_y)
    down_1, queries = together(down_1, queries)
    down_2, down_3 = up_z(down_1, 1), up_z(down_0, 3)
    probs, mixture = attend(info, coderow, queries, keys, values, heads)
    wo = put_one("place_output", lines(wo_own, wo_x, wo_y))
    down_low, down_bias_sum = weigh_cotangent(cotangent, info, small)
    up_x, up_y, mixture, down_low, down_2, wu_own, *wo = together(up_x, up_y, mixture, down_low, down_2, wu_own, *wo)

    wu_a, wu_b = cut_out("cut_up", (up_x, 0, 2), (up_y, 2, 4))
    wu_a, wu_b = over_y(wu_a), over_x(wu_b)
    (wo,) = put_one("place_output_end", [((up_y, up_x)[k // 2], 4 + k % 2, k, 3, 0) for k in range(4)], wo)
    attn_part = project_back("attention_out", [mixture], [wo])
    attn_other = over_mp(attn_part)
    wu = put_one("place_up", lines(wu_own, up_x, up_y))
    by_line = lambda k, a: [(a, s, k, s, 0) for s in range(4)]
    wd = put_one("place_down", by_line(0, down_0) + by_line(1, down_1) + by_line(2, down_2))
    attn_other, wu_a, wu_b, *wu = together(attn_other, wu_a, wu_b, *wu)
    (wu,) = put_one("place_up_end", diagonal(wu_a, wu_b), wu)
    hidden, normed_two, activated, slope = mlp_up(tokens, attn_part, attn_other, small, up_bias, wu)

    grads_of = lambda name, left, right, kind: weight_grads(name, order, left, right, share, kind)
    d_0, d_1, d_2, d_3 = grads_of("down_grads", down_low, [activated], "ring")
    down_3, slope, d_1 = together(down_3, slope, d_1)
    (wd,) = put_one("place_down_end", by_line(3, down_3), wd)
    pre_grad, normed_two_part, up_bias_sum = mlp_back(down_low, slope, wd, wu)
    normed_two_part, pre_grad = together(normed_two_part, pre_grad)
    normed_two_other = over_mp(normed_two_part)
    d_got = up_z(d_1, 1)
    u_own, u_x, u_y, u_a, u_b = grads_of("up_grads", normed_two, [pre_grad], "square")
    u_a, u_b = over_x(u_a), over_y(u_b)
    down_part = project_back("mlp_down", [activated], [wd])
    hidden_grad, attn_low, mixture_grad, mlp_gain_sum = hidden_back(
        hidden, normed_two_part, normed_two_other, cotangent, info, small, wo
    )
    o_own, o_x, o_y, o_a, o_b = grads_of("output_grads", attn_low, [mixture], "square")
    u_a, u_b, down_part, mixture_grad, o_a, o_b, d_got = together(u_a, u_b, down_part, mixture_grad, o_a, o_b, d_got)

    def ring_step(name, mine, got):
        def body(ins, outs):
            for s in range(4):
                outs[0][s] = plus(ins[0][s], ins[1][s]).astype(BF)

        return up_z(combine(name, body, [mine, got], [fourfold])[0], 1)

    def relay_up(ins, outs):
        put_relay(*ins[:4], outs[0].at[:4], outs[1].at[:4], 2)
        outs[0][4:] = ins[4][...]
        outs[1][4:] = ins[5][...]

    up_x, up_y = combine("relay_up", relay_up, [u_x, u_y, u_a, u_b, o_a, o_b], [sixfold] * 2)
    up_x, up_y = over_x(up_x), over_y(up_y)
    d_got = ring_step("ring_two", d_2, d_got)
    dq, dk, dv = attention_backward(queries, keys, values, probs, mixture_grad, tables, heads)
    d_got, dq = together(d_got, dq)
    d_got = ring_step("ring_three", d_3, d_got)
    up_x, up_y, dq, dk, dv, down_part = together(up_x, up_y, dq, dk, dv, down_part)

    down_other = over_mp(down_part)

    def relay_output(ins, outs):
        o_x, o_y, up_x, up_y = ins
        put_relay(o_x, o_y, up_x.at[4:], up_y.at[4:], *outs, 2)

    o_x, o_y = combine("relay_output", relay_output, [o_x, o_y, up_x, up_y], [fourfold] * 2)
    o_x, o_y = over_x(o_x), over_y(o_y)
    pieces = weight_grads("attention_grads", order, normed_one, [dq, dk, dv], share, "line")
    normed_one_part = attention_in_back([dq, dk, dv], [wq, wk, wv], tokens)
    o_x, o_y, normed_one_part, down_other, d_got, *pieces = together(
        o_x, o_y, normed_one_part, down_other, d_got, *pieces
    )

    g0, gx0, gy0, g1, gx1, gy1, g2, gx2, gy2, g3, gx3, gy3, even_x, even_y, odd_x, odd_y = pieces
    like = shape((rows, cols), BF)
    d_cut = upper(share)

    even_x, even_y = over_x(even_x), over_y(even_y)

    def square_sums(ins, outs):
        for n in range(2):
            at = slice(n * share, (n + 1) * share)
            for k in range(4):
                outs[k][at] = plus(*(r[k] for r in ins[3 * n : 3 * n + 3])).astype(outs[k].dtype)

    mlp_sums = combine(
        "sums_square",
        square_sums,
        [o_own, o_x, o_y, u_own, up_x, up_y],
        [shape((2 * share, cols), F32)] + [shape((2 * share, cols), BF)] * 3,
    )
    mlp_one = to_line(mlp_sums[1], 1)
    normed_one_other = over_mp(normed_one_part)
    even_x, even_y, normed_one_other, mlp_one, mlp_two, mlp_three = together(
        even_x, even_y, normed_one_other, mlp_one, *mlp_sums[2:]
    )

    sums = small_sums(normed_one_part, normed_one_other, mlp_gain_sum, down_bias_sum, up_bias_sum)
    x_rows, y_rows = rows + 2 * low, rows + 2 * cut

    def first_step(ins, outs):
        gx2, gy2, even_x, even_y, odd_x, odd_y, d_0, d_got, sums = ins
        to_x, to_y = outs[:2]
        put_relay(gx2, gy2, even_x.at[:cut], even_y.at[:low], to_x.at[:rows], to_y.at[:rows], cut)
        to_x[rows:x_rows] = odd_x[...]
        to_y[rows:y_rows] = odd_y[...]
        diagonal = plus(d_0[3], d_got[3]).astype(BF)
        to_x[x_rows : x_rows + d_cut] = diagonal[:d_cut]
        to_y[y_rows:] = diagonal[d_cut:]
        for s in range(3):
            outs[2 + s][...] = plus(d_0[s], d_got[s]).astype(BF)
        to_x[x_rows + d_cut :] = two_terms(sums[...])

    by_x, by_y, d_own, d_x, d_y = combine(
        "relay_two",
        first_step,
        [gx2, gy2, even_x, even_y, odd_x, odd_y, d_0, d_got, sums],
        [shape((x_rows + d_cut + 2 * SMALL, cols), BF), shape((y_rows + share - d_cut, cols), BF)] + [block] * 3,
    )
    by_x, by_y = over_x(by_x), over_y(by_y)
    mlp_two, mlp_three = to_line(mlp_two, 2), to_line(mlp_three, 3)
    input_grad = input_back(tokens, normed_one_part, normed_one_other, hidden_grad, small)
    by_x, by_y, mlp_two, mlp_three, input_grad = together(by_x, by_y, mlp_two, mlp_three, input_grad)

    wider = shape((rows + 2 * SMALL, cols), BF)

    def second_step(ins, outs):
        g2, by_x, by_y, gx1, gy1, gx3, gy3, d_x, d_y, sums = ins
        two, to_x, to_y, d_to_x, d_to_y, new_sums = outs
        two[:rows] = plus(g2[...], by_x[:rows], by_y[:rows]).astype(BF)
        for n, (gx, gy) in enumerate(((gx1, gy1), (gx3, gy3))):
            via_x = by_x.at[rows + n * low : rows + (n + 1) * low]
            via_y = by_y.at[rows + n * cut : rows + (n + 1) * cut]
            at = slice(n * rows, (n + 1) * rows)
            put_relay(gx, gy, via_x, via_y, to_x.at[at], to_y.at[at], low)
        put_relay(d_x, d_y, by_x.at[x_rows : x_rows + d_cut], by_y.at[y_rows:], d_to_x, d_to_y, d_cut)
        total = sums[...] + one_term(by_x[x_rows + d_cut :])
        new_sums[...] = total
        two[rows:] = two_terms(total)
        to_y[2 * rows :] = two_terms(total)

    two_sum, by_x, by_y, d_x, d_y, sums = combine(
        "sums_two",
        second_step,
        [g2, by_x, by_y, gx1, gy1, gx3, gy3, d_x, d_y, sums],
        [wider, shape((2 * rows, cols), BF), shape((2 * rows + 2 * SMALL, cols), BF), block, block]
        + [shape((SMALL, cols), F32)],
    )
    two_got = to_line(two_sum, 2)
    by_x, by_y = over_x(by_x), over_y(by_y)
    layer_out = finish_output(hidden, down_part, down_other, small)
    by_x, by_y, layer_out, two_got = together(by_x, by_y, layer_out, two_got)

    def third_step(ins, outs):
        g1, g3, by_x, by_y, gx0, gy0, even_x, even_y, d_x, d_y, two_got, sums = ins
        one, three, to_x, to_y, new_sums = outs
        for n, (own, to) in enumerate(((g1, one), (g3, three))):
            at = slice(n * rows, (n + 1) * rows)
            to[:rows] = plus(own[...], by_x[at], by_y[at]).astype(BF)
        put_relay(gx0, gy0, even_x.at[cut:], even_y.at[low:], to_x.at[:rows], to_y.at[:rows], cut)
        to_x[rows:] = d_x[...]
        to_y[rows : rows + share] = d_y[...]
        total = sums[...] + one_term(by_y[2 * rows :])
        one[rows:] = two_terms(total)
        three[rows:] = two_terms(total)
        to_y[rows + share :] = two_got[rows:]
        new_sums[...] = total + one_term(two_got[rows:])

    one_sum, three_sum, gx0, gy0, sums = combine(
        "sums_one_three",
        third_step,
        [g1, g3, by_x, by_y, gx0, gy0, even_x, even_y, d_x, d_y, two_got, sums],
        [wider, wider, shape((rows + share, cols), BF), shape((rows + share + 2 * SMALL, cols), BF)]
        + [shape((SMALL, cols), F32)],
    )
    one_got, three_got = to_line(one_sum, 1), to_line(three_sum, 3)
    gx0, gy0 = over_x(gx0), over_y(gy0)

    def sum_parts(ins, outs):
        for n, out in enumerate(outs):
            out[...] = plus(*(r[n * share : (n + 1) * share] for r in ins))

    result = shape((share, cols), F32)
    output_grad, up_grad = combine("sums_mlp", sum_parts, [mlp_sums[0], mlp_one, mlp_two, mlp_three], [result] * 2)

    parts = [g0, gx0, gy0, one_got, two_got, three_got]

    def last_step(me, *refs):
        ins, d_own, sums, outs = refs[:6], refs[6], refs[7], refs[8:]
        sum_parts(ins, outs[:3])
        outs[3][...] = plus(d_own[...], ins[1][rows:], ins[2][rows : rows + share])
        ends = one_term(ins[2][rows + share :]) + one_term(ins[3][rows:]) + one_term(ins[5][rows:])
        put_own_parts(me[0], sums[...] + ends, outs[4:])

    outs = [result] * 4 + own_shapes(share, cols)
    *grads, down_grad, a, b, c, e = run("sums_attention", last_step, [*parts, d_own, sums], outs, order=me)
    return layer_out, input_grad, [*grads, output_grad, up_grad, down_grad], (a, b, c, e)


def solution(mesh):
    rows = P("dp", None)
    wide = P("dp", "mp")
    tall = P("mp", "dp")
    return jax.shard_map(
        local,
        mesh=mesh,
        in_specs=(rows,) * 5
        + (wide, wide, wide, tall, P("dp"), P("dp"), wide, P("mp"), tall, P("dp")),
        out_specs=(rows, rows, wide, wide, wide, tall, P("dp"), P("dp"), wide, P("mp"), tall, P("dp")),
        check_vma=False,
    )
```
